32 devices in a mesh: dp: 8 (over z, x), mp: 4 (over y, core).
Axes of the slice: x: 2, y: 2, z: 4, core: 2. Of those that a mesh axis runs over, the one named last changes fastest.
Arguments:
- titles: bfloat16 [2048, 768], P('dp')
- w_attn_in: bfloat16 [3, 768, 768], P(None, None, 'mp')
- w_attn_out: bfloat16 [768, 768], P('mp'), may hold values from -0.21875 to 0.21875
- w_ffn_in: bfloat16 [768, 3072], P(None, 'mp'), may hold values from -0.21875 to 0.21875
- w_ffn_out: bfloat16 [3072, 768], P('mp'), may hold values from -0.109375 to 0.109375
- gains: float32 [2, 768], replicated, may hold values from 0.5 to 1.5
- node_table: bfloat16 [4096, 768], P('dp')
- w_graph: bfloat16 [3, 768, 768], P(None, None, 'mp')
- title_nodes: int32 [16], P('dp'), may hold values from 0 to 511, as said below
- send_ids: int32 [8, 8, 256], P('dp'), may hold values from 0 to 511
- tile_cols: int32 [32, 6], P('dp'), may hold values from 0 to 19, as said below
- nbr_slots: int32 [4096, 16], P('dp'), may hold values from 0 to 767
Outputs:
- encoded: bfloat16 [2048, 768], P('dp')
- graph_out: bfloat16 [4096, 768], P('dp', 'mp')
The draws below stay inside these ranges and needn't reach their ends.
Inputs may be any that keep to these rules, and one draw needn't show every extreme that they name: `title_nodes`: within each partition the 2 entries are distinct local node indices. `send_ids`: entries are local node indices of the owner partition. `tile_cols`: the entries of one row are distinct; entry 0 of local row tile r is r.
All inputs are finite; a program needn't handle non-finite values.
Results may differ from the reference program's by a relative error of at most 0.02.
Values may be sent and summed in bfloat16 or wider, within the bound.
No kernel may reach another device: no remote copies, remote signals or barrier semaphores. Data moves between devices by JAX's collectives and lax.ppermute only.
A program may use at most 64 MiB of HBM per device.

```python
import math
import jax
import jax.numpy as jnp
from jax import lax

D = 768
HEADS = 12
FF = 3072
SEQ = 128
GHEADS = 8
TILE = 128
FAR = 4
DEG = 16
TITLES_DEV = 2
NODES_DEV = 512
TPR = 6
HD = 64
GHD = 96
PARTS_SIZE = 8
FETCH = 256
TITLES = 16
TOKENS = 2048
NODES = 4096
KEY_TILES = 20


def projections(key):
    split_keys = jax.random.split(key, 3)
    scale = 1.0 / math.sqrt(D)
    w_query = jax.random.normal(split_keys[0], (D, D), jnp.float32) * scale
    w_key = jax.random.normal(split_keys[1], (D, D), jnp.float32) * scale
    w_value = jax.random.normal(split_keys[2], (D, D), jnp.float32) * scale
    return jnp.stack([w_query, w_key, w_value]).astype(jnp.bfloat16)


def draw_titles(key, part):
    key = jax.random.fold_in(key, 11)
    values = jax.random.normal(key, (TOKENS, D), jnp.float32)
    return values.astype(jnp.bfloat16)


def draw_w_attn_in(key, part):
    key = jax.random.fold_in(key, 15)
    return projections(key)


def draw_node_table(key, part):
    key = jax.random.fold_in(key, 12)
    values = jax.random.normal(key, (NODES, D), jnp.float32)
    return values.astype(jnp.bfloat16)


def draw_w_graph(key, part):
    key = jax.random.fold_in(key, 16)
    return projections(key)


def draw_title_nodes(key, part):
    key = jax.random.fold_in(key, 13)
    part_keys = jax.random.split(key, TITLES // TITLES_DEV)
    picked = jax.vmap(lambda one_key: jax.random.permutation(one_key, NODES_DEV)[:TITLES_DEV])(part_keys)
    return picked.reshape(-1).astype(jnp.int32)


def draw_tile_cols(key, part):
    key = jax.random.fold_in(key, 14)
    row_tiles = NODES_DEV // TILE
    part_count = NODES // NODES_DEV
    part_keys = jax.random.split(key, part_count)

    def one_part(part_key):
        split_keys = jax.random.split(part_key, 3)
        fetched = jax.random.permutation(split_keys[0], FAR * row_tiles).astype(jnp.int32)
        fetched = fetched.reshape(row_tiles, FAR) + row_tiles
        own_tiles = jnp.arange(row_tiles, dtype=jnp.int32)
        other = jax.random.randint(split_keys[1], (row_tiles,), 0, row_tiles - 1, jnp.int32)
        other = other + (other >= own_tiles).astype(jnp.int32)
        remaining = jnp.concatenate([fetched, other[:, None]], axis=1)
        row_keys = jax.random.split(split_keys[2], row_tiles)
        remaining = jax.vmap(lambda one_key, entries: jax.random.permutation(one_key, entries))(row_keys, remaining)
        return jnp.concatenate([own_tiles[:, None], remaining], axis=1)
    return jax.vmap(one_part)(part_keys).reshape(-1, TPR).astype(jnp.int32)


def set_ends(drawn, stream_key, least, largest):
    dims = drawn.shape
    index_at = [jax.random.randint(jax.random.fold_in(stream_key, axis), (), 0, dims[axis]) for axis in range(len(dims))]
    drawn = drawn.at[tuple(index_at)].set(least)
    longest = dims.index(max(dims))
    index_at[longest] = (index_at[longest] + 1) % dims[longest]
    return drawn.at[tuple(index_at)].set(largest)


def level_of(stream_key, shape, pieces, low, high):
    level, own = 1.0, jax.random.fold_in(stream_key, 6)
    for dim, shards_of in pieces:
        draws = jnp.exp(jax.random.uniform(jax.random.fold_in(own, dim), (shards_of,), jnp.float32, low / len(pieces), high / len(pieces)))
        level = level * jnp.repeat(draws, shape[dim] // shards_of).reshape([-1 if axis == dim else 1 for axis in range(len(shape))])
    return level


def bell_draw(key, extent, spread, reach, cuts=(), held_as=jnp.bfloat16):
    values = spread * jax.random.normal(key, extent, jnp.float32)
    if cuts:
        values = values * level_of(key, extent, cuts, -0.22, 0.18)
    return jnp.clip(values, -reach, reach).astype(held_as)


def setup_inputs(seed: int = 0) -> dict:
    keys = jax.random.split(jax.random.key(seed), 13)
    titles = draw_titles(jax.random.fold_in(keys[12], 71), 0)
    w_attn_in = draw_w_attn_in(jax.random.fold_in(keys[12], 71), 0)
    w_attn_out = bell_draw(keys[2], (D, D), D ** -0.5, 0.21875, ((0, 4),))
    w_ffn_in = bell_draw(keys[3], (D, FF), D ** -0.5, 0.21875, ((1, 4),))
    w_ffn_out = bell_draw(keys[4], (FF, D), FF ** -0.5, 0.109375, ((0, 4),))
    gains = jnp.clip(1.0 + 0.1 * jax.random.normal(keys[5], (2, D), jnp.float32), 0.5, 1.5)
    node_table = draw_node_table(jax.random.fold_in(keys[12], 71), 0)
    w_graph = draw_w_graph(jax.random.fold_in(keys[12], 71), 0)
    title_nodes = draw_title_nodes(jax.random.fold_in(keys[12], 71), 0)
    send_ids = set_ends(jax.random.randint(keys[9], (PARTS_SIZE, PARTS_SIZE, FETCH), 0, NODES_DEV), jax.random.fold_in(keys[9], 1), 0, NODES_DEV - 1).astype(jnp.int32)
    tile_cols = draw_tile_cols(jax.random.fold_in(keys[12], 71), 0)
    nbr_slots = set_ends(jax.random.randint(keys[11], (NODES, DEG), 0, TPR * TILE), jax.random.fold_in(keys[11], 1), 0, (TPR * TILE) - 1).astype(jnp.int32)
    return {"titles": titles, "w_attn_in": w_attn_in, "w_attn_out": w_attn_out, "w_ffn_in": w_ffn_in, "w_ffn_out": w_ffn_out, "gains": gains, "node_table": node_table, "w_graph": w_graph, "title_nodes": title_nodes, "send_ids": send_ids, "tile_cols": tile_cols, "nbr_slots": nbr_slots}


eps_norm = 1e-06

def layer_norm(values, gain):
    mean = lax.optimization_barrier(jnp.mean(values, axis=-1, keepdims=True))
    centred = values - mean
    var = lax.optimization_barrier(jnp.mean(centred * centred, axis=-1, keepdims=True))
    return centred * lax.rsqrt(var + eps_norm) * gain

def reference(titles, w_attn_in, w_attn_out, w_ffn_in, w_ffn_out, gains, node_table, w_graph, title_nodes, send_ids, tile_cols, nbr_slots):
    bf = jnp.bfloat16
    f32 = jnp.float32
    query = jnp.dot(titles, w_attn_in[0], preferred_element_type=f32).astype(bf)
    keyed = jnp.dot(titles, w_attn_in[1], preferred_element_type=f32).astype(bf)
    valued = jnp.dot(titles, w_attn_in[2], preferred_element_type=f32).astype(bf)
    query = query.reshape(TITLES, SEQ, HEADS, HD).astype(f32)
    keyed = keyed.reshape(TITLES, SEQ, HEADS, HD).astype(f32)
    valued = valued.reshape(TITLES, SEQ, HEADS, HD).astype(f32)
    scores = jnp.einsum('bqhd,bkhd->bhqk', query, keyed) / jnp.sqrt(f32(HD))
    probs = jax.nn.softmax(scores, axis=-1).astype(bf)
    context = jnp.einsum('bhqk,bkhd->bqhd', probs.astype(f32), valued).astype(bf).reshape(TOKENS, D)
    attn = jnp.dot(context, w_attn_out, preferred_element_type=f32)
    hidden_one = layer_norm(titles.astype(f32) + attn, gains[0]).astype(bf)
    inner = jax.nn.gelu(jnp.dot(hidden_one, w_ffn_in, preferred_element_type=f32), approximate=False).astype(bf)
    ffn = jnp.dot(inner, w_ffn_out, preferred_element_type=f32)
    encoded = layer_norm(hidden_one.astype(f32) + ffn, gains[1]).astype(bf)
    first_tokens = encoded.reshape(TITLES, SEQ, D)[:, 0]
    node_rows = jnp.arange(TITLES, dtype=jnp.int32) // TITLES_DEV * NODES_DEV + title_nodes
    features = node_table.at[node_rows].set(first_tokens)
    graph_q = jnp.dot(features, w_graph[0], preferred_element_type=f32).astype(bf)
    graph_k = jnp.dot(features, w_graph[1], preferred_element_type=f32).astype(bf)
    graph_v = jnp.dot(features, w_graph[2], preferred_element_type=f32).astype(bf)
    row_tiles = NODES_DEV // TILE
    columns = jnp.arange(TPR * TILE, dtype=jnp.int32)
    own_pos = jnp.arange(TILE, dtype=jnp.int32)
    self_mask = columns[None, None, :] == own_pos[None, :, None]

    def one_part(part_index):
        start = (part_index * NODES_DEV).astype(jnp.int32)
        fetch = (jnp.arange(PARTS_SIZE, dtype=jnp.int32) * NODES_DEV)[:, None] + send_ids[:, part_index, :]
        fetch = fetch.reshape(-1)
        key_rows = jnp.concatenate([lax.dynamic_slice_in_dim(graph_k, start, NODES_DEV, 0), graph_k[fetch]], axis=0)
        value_rows = jnp.concatenate([lax.dynamic_slice_in_dim(graph_v, start, NODES_DEV, 0), graph_v[fetch]], axis=0)
        key_rows = key_rows.reshape(KEY_TILES, TILE, D)
        value_rows = value_rows.reshape(KEY_TILES, TILE, D)
        cols = lax.dynamic_slice_in_dim(tile_cols, (part_index * row_tiles).astype(jnp.int32), row_tiles, 0)
        key_tiles = key_rows[cols].reshape(row_tiles, TPR * TILE, GHEADS, GHD).astype(f32)
        value_tiles = value_rows[cols].reshape(row_tiles, TPR * TILE, GHEADS, GHD).astype(f32)
        queries = lax.dynamic_slice_in_dim(graph_q, start, NODES_DEV, 0).reshape(row_tiles, TILE, GHEADS, GHD).astype(f32)
        scores_g = jnp.einsum('rqhd,rkhd->rhqk', queries, key_tiles) / jnp.sqrt(f32(GHD))
        slots = lax.dynamic_slice_in_dim(nbr_slots, start, NODES_DEV, 0).reshape(row_tiles, TILE, DEG)
        edges = jnp.any(slots[..., None] == columns, axis=2) | self_mask
        edges = edges[:, None, :, :]
        masked = jnp.where(edges, scores_g, -jnp.inf)
        top = lax.optimization_barrier(jnp.max(masked, axis=-1, keepdims=True))
        expo = jnp.where(edges, jnp.exp(masked - top), 0.0)
        weights = (expo / lax.optimization_barrier(jnp.sum(expo, axis=-1, keepdims=True))).astype(bf)
        out = jnp.einsum('rhqk,rkhd->rqhd', weights.astype(f32), value_tiles)
        return out.reshape(NODES_DEV, D).astype(bf)
    graph_out = lax.map(one_part, jnp.arange(PARTS_SIZE, dtype=jnp.int32)).reshape(NODES, D)
    return (encoded, graph_out)
```

```python
import jax
import jax.numpy as jnp
from jax import lax
from jax.experimental import pallas as pl
from jax.experimental.pallas import tpu as pltpu
from jax.sharding import PartitionSpec as P

SEQ = 128
TILE = 128
DEG = 16
TPR = 6
HD = 64
GHD = 96

eps_norm = 1e-06
bf = jnp.bfloat16
f32 = jnp.float32

VMEM = pl.BlockSpec(memory_space=pltpu.VMEM)
SMEM = pl.BlockSpec(memory_space=pltpu.SMEM)
NT = (((1,), (1,)), ((), ()))


def call(kernel, outs, args, smem=(), scratch=(), flops=0, name=None):
    specs = [SMEM if i in smem else VMEM for i in range(len(args))]
    nbytes = sum(a.size * a.dtype.itemsize for a in args)
    return pl.pallas_call(
        kernel,
        out_shape=outs,
        in_specs=specs,
        out_specs=jax.tree.map(lambda _: VMEM, outs),
        scratch_shapes=list(scratch),
        compiler_params=pltpu.CompilerParams(vmem_limit_bytes=40 * 1024 * 1024),
        cost_estimate=pl.CostEstimate(flops=flops, bytes_accessed=nbytes, transcendentals=0),
        name=name,
    )(*args)


def shape(dims, dtype):
    return jax.ShapeDtypeStruct(dims, dtype)


def dot(a, b):
    return jnp.dot(a, b, preferred_element_type=f32)


def dot_nt(a, b):
    return lax.dot_general(a, b, NT, preferred_element_type=f32)


def layer_norm(values, gain):
    mean = jnp.mean(values, axis=-1, keepdims=True)
    centred = values - mean
    var = jnp.mean(centred * centred, axis=-1, keepdims=True)
    return centred * lax.rsqrt(var + eps_norm) * gain


def send_kernel(table_ref, w_ref, ids_ref, sent_ref, kv_ref, q_ref):
    table = table_ref[...]
    cols = w_ref.shape[2]
    kv_ref[:, :cols] = dot(table, w_ref[1]).astype(bf)
    kv_ref[:, cols:] = dot(table, w_ref[2]).astype(bf)
    kv = kv_ref[...]
    nodes = table.shape[0]
    ids = ids_ref[...].astype(f32).T.astype(jnp.int32)
    for tile in range(ids.shape[1]):
        lanes = lax.broadcasted_iota(jnp.int32, (TILE, nodes), 1)
        hot = jnp.where(lanes == ids[:, tile : tile + 1], 1.0, 0.0).astype(bf)
        sent_ref[tile * TILE : (tile + 1) * TILE, :] = dot(hot, kv).astype(bf)
    q_ref[...] = dot(table, w_ref[0]).astype(bf)


def mask_kernel(slots_ref, mask_ref):
    rows = slots_ref.shape[0]
    for tile in range(rows // TILE):
        slots = slots_ref[tile * TILE : (tile + 1) * TILE, :]
        lanes = lax.broadcasted_iota(jnp.int32, (TILE, TPR * TILE), 1)
        edges = lanes == lax.broadcasted_iota(jnp.int32, (TILE, TPR * TILE), 0)
        for edge in range(DEG):
            edges = edges | (lanes == slots[:, edge : edge + 1])
        mask_ref[tile * TILE : (tile + 1) * TILE, :] = jnp.where(edges, 1.0, 0.0).astype(bf)


def attn_kernel(who_ref, titles_ref, w_in_ref, w_out_ref, *refs):
    outs, total = refs[:-1], refs[-1]
    titles = titles_ref[...]
    q = dot(titles, w_in_ref[0]).astype(bf)
    k = dot(titles, w_in_ref[1]).astype(bf)
    v = dot(titles, w_in_ref[2]).astype(bf)
    cols = q.shape[1]
    heads = cols // HD
    lanes = lax.broadcasted_iota(jnp.int32, (SEQ, cols), 1) // HD
    for title in range(titles.shape[0] // SEQ):
        rows = slice(title * SEQ, (title + 1) * SEQ)
        qt, kt, vt = q[rows], k[rows], v[rows]
        stacked = jnp.concatenate(
            [jnp.where(lanes == h, qt, jnp.zeros_like(qt)) for h in range(heads)], axis=0
        )
        scores = dot_nt(stacked, kt) * (1.0 / HD**0.5)
        expo = jnp.exp(scores - jnp.max(scores, axis=-1, keepdims=True))
        probs = (expo / jnp.sum(expo, axis=-1, keepdims=True)).astype(bf)
        mixed = dot(probs, vt)
        context = mixed[:SEQ]
        for h in range(1, heads):
            context = jnp.where(lanes == h, mixed[h * SEQ : (h + 1) * SEQ], context)
        total[rows, :] = dot(context.astype(bf), w_out_ref[...])
    chunk = outs[0].shape[0]
    for step, out in enumerate(outs):
        out[...] = total[pl.ds(pl.multiple_of(who_ref[step] * chunk, chunk), chunk), :].astype(out.dtype)


def norm_one_kernel(who_ref, titles_ref, gains_ref, own_ref, *refs):
    parts, out = refs[:-1], refs[-1]
    chunk = own_ref.shape[0]
    total = own_ref[...]
    for part in parts:
        total = total + part[...].astype(f32)
    base = titles_ref[pl.ds(pl.multiple_of(who_ref[0] * chunk, chunk), chunk), :].astype(f32)
    out[...] = layer_norm(base + total, gains_ref[0:1, :]).astype(bf)


def gelu(x):
    return 0.5 * x * (1.0 + lax.erf(x * (0.5**0.5)))


def ffn_kernel(w_in_ref, w_out_ref, *refs):
    count = len(refs) // 2
    ins, outs = refs[:count], refs[count:]
    chunk = ins[0].shape[0]
    hidden = jnp.concatenate([ref[...] for ref in ins], axis=0)
    inner = gelu(dot(hidden, w_in_ref[...])).astype(bf)
    total = dot(inner, w_out_ref[...])
    for step, out in enumerate(outs):
        out[...] = total[step * chunk : (step + 1) * chunk].astype(out.dtype)


def norm_two_kernel(hidden_ref, gains_ref, own_ref, *refs):
    parts, out, first = refs[:-2], refs[-2], refs[-1]
    total = own_ref[...]
    for part in parts:
        total = total + part[...].astype(f32)
    done = layer_norm(hidden_ref[...].astype(f32) + total, gains_ref[1:2, :]).astype(bf)
    out[...] = done
    first[...] = done[0:1]


def place_kernel(who_ref, *refs):
    chunks, out = refs[:-1], refs[-1]
    chunk = chunks[0].shape[0]
    for step, ref in enumerate(chunks):
        out[pl.ds(pl.multiple_of(who_ref[step] * chunk, chunk), chunk), :] = ref[...]


def graph_kernel(
    cols_ref, nodes_ref, place_ref, q_ref, kv_ref, far_ref, codes_ref, firsts_ref, w_ref, mask_ref,
    out_ref, k_all, v_all,
):
    cols = q_ref.shape[1]
    firsts = firsts_ref[...]
    count = firsts.shape[0]
    first_kv = jnp.concatenate([dot(firsts, w_ref[1]), dot(firsts, w_ref[2])], axis=1).astype(bf)
    first_q = dot(firsts, w_ref[0]).astype(bf)
    codes = codes_ref[...].astype(f32).T.astype(jnp.int32)
    nodes = q_ref.shape[0]
    row_tiles = nodes // TILE
    lanes = lax.broadcasted_iota(jnp.int32, (TILE, count), 1)
    sub = lax.broadcasted_iota(jnp.int32, (TILE, 1), 0)

    def own_code(tile):
        code = jnp.full((TILE, 1), -1, jnp.int32)
        for title in range(nodes_ref.shape[0]):
            code = jnp.where(sub + tile * TILE == nodes_ref[title], place_ref[title], code)
        return code

    for tile in range(row_tiles + far_ref.shape[0] // TILE):
        if tile < row_tiles:
            code = own_code(tile)
            rows = kv_ref[tile * TILE : (tile + 1) * TILE, :]
        else:
            far = tile - row_tiles
            code = codes[:, far : far + 1]
            rows = far_ref[far * TILE : (far + 1) * TILE, :]
        hot = jnp.where(lanes == code, 1.0, 0.0).astype(bf)
        fixed = jnp.where(code >= 0, dot(hot, first_kv), rows.astype(f32)).astype(bf)
        k_all[tile * TILE : (tile + 1) * TILE, :] = fixed[:, :cols]
        v_all[tile * TILE : (tile + 1) * TILE, :] = fixed[:, cols:]

    heads = cols // GHD
    head_of = lax.broadcasted_iota(jnp.int32, (TILE, cols), 1) // GHD
    for tile in range(row_tiles):
        code = own_code(tile)
        hot = jnp.where(lanes == code, 1.0, 0.0).astype(bf)
        rows = q_ref[tile * TILE : (tile + 1) * TILE, :].astype(f32)
        q = jnp.where(code >= 0, dot(hot, first_q), rows)
        stacked = jnp.concatenate(
            [jnp.where(head_of == h, q, 0.0) for h in range(heads)], axis=0
        ).astype(bf)
        starts = [pl.multiple_of(cols_ref[tile, c] * TILE, TILE) for c in range(TPR)]
        scores = jnp.concatenate(
            [dot_nt(stacked, k_all[pl.ds(start, TILE), :]) for start in starts], axis=1
        ) * (1.0 / GHD**0.5)
        mask = mask_ref[tile * TILE : (tile + 1) * TILE, :].astype(f32)
        mask = jnp.concatenate([mask] * heads, axis=0) > 0.5
        masked = jnp.where(mask, scores, -jnp.inf)
        expo = jnp.exp(masked - jnp.max(masked, axis=-1, keepdims=True))
        weights = (expo / jnp.sum(expo, axis=-1, keepdims=True)).astype(bf)
        mixed = jnp.zeros((heads * TILE, cols), f32)
        for c, start in enumerate(starts):
            mixed = mixed + dot(weights[:, c * TILE : (c + 1) * TILE], v_all[pl.ds(start, TILE), :])
        out = mixed[:TILE]
        for h in range(1, heads):
            out = jnp.where(head_of == h, mixed[h * TILE : (h + 1) * TILE], out)
        out_ref[tile * TILE : (tile + 1) * TILE, :] = out.astype(bf)


def local(

    titles,
    w_attn_in,
    w_attn_out,
    w_ffn_in,
    w_ffn_out,
    gains,
    node_table,
    w_graph,
    title_nodes,
    send_ids,
    tile_cols,
    nbr_slots,
):
    tok_rows, width = titles.shape
    nodes = node_table.shape[0]
    cols = w_graph.shape[2]
    mp = lax.axis_size("mp")
    dp = lax.axis_size("dp")
    me_mp = lax.axis_index("mp").astype(jnp.int32)
    me_dp = lax.axis_index("dp").astype(jnp.int32)
    who = me_mp ^ jnp.arange(mp, dtype=jnp.int32)
    chunk = tok_rows // mp
    per_part = title_nodes.shape[0]
    fetch = send_ids.shape[2]

    def swap(value, step):
        return lax.ppermute(value, "mp", [(i, i ^ step) for i in range(mp)])

    ids = send_ids.reshape(-1, TILE)
    sent, kv, q = call(
        send_kernel,
        (shape((dp * fetch, 2 * cols), bf), shape((nodes, 2 * cols), bf), shape((nodes, cols), bf)),
        (node_table, w_graph, ids),
        flops=2 * nodes * width * 3 * cols + 2 * dp * fetch * nodes * 2 * cols,
        name="send",
    )
    far = lax.all_to_all(
        sent.reshape(dp, fetch, 2 * cols), "dp", split_axis=0, concat_axis=0, tiled=True
    ).reshape(dp * fetch, 2 * cols)
    titles_at = jnp.arange(per_part, dtype=jnp.int32) * SEQ // chunk
    place = me_dp * mp + titles_at
    code = jnp.full(send_ids.shape[1:], -1, jnp.int32)
    for title in range(per_part):
        code = jnp.where(send_ids[0] == title_nodes[title], place[title], code)
    codes = lax.all_to_all(code, "dp", split_axis=0, concat_axis=0, tiled=True).reshape(-1, TILE)

    terms = call(
        attn_kernel,
        tuple(shape((chunk, width), bf if step else f32) for step in range(mp)),
        (who, titles, w_attn_in, w_attn_out),
        smem=(0,),
        scratch=[pltpu.VMEM((tok_rows, width), f32)],
        flops=2 * tok_rows * width * 4 * w_attn_in.shape[2],
        name="attn",
    )
    parts = [swap(terms[step], step) for step in range(1, mp)]
    hidden = call(
        norm_one_kernel,
        shape((chunk, width), bf),
        (who, titles, gains, terms[0], *parts),
        smem=(0,),
        name="norm_one",
    )
    hiddens = [hidden] + [swap(hidden, step) for step in range(1, mp)]
    terms = call(
        ffn_kernel,
        tuple(shape((chunk, width), bf if step else f32) for step in range(mp)),
        (w_ffn_in, w_ffn_out, *hiddens),
        flops=4 * tok_rows * width * w_ffn_in.shape[1],
        name="ffn",
    )
    parts = [swap(terms[step], step) for step in range(1, mp)]
    done, first = call(
        norm_two_kernel,
        (shape((chunk, width), bf), shape((1, width), bf)),
        (hidden, gains, terms[0], *parts),
        name="norm_two",
    )
    firsts = lax.all_to_all(
        jnp.broadcast_to(first, (dp * mp, width)), ("dp", "mp"), split_axis=0, concat_axis=0, tiled=True
    )
    dones = [done] + [swap(done, step) for step in range(1, mp)]
    encoded = call(
        place_kernel, shape((tok_rows, width), bf), (who, *dones), smem=(0,), name="place"
    )

    mask = call(mask_kernel, shape((nodes, TPR * TILE), bf), (nbr_slots,), flops=10**9, name="mask")
    graph_out = call(
        graph_kernel,
        shape((nodes, cols), bf),
        (tile_cols, title_nodes, place, q, kv, far, codes, firsts, w_graph, mask),
        smem=(0, 1, 2),
        scratch=[
            pltpu.VMEM((nodes + dp * fetch, cols), bf),
            pltpu.VMEM((nodes + dp * fetch, cols), bf),
        ],
        flops=10**9,
        name="graph",
    )
    return (encoded, graph_out)


def solution(mesh):
    in_specs = (
        P("dp", None),
        P(None, None, "mp"),
        P("mp", None),
        P(None, "mp"),
        P("mp", None),
        P(),
        P("dp", None),
        P(None, None, "mp"),
        P("dp"),
        P("dp", None, None),
        P("dp", None),
        P("dp", None),
    )
    out_specs = (P("dp", None), P("dp", "mp"))
    return jax.shard_map(
        local, mesh=mesh, in_specs=in_specs, out_specs=out_specs, check_vma=False
    )
```

```python
import jax
import jax.numpy as jnp
from jax import lax
from jax.experimental import pallas as pl
from jax.experimental.pallas import tpu as pltpu
from jax.sharding import PartitionSpec as P

SEQ = 128
TILE = 128
DEG = 16
TPR = 6
HD = 64
GHD = 96

eps_norm = 1e-06
bf = jnp.bfloat16
f32 = jnp.float32

VMEM = pl.BlockSpec(memory_space=pltpu.VMEM)
SMEM = pl.BlockSpec(memory_space=pltpu.SMEM)
HBM = pl.BlockSpec(memory_space=pl.ANY)
AUTO = pl.BlockSpec()
NT = (((1,), (1,)), ((), ()))
TN = (((0,), (0,)), ((), ()))


def call(kernel, outs, args, smem=(), hbm=(), auto=(), scratch=(), out_specs=None, flops=0, name=None):
    def spec(i):
        return SMEM if i in smem else HBM if i in hbm else AUTO if i in auto else VMEM

    specs = [spec(i) for i in range(len(args))]
    nbytes = sum(a.size * a.dtype.itemsize for a in args)
    return pl.pallas_call(
        kernel,
        out_shape=outs,
        in_specs=specs,
        out_specs=jax.tree.map(lambda _: VMEM, outs) if out_specs is None else out_specs,
        scratch_shapes=list(scratch),
        compiler_params=pltpu.CompilerParams(vmem_limit_bytes=40 * 1024 * 1024),
        cost_estimate=pl.CostEstimate(flops=flops, bytes_accessed=nbytes, transcendentals=0),
        name=name,
    )(*args)


def shape(dims, dtype):
    return jax.ShapeDtypeStruct(dims, dtype)


def dot(a, b):
    return jnp.dot(a, b, preferred_element_type=f32)


def dot_nt(a, b):
    return lax.dot_general(a, b, NT, preferred_element_type=f32)


def dot_tn(a, b):
    return lax.dot_general(a, b, TN, preferred_element_type=f32)


def layer_norm(values, gain):
    mean = jnp.mean(values, axis=-1, keepdims=True)
    centred = values - mean
    var = jnp.mean(centred * centred, axis=-1, keepdims=True)
    return centred * lax.rsqrt(var + eps_norm) * gain


def send_kernel(me_ref, at_ref, ids_ref, table_ref, w_ref, sent_ref, kv_ref, q_ref):
    table = table_ref[...]
    cols = w_ref.shape[1]
    kv = jnp.concatenate([dot_nt(table, w_ref[1]), dot_nt(table, w_ref[2])], axis=1).astype(bf)
    kv_ref[...] = kv
    nodes = table.shape[0]
    per_part = at_ref.shape[0]
    parts, fetch = ids_ref.shape
    ids = ids_ref[...].astype(f32).T.astype(jnp.int32)
    lanes = lax.broadcasted_iota(jnp.int32, (fetch, nodes), 1)
    lead = lax.broadcasted_iota(jnp.int32, (fetch, 2 * cols), 1) == 0
    for part in range(parts):
        picked = ids[:, part : part + 1]
        hot = jnp.where(lanes == picked, 1.0, 0.0).astype(bf)
        rows = dot(hot, kv)
        code = jnp.full((fetch, 1), -1, jnp.int32)
        for title in range(per_part):
            code = jnp.where(picked == at_ref[title], me_ref[0] * per_part + title, code)
        mark = jnp.where(lead, jnp.nan, code.astype(f32))
        sent_ref[part * fetch : (part + 1) * fetch, :] = jnp.where(code >= 0, mark, rows).astype(bf)
    q_ref[...] = dot_nt(w_ref[0], table).astype(bf)


def mask_kernel(slots_ref, mask_ref):
    nodes = slots_ref.shape[1]
    for tile in range(nodes // TILE):
        slots = slots_ref[:, tile * TILE : (tile + 1) * TILE]
        keys = lax.broadcasted_iota(jnp.int32, (TPR * TILE, TILE), 0)
        edges = keys == lax.broadcasted_iota(jnp.int32, (TPR * TILE, TILE), 1)
        for edge in range(DEG):
            edges = edges | (keys == slots[edge : edge + 1, :])
        mask_ref[:, tile * TILE : (tile + 1) * TILE] = jnp.where(edges, 1.0, 0.0).astype(bf)


def attn_kernel(who_ref, titles_ref, w_in_ref, w_out_ref, *refs):
    outs, total = refs[:-1], refs[-1]
    titles = titles_ref[...]
    q = dot_nt(titles, w_in_ref[0]).astype(bf)
    k = dot_nt(titles, w_in_ref[1]).astype(bf)
    v = dot_nt(titles, w_in_ref[2]).astype(bf)
    cols = q.shape[1]
    heads = cols // HD
    lanes = lax.broadcasted_iota(jnp.int32, (SEQ, cols), 1) // HD
    for title in range(titles.shape[0] // SEQ):
        rows = slice(title * SEQ, (title + 1) * SEQ)
        qt, kt, vt = q[rows], k[rows], v[rows]
        stacked = jnp.concatenate(
            [jnp.where(lanes == h, qt, jnp.zeros_like(qt)) for h in range(heads)], axis=0
        )
        scores = dot_nt(stacked, kt) * (1.0 / HD**0.5)
        expo = jnp.exp(scores - jnp.max(scores, axis=-1, keepdims=True))
        probs = (expo / jnp.sum(expo, axis=-1, keepdims=True)).astype(bf)
        mixed = dot(probs, vt)
        context = mixed[:SEQ]
        for h in range(1, heads):
            context = jnp.where(lanes == h, mixed[h * SEQ : (h + 1) * SEQ], context)
        total[rows, :] = dot(context.astype(bf), w_out_ref[...])
    chunk = outs[0].shape[0]
    for step, out in enumerate(outs):
        out[...] = total[pl.ds(pl.multiple_of(who_ref[step] * chunk, chunk), chunk), :].astype(out.dtype)


def norm_one_kernel(who_ref, titles_ref, gains_ref, own_ref, *refs):
    parts, out = refs[:-1], refs[-1]
    chunk = own_ref.shape[0]
    total = own_ref[...]
    for part in parts:
        total = total + part[...].astype(f32)
    base = titles_ref[pl.ds(pl.multiple_of(who_ref[0] * chunk, chunk), chunk), :].astype(f32)
    out[...] = layer_norm(base + total, gains_ref[0:1, :]).astype(bf)


def gelu(x):
    return 0.5 * x * (1.0 + lax.erf(x * (0.5**0.5)))


def ffn_kernel(w_in_ref, w_out_ref, *refs):
    count = len(refs) // 2
    ins, outs = refs[:count], refs[count:]
    chunk = ins[0].shape[0]
    hidden = jnp.concatenate([ref[...] for ref in ins], axis=0)
    inner = gelu(dot(hidden, w_in_ref[...])).astype(bf)
    total = dot(inner, w_out_ref[...])
    for step, out in enumerate(outs):
        out[...] = total[step * chunk : (step + 1) * chunk].astype(out.dtype)


def norm_two_kernel(hidden_ref, gains_ref, own_ref, *refs):
    parts, out = refs[:-1], refs[-1]
    total = own_ref[...]
    for part in parts:
        total = total + part[...].astype(f32)
    out[...] = layer_norm(hidden_ref[...].astype(f32) + total, gains_ref[1:2, :]).astype(bf)


def place_kernel(who_ref, *refs):
    chunks, out, first = refs[:-2], refs[-2], refs[-1]
    chunk = chunks[0].shape[0]
    for step, ref in enumerate(chunks):
        out[pl.ds(pl.multiple_of(who_ref[step] * chunk, chunk), chunk), :] = ref[...]
    for title in range(first.shape[0]):
        first[title : title + 1, :] = out[title * SEQ : title * SEQ + 1, :]


def graph_kernel(
    cols_ref, at_ref, me_ref, firsts_ref, q_hbm, kv_hbm, far_hbm, w_hbm, mask_hbm,
    out_ref, k_all, v_all, q_ref, kv_ref, far_ref, w_ref, mask_ref, sems,
):
    moves = [
        pltpu.make_async_copy(source, target, sems.at[i])
        for i, (source, target) in enumerate(
            ((w_hbm, w_ref), (kv_hbm, kv_ref), (far_hbm, far_ref), (q_hbm, q_ref), (mask_hbm, mask_ref))
        )
    ]
    for move in moves:
        move.start()
    cols, nodes = q_ref.shape
    row_tiles = nodes // TILE
    per_part = at_ref.shape[0]
    firsts = firsts_ref[...]
    count = firsts.shape[0]
    moves[0].wait()
    first_kv = jnp.concatenate([dot_nt(firsts, w_ref[1]), dot_nt(firsts, w_ref[2])], axis=1).astype(bf)
    first_q = dot_nt(w_ref[0], firsts)
    lanes = lax.broadcasted_iota(jnp.int32, (TILE, count), 1).astype(f32)
    sub = lax.broadcasted_iota(jnp.int32, (TILE, 1), 0)
    slots = lax.broadcasted_iota(jnp.int32, (1, count), 1)

    moves[1].wait()
    for tile in range(row_tiles + far_ref.shape[0] // TILE):
        if tile < row_tiles:
            rows = kv_ref[tile * TILE : (tile + 1) * TILE, :].astype(f32)
            code = jnp.full((TILE, 1), -1, jnp.int32)
            for title in range(per_part):
                mine = me_ref[0] * per_part + title
                code = jnp.where(sub + tile * TILE == at_ref[title], mine, code)
            code = code.astype(f32)
        else:
            if tile == row_tiles:
                moves[2].wait()
            far = tile - row_tiles
            rows = far_ref[far * TILE : (far + 1) * TILE, :].astype(f32)
            code = jnp.where(rows[:, 0:1] != rows[:, 0:1], rows[:, 1:2], -1.0)
        hot = jnp.where(lanes == code, 1.0, 0.0).astype(bf)
        fixed = jnp.where(code >= 0.0, dot(hot, first_kv), rows).astype(bf)
        k_all[tile * TILE : (tile + 1) * TILE, :] = fixed[:, :cols]
        v_all[tile * TILE : (tile + 1) * TILE, :] = fixed[:, cols:]

    moves[3].wait()
    moves[4].wait()
    heads = cols // GHD
    head_of = lax.broadcasted_iota(jnp.int32, (cols, TILE), 0) // GHD
    node_lane = lax.broadcasted_iota(jnp.int32, (cols, TILE), 1)
    own_q = [
        jnp.sum(jnp.where(slots == me_ref[0] * per_part + title, first_q, 0.0), axis=1, keepdims=True)
        for title in range(per_part)
    ]
    for tile in range(row_tiles):
        q = q_ref[:, tile * TILE : (tile + 1) * TILE].astype(f32)
        for title in range(per_part):
            q = jnp.where(node_lane + tile * TILE == at_ref[title], own_q[title], q)
        stacked = jnp.concatenate(
            [jnp.where(head_of == h, q, 0.0) for h in range(heads)], axis=1
        ).astype(bf)
        starts = [pl.multiple_of(cols_ref[tile, c] * TILE, TILE) for c in range(TPR)]
        scores = jnp.concatenate(
            [dot(k_all[pl.ds(start, TILE), :], stacked) for start in starts], axis=0
        ) * (1.0 / GHD**0.5)
        mask = mask_ref[:, tile * TILE : (tile + 1) * TILE].astype(f32)
        mask = jnp.concatenate([mask] * heads, axis=1) > 0.5
        masked = jnp.where(mask, scores, -jnp.inf)
        expo = jnp.exp(masked - jnp.max(masked, axis=0, keepdims=True))
        weights = (expo * (1.0 / jnp.sum(expo, axis=0, keepdims=True))).astype(bf)
        mixed = jnp.zeros((cols, heads * TILE), f32)
        for c, start in enumerate(starts):
            mixed = mixed + dot_tn(v_all[pl.ds(start, TILE), :], weights[c * TILE : (c + 1) * TILE])
        out = mixed[:, :TILE]
        for h in range(1, heads):
            out = jnp.where(head_of == h, mixed[:, h * TILE : (h + 1) * TILE], out)
        out_ref[:, tile * TILE : (tile + 1) * TILE] = out.astype(bf)


def local(

    titles,
    w_attn_in,
    w_attn_out,
    w_ffn_in,
    w_ffn_out,
    gains,
    node_table,
    w_graph,
    title_nodes,
    send_ids,
    tile_cols,
    nbr_slots,
):
    tok_rows, width = titles.shape
    nodes = node_table.shape[0]
    cols = w_graph.shape[2]
    mp = lax.axis_size("mp")
    dp = lax.axis_size("dp")
    me_mp = lax.axis_index("mp").astype(jnp.int32)
    me_dp = lax.axis_index("dp").astype(jnp.int32).reshape(1)
    who = me_mp ^ jnp.arange(mp, dtype=jnp.int32)
    chunk = tok_rows // mp
    per_part = title_nodes.shape[0]
    fetch = send_ids.shape[2]

    def swap(value, step):
        return lax.ppermute(value, "mp", [(i, i ^ step) for i in range(mp)])

    w_attn_in = jnp.swapaxes(w_attn_in, 1, 2)
    w_graph = jnp.swapaxes(w_graph, 1, 2)
    sent, kv, q = call(
        send_kernel,
        (shape((dp * fetch, 2 * cols), bf), shape((nodes, 2 * cols), bf), shape((cols, nodes), bf)),
        (me_dp, title_nodes, send_ids[0], node_table, w_graph),
        smem=(0, 1),
        auto=(2, 3, 4),

        flops=2 * nodes * width * 3 * cols + 2 * dp * fetch * nodes * 2 * cols,
        name="send",
    )
    far = lax.all_to_all(
        sent.reshape(dp, fetch, 2 * cols), "dp", split_axis=0, concat_axis=0, tiled=True
    ).reshape(dp * fetch, 2 * cols)
    titles, _ = lax.optimization_barrier((titles, sent))

    terms = call(
        attn_kernel,
        tuple(shape((chunk, width), bf if step else f32) for step in range(mp)),
        (who, titles, w_attn_in, w_attn_out),
        smem=(0,),
        auto=(1, 2, 3),
        scratch=[pltpu.VMEM((tok_rows, width), f32)],
        flops=2 * tok_rows * width * 4 * w_attn_in.shape[1],
        name="attn",
    )
    parts = [swap(terms[step], step) for step in range(1, mp)]
    hidden = call(
        norm_one_kernel,
        shape((chunk, width), bf),
        (who, titles, gains, terms[0], *parts),
        smem=(0,),
        name="norm_one",
    )
    hiddens = [hidden] + [swap(hidden, step) for step in range(1, mp)]
    terms = call(
        ffn_kernel,
        tuple(shape((chunk, width), bf if step else f32) for step in range(mp)),
        (w_ffn_in, w_ffn_out, *hiddens),
        flops=4 * tok_rows * width * w_ffn_in.shape[1],
        name="ffn",
    )
    parts = [swap(terms[step], step) for step in range(1, mp)]
    done = call(
        norm_two_kernel,
        shape((chunk, width), bf),
        (hidden, gains, terms[0], *parts),
        name="norm_two",
    )
    dones = [done] + [swap(done, step) for step in range(1, mp)]
    encoded, first = call(
        place_kernel,
        (shape((tok_rows, width), bf), shape((per_part, width), bf)),
        (who, *dones),
        smem=(0,),
        name="place",
    )
    firsts = lax.all_gather(first, "dp", axis=0, tiled=True)

    mask = call(
        mask_kernel, shape((TPR * TILE, nodes), bf), (nbr_slots.T,), flops=10**9, name="mask"
    )
    graph_out = call(
        graph_kernel,
        shape((cols, nodes), bf),
        (tile_cols, title_nodes, me_dp, firsts, q, kv, far, w_graph, mask),
        smem=(0, 1, 2),
        hbm=(4, 5, 6, 7, 8),
        scratch=[
            pltpu.VMEM((nodes + dp * fetch, cols), bf),
            pltpu.VMEM((nodes + dp * fetch, cols), bf),
            pltpu.VMEM(q.shape, bf),
            pltpu.VMEM(kv.shape, bf),
            pltpu.VMEM(far.shape, bf),
            pltpu.VMEM(w_graph.shape, bf),
            pltpu.VMEM(mask.shape, bf),
            pltpu.SemaphoreType.DMA((5,)),
        ],
        flops=10**9,
        name="graph",
    )
    return (encoded, graph_out.T)


def solution(mesh):
    in_specs = (
        P("dp", None),
        P(None, None, "mp"),
        P("mp", None),
        P(None, "mp"),
        P("mp", None),
        P(),
        P("dp", None),
        P(None, None, "mp"),
        P("dp"),
        P("dp", None, None),
        P("dp", None),
        P("dp", None),
    )
    out_specs = (P("dp", None), P("dp", "mp"))
    return jax.shard_map(
        local, mesh=mesh, in_specs=in_specs, out_specs=out_specs, check_vma=False
    )
```

```python
import jax
import jax.numpy as jnp
from jax import lax
from jax.experimental import pallas as pl
from jax.experimental.pallas import tpu as pltpu
from jax.sharding import PartitionSpec as P

SEQ = 128
TILE = 128
DEG = 16
TPR = 6
HD = 64
GHD = 96

eps_norm = 1e-06
bf = jnp.bfloat16
f32 = jnp.float32

VMEM = pl.BlockSpec(memory_space=pltpu.VMEM)
SMEM = pl.BlockSpec(memory_space=pltpu.SMEM)
ANY = pl.BlockSpec(memory_space=pl.ANY)
NT = (((1,), (1,)), ((), ()))
TN = (((0,), (0,)), ((), ()))


def call(kernel, outs, args, smem=(), hbm=(), scratch=(), flops=0, name=None):
    count, out_count, own = len(args), len(jax.tree.leaves(outs)), len(scratch)
    specs = [SMEM if i in smem else ANY if i in hbm else VMEM for i in range(count)]
    nbytes = sum(a.size * a.dtype.itemsize for a in args)
    buffers = [pltpu.VMEM(args[i].shape, args[i].dtype) for i in hbm]
    sems = [pltpu.SemaphoreType.DMA((len(hbm),))] if hbm else []

    def body(*refs):
        ins, rest = list(refs[:count]), refs[count:]
        kept, moved = rest[: out_count + own], rest[out_count + own :]
        moves = {}
        for j, i in enumerate(hbm):
            moves[i] = pltpu.make_async_copy(ins[i], moved[j], moved[-1].at[j])
            moves[i].start()
            ins[i] = moved[j]

        def ready(*wanted):
            for i in wanted:
                moves[i].wait()

        kernel(ready, *ins, *kept)

    return pl.pallas_call(
        body,
        out_shape=outs,
        in_specs=specs,
        out_specs=jax.tree.map(lambda _: VMEM, outs),
        scratch_shapes=list(scratch) + buffers + sems,
        compiler_params=pltpu.CompilerParams(vmem_limit_bytes=40 * 1024 * 1024),
        cost_estimate=pl.CostEstimate(flops=flops, bytes_accessed=nbytes, transcendentals=0),
        name=name,
    )(*args)


def shape(dims, dtype):
    return jax.ShapeDtypeStruct(dims, dtype)


def dot(a, b):
    return jnp.dot(a, b, preferred_element_type=f32)


def dot_nt(a, b):
    return lax.dot_general(a, b, NT, preferred_element_type=f32)


def dot_tn(a, b):
    return lax.dot_general(a, b, TN, preferred_element_type=f32)


def layer_norm(values, gain):
    mean = jnp.mean(values, axis=-1, keepdims=True)
    centred = values - mean
    var = jnp.mean(centred * centred, axis=-1, keepdims=True)
    return centred * lax.rsqrt(var + eps_norm) * gain


def send_kernel(ready, me_ref, at_ref, ids_ref, table_ref, w_ref, kv_ref, q_ref, sent_ref):
    cols = w_ref.shape[1]
    per_part = at_ref.shape[0]
    fetch, nodes = ids_ref.shape[1], table_ref.shape[0]
    ready(2, 3, 4)
    table = table_ref[...]
    kv = jnp.concatenate([dot_nt(table, w_ref[1]), dot_nt(table, w_ref[2])], axis=1).astype(bf)
    ids = ids_ref[...].astype(f32).T.astype(jnp.int32)
    lanes = lax.broadcasted_iota(jnp.int32, (fetch, nodes), 1)
    lead = lax.broadcasted_iota(jnp.int32, (fetch, 2 * cols), 1) == 0
    for part in range(ids.shape[1]):
        step = me_ref[0] ^ part
        picked = ids[:, part : part + 1]
        hot = jnp.where(lanes == picked, 1.0, 0.0).astype(bf)
        rows = dot(hot, kv)
        code = jnp.full((fetch, 1), -1, jnp.int32)
        for title in range(per_part):
            code = jnp.where(picked == at_ref[title], step * per_part + title, code)
        mark = jnp.where(lead, jnp.nan, code.astype(f32))
        sent_ref[part * fetch : (part + 1) * fetch, :] = jnp.where(code >= 0, mark, rows).astype(bf)
    kv_ref[...] = kv
    q_ref[...] = dot_nt(table, w_ref[0]).astype(bf)


def mask_kernel(ready, slots_ref, mask_ref):
    all_slots = slots_ref[...].astype(f32).T.astype(jnp.int32)
    for tile in range(all_slots.shape[0] // TILE):
        slots = all_slots[tile * TILE : (tile + 1) * TILE, :]
        lanes = lax.broadcasted_iota(jnp.int32, (TILE, TPR * TILE), 1)
        edges = lanes == lax.broadcasted_iota(jnp.int32, (TILE, TPR * TILE), 0)
        for edge in range(DEG):
            edges = edges | (lanes == slots[:, edge : edge + 1])
        mask_ref[tile * TILE : (tile + 1) * TILE, :] = jnp.where(edges, 1.0, 0.0).astype(bf)


def attn_kernel(ready, who_ref, titles_ref, w_in_ref, w_out_ref, *refs):
    outs, total = refs[:-1], refs[-1]
    titles = titles_ref[...]
    q = dot_nt(titles, w_in_ref[0]).astype(bf)
    k = dot_nt(titles, w_in_ref[1]).astype(bf)
    v = dot_nt(titles, w_in_ref[2]).astype(bf)
    cols = q.shape[1]
    heads = cols // HD
    lanes = lax.broadcasted_iota(jnp.int32, (SEQ, cols), 1) // HD
    for title in range(titles.shape[0] // SEQ):
        rows = slice(title * SEQ, (title + 1) * SEQ)
        qt, kt, vt = q[rows], k[rows], v[rows]
        stacked = jnp.concatenate(
            [jnp.where(lanes == h, qt, jnp.zeros_like(qt)) for h in range(heads)], axis=0
        )
        scores = dot_nt(stacked, kt) * (1.0 / HD**0.5)
        expo = jnp.exp(scores - jnp.max(scores, axis=-1, keepdims=True))
        probs = (expo / jnp.sum(expo, axis=-1, keepdims=True)).astype(bf)
        mixed = dot(probs, vt)
        context = mixed[:SEQ]
        for h in range(1, heads):
            context = jnp.where(lanes == h, mixed[h * SEQ : (h + 1) * SEQ], context)
        total[rows, :] = dot(context.astype(bf), w_out_ref[...])
    chunk = outs[0].shape[0]
    for step, out in enumerate(outs):
        out[...] = total[pl.ds(pl.multiple_of(who_ref[step] * chunk, chunk), chunk), :].astype(out.dtype)


def norm_one_kernel(ready, who_ref, titles_ref, gains_ref, own_ref, *refs):
    parts, out = refs[:-1], refs[-1]
    chunk = own_ref.shape[0]
    total = own_ref[...]
    for part in parts:
        total = total + part[...].astype(f32)
    base = titles_ref[pl.ds(pl.multiple_of(who_ref[0] * chunk, chunk), chunk), :].astype(f32)
    out[...] = layer_norm(base + total, gains_ref[0:1, :]).astype(bf)


def gelu(x):
    return 0.5 * x * (1.0 + lax.erf(x * (0.5**0.5)))


def ffn_kernel(ready, w_in_ref, w_out_ref, *refs):
    count = len(refs) // 2
    ins, outs = refs[:count], refs[count:]
    chunk = ins[0].shape[0]
    hidden = jnp.concatenate([ref[...] for ref in ins], axis=0)
    inner = gelu(dot(hidden, w_in_ref[...])).astype(bf)
    total = dot(inner, w_out_ref[...])
    for step, out in enumerate(outs):
        out[...] = total[step * chunk : (step + 1) * chunk].astype(out.dtype)


def norm_two_kernel(ready, hidden_ref, gains_ref, own_ref, *refs):
    parts, out = refs[:-1], refs[-1]
    total = own_ref[...]
    for part in parts:
        total = total + part[...].astype(f32)
    out[...] = layer_norm(hidden_ref[...].astype(f32) + total, gains_ref[1:2, :]).astype(bf)


def place_kernel(ready, who_ref, *refs):
    chunks, out, first = refs[:-2], refs[-2], refs[-1]
    chunk = chunks[0].shape[0]
    for step, ref in enumerate(chunks):
        out[pl.ds(pl.multiple_of(who_ref[step] * chunk, chunk), chunk), :] = ref[...]
    for title in range(first.shape[0]):
        first[title : title + 1, :] = out[title * SEQ : title * SEQ + 1, :]


def graph_kernel(
    ready, cols_ref, at_ref, q_ref, kv_ref, w_ref, mask_ref, far_ref, *refs
):
    *firsts, out_ref, k_all, v_all, firsts_ref = refs
    nodes, cols = q_ref.shape
    per_part = at_ref.shape[0]
    row_tiles = nodes // TILE
    for step, ref in enumerate(firsts):
        firsts_ref[step * per_part : (step + 1) * per_part, :] = ref[...].astype(f32)
    first = firsts_ref[...].astype(bf)
    count = first.shape[0]
    ready(4)
    first_kv = jnp.concatenate([dot_nt(first, w_ref[1]), dot_nt(first, w_ref[2])], axis=1).astype(bf)
    first_q = dot_nt(first, w_ref[0])
    lanes = lax.broadcasted_iota(jnp.int32, (TILE, count), 1).astype(f32)
    sub = lax.broadcasted_iota(jnp.int32, (TILE, 1), 0)

    ready(3)
    for tile in range(row_tiles + far_ref.shape[0] // TILE):
        if tile < row_tiles:
            rows = kv_ref[tile * TILE : (tile + 1) * TILE, :].astype(f32)
            code = jnp.full((TILE, 1), -1.0, f32)
            for title in range(per_part):
                code = jnp.where(sub + tile * TILE == at_ref[title], float(title), code)
        else:
            if tile == row_tiles:
                ready(6)
            start = (tile - row_tiles) * TILE
            rows = far_ref[start : start + TILE, :].astype(f32)
            code = jnp.where(rows[:, 0:1] != rows[:, 0:1], rows[:, 1:2], -1.0)
        hot = jnp.where(lanes == code, 1.0, 0.0).astype(bf)
        fixed = jnp.where(code >= 0.0, dot(hot, first_kv), rows).astype(bf)
        k_all[tile * TILE : (tile + 1) * TILE, :] = fixed[:, :cols]
        v_all[tile * TILE : (tile + 1) * TILE, :] = fixed[:, cols:]

    ready(2, 5)
    heads = cols // GHD
    head_of = lax.broadcasted_iota(jnp.int32, (TILE, cols), 1) // GHD
    for tile in range(row_tiles):
        q = q_ref[tile * TILE : (tile + 1) * TILE, :].astype(f32)
        for title in range(per_part):
            q = jnp.where(sub + tile * TILE == at_ref[title], first_q[title : title + 1], q)
        stacked = jnp.concatenate(
            [jnp.where(head_of == h, q, 0.0) for h in range(heads)], axis=0
        ).astype(bf)
        starts = [pl.multiple_of(cols_ref[tile, c] * TILE, TILE) for c in range(TPR)]
        keys = jnp.concatenate([k_all[pl.ds(start, TILE), :] for start in starts], axis=0)
        values = jnp.concatenate([v_all[pl.ds(start, TILE), :] for start in starts], axis=0)
        scores = dot_nt(stacked, keys) * (1.0 / GHD**0.5)
        mask = mask_ref[tile * TILE : (tile + 1) * TILE, :].astype(f32)
        mask = jnp.concatenate([mask] * heads, axis=0) > 0.5
        masked = jnp.where(mask, scores, -jnp.inf)
        expo = jnp.exp(masked - jnp.max(masked, axis=-1, keepdims=True))
        weights = (expo * (1.0 / jnp.sum(expo, axis=-1, keepdims=True))).astype(bf)
        mixed = dot(weights, values)
        out = mixed[:TILE]
        for h in range(1, heads):
            out = jnp.where(head_of == h, mixed[h * TILE : (h + 1) * TILE], out)
        out_ref[:, tile * TILE : (tile + 1) * TILE] = out.T.astype(bf)


def local(

    titles,
    w_attn_in,
    w_attn_out,
    w_ffn_in,
    w_ffn_out,
    gains,
    node_table,
    w_graph,
    title_nodes,
    send_ids,
    tile_cols,
    nbr_slots,
):
    tok_rows, width = titles.shape
    nodes = node_table.shape[0]
    cols = w_graph.shape[2]
    mp = lax.axis_size("mp")
    dp = lax.axis_size("dp")
    me_mp = lax.axis_index("mp").astype(jnp.int32)
    me_dp = lax.axis_index("dp").astype(jnp.int32).reshape(1)
    who = me_mp ^ jnp.arange(mp, dtype=jnp.int32)
    chunk = tok_rows // mp
    per_part = title_nodes.shape[0]
    fetch = send_ids.shape[2]

    def swap(value, step, axis="mp"):
        return lax.ppermute(value, axis, [(i, i ^ step) for i in range(lax.axis_size(axis))])

    w_attn_in = jnp.swapaxes(w_attn_in, 1, 2)
    w_graph = jnp.swapaxes(w_graph, 1, 2)
    kv, q, sent = call(
        send_kernel,
        (shape((nodes, 2 * cols), bf), shape((nodes, cols), bf), shape((dp * fetch, 2 * cols), bf)),
        (me_dp, title_nodes, send_ids[0], node_table, w_graph),
        smem=(0, 1),
        hbm=(2, 3, 4),
        flops=2 * nodes * width * 3 * cols + 2 * dp * fetch * nodes * 2 * cols,
        name="send",
    )
    far = lax.all_to_all(
        sent.reshape(dp, fetch, 2 * cols), "dp", split_axis=0, concat_axis=0, tiled=True
    ).reshape(dp * fetch, 2 * cols)
    titles, _ = lax.optimization_barrier((titles, kv))

    terms = call(
        attn_kernel,
        tuple(shape((chunk, width), bf if step else f32) for step in range(mp)),
        (who, titles, w_attn_in, w_attn_out),
        smem=(0,),
        scratch=[pltpu.VMEM((tok_rows, width), f32)],
        flops=2 * tok_rows * width * 4 * w_attn_in.shape[1],
        name="attn",
    )
    parts = [swap(terms[step], step) for step in range(1, mp)]
    hidden = call(
        norm_one_kernel,
        shape((chunk, width), bf),
        (who, titles, gains, terms[0], *parts),
        smem=(0,),
        name="norm_one",
    )
    hiddens = [hidden] + [swap(hidden, step) for step in range(1, mp)]
    terms = call(
        ffn_kernel,
        tuple(shape((chunk, width), bf if step else f32) for step in range(mp)),
        (w_ffn_in, w_ffn_out, *hiddens),
        flops=4 * tok_rows * width * w_ffn_in.shape[1],
        name="ffn",
    )
    parts = [swap(terms[step], step) for step in range(1, mp)]
    done = call(
        norm_two_kernel,
        shape((chunk, width), bf),
        (hidden, gains, terms[0], *parts),
        name="norm_two",
    )
    dones = [done] + [swap(done, step) for step in range(1, mp)]
    encoded, first = call(
        place_kernel,
        (shape((tok_rows, width), bf), shape((per_part, width), bf)),
        (who, *dones),
        smem=(0,),
        name="place",
    )
    firsts = [first] + [swap(first, step, "dp") for step in range(1, dp)]

    mask = call(
        mask_kernel, shape((nodes, TPR * TILE), bf), (nbr_slots.T,), flops=10**9, name="mask"
    )
    keys = nodes + dp * fetch
    graph_out = call(
        graph_kernel,
        shape((cols, nodes), bf),
        (tile_cols, title_nodes, q, kv, w_graph, mask, far, *firsts),
        smem=(0, 1),
        hbm=(2, 3, 4, 5, 6),
        scratch=[
            pltpu.VMEM((keys, cols), bf),
            pltpu.VMEM((keys, cols), bf),
            pltpu.VMEM((dp * per_part, width), f32),
        ],
        flops=10**9,
        name="graph",
    )
    return (encoded, graph_out.T)


def solution(mesh):
    in_specs = (
        P("dp", None),
        P(None, None, "mp"),
        P("mp", None),
        P(None, "mp"),
        P("mp", None),
        P(),
        P("dp", None),
        P(None, None, "mp"),
        P("dp"),
        P("dp", None, None),
        P("dp", None),
        P("dp", None),
    )
    out_specs = (P("dp", None), P("dp", "mp"))
    return jax.shard_map(
        local, mesh=mesh, in_specs=in_specs, out_specs=out_specs, check_vma=False
    )
```

```python
import jax
import jax.numpy as jnp
from jax import lax
from jax.experimental import pallas as pl
from jax.experimental.pallas import tpu as pltpu
from jax.sharding import PartitionSpec as P

SEQ = 128
TILE = 128
DEG = 16
TPR = 6
HD = 64
GHD = 96

eps_norm = 1e-06
bf = jnp.bfloat16
f32 = jnp.float32

VMEM = pl.BlockSpec(memory_space=pltpu.VMEM)
SMEM = pl.BlockSpec(memory_space=pltpu.SMEM)
HBM = pl.BlockSpec(memory_space=pltpu.HBM)
PAD = 16
NT = (((1,), (1,)), ((), ()))
TN = (((0,), (0,)), ((), ()))


def call(kernel, outs, args, smem=(), hbm=(), scratch=(), out_specs=None, flops=0, name=None):
    count, out_count, own = len(args), len(jax.tree.leaves(outs)), len(scratch)
    specs = [SMEM if i in smem else HBM if i in hbm else VMEM for i in range(count)]
    nbytes = sum(a.size * a.dtype.itemsize for a in args)
    buffers = [pltpu.VMEM(args[i].shape, args[i].dtype) for i in hbm]
    sems = [pltpu.SemaphoreType.DMA((len(hbm),))] if hbm else []

    def body(*refs):
        ins, rest = list(refs[:count]), refs[count:]
        kept, moved = rest[: out_count + own], rest[out_count + own :]
        moves = {}
        for j, i in enumerate(hbm):
            moves[i] = pltpu.make_async_copy(ins[i], moved[j], moved[-1].at[j])
            moves[i].start()
            ins[i] = moved[j]

        def ready(*wanted):
            for i in wanted:
                moves[i].wait()

        kernel(ready, *ins, *kept)

    return pl.pallas_call(
        body,
        out_shape=outs,
        in_specs=specs,
        out_specs=jax.tree.map(lambda _: VMEM, outs) if out_specs is None else out_specs,
        scratch_shapes=list(scratch) + buffers + sems,
        compiler_params=pltpu.CompilerParams(vmem_limit_bytes=40 * 1024 * 1024),
        cost_estimate=pl.CostEstimate(flops=flops, bytes_accessed=nbytes, transcendentals=0),
        name=name,
    )(*args)


def shape(dims, dtype):
    return jax.ShapeDtypeStruct(dims, dtype)


def dot(a, b):
    return jnp.dot(a, b, preferred_element_type=f32)


def dot_nt(a, b):
    return lax.dot_general(a, b, NT, preferred_element_type=f32)


def dot_tn(a, b):
    return lax.dot_general(a, b, TN, preferred_element_type=f32)


def layer_norm(values, gain):
    mean = jnp.mean(values, axis=-1, keepdims=True)
    centred = values - mean
    var = jnp.mean(centred * centred, axis=-1, keepdims=True)
    return centred * lax.rsqrt(var + eps_norm) * gain


def send_kernel(ready, me_ref, at_ref, ids_ref, table_ref, w_ref, sent_ref, rows_ref, sems):
    cols = w_ref.shape[1]
    per_part = at_ref.shape[0]
    fetch, nodes = ids_ref.shape[1], table_ref.shape[0]
    ready(2, 3, 4)
    table = table_ref[...]
    kv = jnp.concatenate([dot_nt(table, w_ref[1]), dot_nt(table, w_ref[2])], axis=1).astype(bf)
    ids = ids_ref[...].astype(f32).T.astype(jnp.int32)
    lanes = lax.broadcasted_iota(jnp.int32, (fetch, nodes), 1)
    lead = lax.broadcasted_iota(jnp.int32, (fetch, 2 * cols), 1) == 0
    moves = []
    for part in range(ids.shape[1]):
        step = me_ref[0] ^ part
        picked = ids[:, part : part + 1]
        hot = jnp.where(lanes == picked, 1.0, 0.0).astype(bf)
        rows = dot(hot, kv)
        code = jnp.full((fetch, 1), -1, jnp.int32)
        for title in range(per_part):
            code = jnp.where(picked == at_ref[title], step * per_part + title, code)
        mark = jnp.where(lead, jnp.nan, code.astype(f32))
        at = pl.ds(part * fetch, fetch)
        rows_ref[at, :] = jnp.where(code >= 0, mark, rows).astype(bf)
        moves.append(pltpu.make_async_copy(rows_ref.at[at, :], sent_ref.at[at, :], sems.at[part]))
        moves[-1].start()
    for move in moves:
        move.wait()


def mask_kernel(ready, slots_ref, mask_ref):
    all_slots = slots_ref[...].astype(f32).T.astype(jnp.int32)
    for tile in range(all_slots.shape[0] // TILE):
        slots = all_slots[tile * TILE : (tile + 1) * TILE, :]
        lanes = lax.broadcasted_iota(jnp.int32, (TILE, TPR * TILE), 1)
        edges = lanes == lax.broadcasted_iota(jnp.int32, (TILE, TPR * TILE), 0)
        for edge in range(DEG):
            edges = edges | (lanes == slots[:, edge : edge + 1])
        mask_ref[tile * TILE : (tile + 1) * TILE, :] = jnp.where(edges, 1.0, 0.0).astype(bf)


def attn_kernel(ready, who_ref, titles_ref, w_in_ref, w_out_ref, *refs):
    outs, total = refs[:-1], refs[-1]
    titles = titles_ref[...]
    q = dot_nt(titles, w_in_ref[0]).astype(bf)
    k = dot_nt(titles, w_in_ref[1]).astype(bf)
    v = dot_nt(titles, w_in_ref[2]).astype(bf)
    cols = q.shape[1]
    heads = cols // HD
    lanes = lax.broadcasted_iota(jnp.int32, (SEQ, cols), 1) // HD
    for title in range(titles.shape[0] // SEQ):
        rows = slice(title * SEQ, (title + 1) * SEQ)
        qt, kt, vt = q[rows], k[rows], v[rows]
        stacked = jnp.concatenate(
            [jnp.where(lanes == h, qt, jnp.zeros_like(qt)) for h in range(heads)], axis=0
        )
        scores = dot_nt(stacked, kt) * (1.0 / HD**0.5)
        expo = jnp.exp(scores - jnp.max(scores, axis=-1, keepdims=True))
        probs = (expo / jnp.sum(expo, axis=-1, keepdims=True)).astype(bf)
        mixed = dot(probs, vt)
        context = mixed[:SEQ]
        for h in range(1, heads):
            context = jnp.where(lanes == h, mixed[h * SEQ : (h + 1) * SEQ], context)
        total[rows, :] = dot(context.astype(bf), w_out_ref[...])
    chunk = outs[0].shape[0] - PAD
    firsts = first_rows(total)
    for step, out in enumerate(outs):
        at = pl.ds(pl.multiple_of(who_ref[step] * chunk, chunk), chunk)
        out[:chunk, :] = total[at, :].astype(out.dtype)
        out[chunk:, :] = firsts.astype(out.dtype)


def first_rows(ref):
    sub = lax.broadcasted_iota(jnp.int32, (PAD, ref.shape[1]), 0)
    rows = jnp.zeros((PAD, ref.shape[1]), f32)
    for title in range(ref.shape[0] // SEQ):
        row = ref[title * SEQ : title * SEQ + 1, :].astype(f32)
        rows = jnp.where(sub == title, row, rows)
    return rows


def norm_one_kernel(
    ready, who_ref, titles_ref, gains_ref, w_in_ref, w_out_ref, own_ref, *refs
):
    *parts, out, first_hidden, first_terms = refs
    chunk = own_ref.shape[0] - PAD
    total = own_ref[...]
    for part in parts:
        total = total + part[...].astype(f32)
    at = pl.ds(pl.multiple_of(who_ref[0] * chunk, chunk), chunk)
    base = jnp.concatenate([titles_ref[at, :].astype(f32), first_rows(titles_ref)], axis=0)
    hidden = layer_norm(base + total, gains_ref[0:1, :]).astype(bf)
    out[:chunk, :] = hidden[:chunk]
    firsts = hidden[chunk:]
    first_hidden[...] = firsts
    terms = dot(gelu(dot(firsts, w_in_ref[...])).astype(bf), w_out_ref[...])
    first_terms[...] = terms
    out[chunk:, :] = terms.astype(bf)


def gelu(x):
    return 0.5 * x * (1.0 + lax.erf(x * (0.5**0.5)))


def ffn_kernel(ready, w_in_ref, w_out_ref, gains_ref, first_hidden, first_terms, *refs):
    *refs, first = refs
    count = len(refs) // 2
    ins, outs = refs[:count], refs[count:]
    chunk = outs[0].shape[0]
    hidden = jnp.concatenate([ref[:chunk, :] for ref in ins], axis=0)
    inner = gelu(dot(hidden, w_in_ref[...])).astype(bf)
    total = dot(inner, w_out_ref[...])
    for step, out in enumerate(outs):
        out[...] = total[step * chunk : (step + 1) * chunk].astype(out.dtype)
    terms = first_terms[...]
    for ref in ins[1:]:
        terms = terms + ref[chunk:, :].astype(f32)
    done = layer_norm(first_hidden[...].astype(f32) + terms, gains_ref[1:2, :])
    first[...] = done[: first.shape[0]].astype(bf)


def norm_two_kernel(ready, hidden_ref, gains_ref, own_ref, *refs):
    *refs, out = refs
    parts = [ref for ref in refs if ref.shape == own_ref.shape]
    firsts = [ref for ref in refs if ref.shape != own_ref.shape]
    chunk = own_ref.shape[0]
    total = own_ref[...]
    for part in parts:
        total = total + part[...].astype(f32)
    hidden = hidden_ref[:chunk, :].astype(f32)
    out[:chunk, :] = layer_norm(hidden + total, gains_ref[1:2, :]).astype(bf)
    tail = out.shape[0] - chunk
    sub = lax.broadcasted_iota(jnp.int32, (tail, out.shape[1]), 0)
    rows = jnp.zeros((tail, out.shape[1]), f32)
    for turn, ref in enumerate(firsts):
        per_part = ref.shape[0]
        for title in range(per_part):
            row = ref[title : title + 1, :].astype(f32)
            rows = jnp.where(sub == turn * per_part + title, row, rows)
    out[chunk:, :] = rows.astype(bf)


def place_kernel(ready, who_ref, *refs):
    *chunks, out = refs
    chunk = out.shape[0] // len(chunks)
    for step, ref in enumerate(chunks):
        out[pl.ds(pl.multiple_of(who_ref[step] * chunk, chunk), chunk), :] = ref[:chunk, :]


def own_kernel(ready, who_ref, at_ref, table_ref, w_ref, first_ref, *refs):
    *chunks, kv_ref, q_ref, first_kv_ref, features, firsts = refs
    members = len(chunks)
    per_part, width = first_ref.shape
    cols = w_ref.shape[1]
    turns = firsts.shape[0] // per_part // members
    for step, ref in enumerate(chunks):
        base = ref.shape[0] - tail_rows(turns * per_part)
        rows = ref[base:, :].astype(f32)
        for turn in range(turns):
            for title in range(per_part):
                place = (turn * members + who_ref[step]) * per_part + title
                firsts[pl.ds(place, 1), :] = rows[turn * per_part + title][None]
    firsts[0:per_part, :] = first_ref[...].astype(f32)
    ready(2, 3)
    nodes = table_ref.shape[0]
    for tile in range(nodes // TILE):
        span = slice(tile * TILE, (tile + 1) * TILE)
        rows = table_ref[span, :].astype(f32)
        sub = lax.broadcasted_iota(jnp.int32, (TILE, width), 0) + tile * TILE
        for title in range(per_part):
            rows = jnp.where(sub == at_ref[title], firsts[title : title + 1, :], rows)
        features[span, :] = rows.astype(bf)
    first = firsts[...].astype(bf)
    table = features[...]
    for j in (1, 2):
        span = slice((j - 1) * cols, j * cols)
        first_kv_ref[:, span] = dot_nt(first, w_ref[j]).astype(bf)
        kv_ref[:, span] = dot_nt(table, w_ref[j]).astype(bf)
    q_ref[...] = dot_nt(table, w_ref[0]).astype(bf)


def tail_rows(count):
    return -(-count // PAD) * PAD


def graph_kernel(
    ready, cols_ref, q_ref, kv_ref, first_ref, mask_ref, far_ref, out_ref, k_all, v_all
):
    nodes, cols = q_ref.shape
    row_tiles = nodes // TILE
    first_kv = first_ref[...]
    k_all[:nodes, :] = kv_ref[:, :cols]
    v_all[:nodes, :] = kv_ref[:, cols:]
    lanes = lax.broadcasted_iota(jnp.int32, (TILE, first_kv.shape[0]), 1).astype(f32)
    for tile in range(far_ref.shape[0] // TILE):
        rows = far_ref[tile * TILE : (tile + 1) * TILE, :].astype(f32)
        code = jnp.where(rows[:, 0:1] != rows[:, 0:1], rows[:, 1:2], -1.0)
        hot = jnp.where(lanes == code, 1.0, 0.0).astype(bf)
        fixed = jnp.where(code >= 0.0, dot(hot, first_kv), rows).astype(bf)
        span = slice(nodes + tile * TILE, nodes + (tile + 1) * TILE)
        k_all[span, :] = fixed[:, :cols]
        v_all[span, :] = fixed[:, cols:]

    heads = cols // GHD
    head_of = lax.broadcasted_iota(jnp.int32, (TILE, cols), 1) // GHD
    for tile in range(row_tiles):
        q = q_ref[tile * TILE : (tile + 1) * TILE, :]
        stacked = jnp.concatenate(
            [jnp.where(head_of == h, q, jnp.zeros_like(q)) for h in range(heads)], axis=0
        )
        starts = [pl.multiple_of(cols_ref[tile, c] * TILE, TILE) for c in range(TPR)]
        keys = jnp.concatenate([k_all[pl.ds(start, TILE), :] for start in starts], axis=0)
        values = jnp.concatenate([v_all[pl.ds(start, TILE), :] for start in starts], axis=0)
        scores = dot_nt(stacked, keys) * (1.0 / GHD**0.5)
        mask = mask_ref[tile * TILE : (tile + 1) * TILE, :].astype(f32)
        mask = jnp.concatenate([mask] * heads, axis=0) > 0.5
        masked = jnp.where(mask, scores, -jnp.inf)
        expo = jnp.exp(masked - jnp.max(masked, axis=-1, keepdims=True))
        scale = 1.0 / jnp.sum(expo, axis=-1, keepdims=True)
        mixed = dot(expo.astype(bf), values) * scale
        out = mixed[:TILE]
        for h in range(1, heads):
            out = jnp.where(head_of == h, mixed[h * TILE : (h + 1) * TILE], out)
        out_ref[:, tile * TILE : (tile + 1) * TILE] = out.T.astype(bf)


def local(

    titles,
    w_attn_in,
    w_attn_out,
    w_ffn_in,
    w_ffn_out,
    gains,
    node_table,
    w_graph,
    title_nodes,
    send_ids,
    tile_cols,
    nbr_slots,
):
    tok_rows, width = titles.shape
    nodes = node_table.shape[0]
    cols = w_graph.shape[2]
    mp = lax.axis_size("mp")
    dp = lax.axis_size("dp")
    me_mp = lax.axis_index("mp").astype(jnp.int32)
    me_dp = lax.axis_index("dp").astype(jnp.int32).reshape(1)
    who = me_mp ^ jnp.arange(mp, dtype=jnp.int32)
    chunk = tok_rows // mp
    per_part = title_nodes.shape[0]
    fetch = send_ids.shape[2]

    def swap(value, step, axis="mp"):
        return lax.ppermute(value, axis, [(i, i ^ step) for i in range(lax.axis_size(axis))])

    w_attn_in = jnp.swapaxes(w_attn_in, 1, 2)
    w_graph = jnp.swapaxes(w_graph, 1, 2)
    sent = call(
        send_kernel,
        shape((dp * fetch, 2 * cols), bf),
        (me_dp, title_nodes, send_ids[0], node_table, w_graph),
        smem=(0, 1),
        hbm=(2, 3, 4),
        out_specs=HBM,
        scratch=[pltpu.VMEM((dp * fetch, 2 * cols), bf), pltpu.SemaphoreType.DMA((dp,))],
        flops=2 * nodes * width * 2 * cols + 2 * dp * fetch * nodes * 2 * cols,
        name="send",
    )
    far = lax.all_to_all(
        sent.reshape(dp, fetch, 2 * cols), "dp", split_axis=0, concat_axis=0, tiled=True
    ).reshape(dp * fetch, 2 * cols)
    titles, _ = lax.optimization_barrier((titles, sent))

    terms = call(
        attn_kernel,
        tuple(shape((chunk + PAD, width), bf if step else f32) for step in range(mp)),
        (who, titles, w_attn_in, w_attn_out),
        smem=(0,),
        scratch=[pltpu.VMEM((tok_rows, width), f32)],
        flops=2 * tok_rows * width * 4 * w_attn_in.shape[1],
        name="attn",
    )
    parts = [swap(terms[step], step) for step in range(1, mp)]
    hidden, first_hidden, first_terms = call(
        norm_one_kernel,
        (shape((chunk + PAD, width), bf), shape((PAD, width), bf), shape((PAD, width), f32)),
        (who, titles, gains, w_ffn_in, w_ffn_out, terms[0], *parts),
        smem=(0,),
        name="norm_one",
    )
    hiddens = [hidden] + [swap(hidden, step) for step in range(1, mp)]
    *terms, first = call(
        ffn_kernel,
        tuple(shape((chunk, width), bf if step else f32) for step in range(mp))
        + (shape((per_part, width), bf),),
        (w_ffn_in, w_ffn_out, gains, first_hidden, first_terms, *hiddens),
        flops=4 * tok_rows * width * w_ffn_in.shape[1],
        name="ffn",
    )
    parts = [swap(terms[step], step) for step in range(1, mp)]
    turns = dp // mp
    firsts = [
        lax.ppermute(
            first,
            ("dp", "mp"),
            [
                (p * mp + m, (p ^ (turn * mp + m)) * mp + m)
                for p in range(dp)
                for m in range(mp)
                if turn or m
            ],
        )
        for turn in range(turns)
    ]
    done = call(
        norm_two_kernel,
        shape((chunk + tail_rows(turns * per_part), width), bf),
        (hidden, gains, terms[0], *parts, *firsts),
        name="norm_two",
    )
    dones = [done] + [swap(done, step) for step in range(1, mp)]

    mask = call(
        mask_kernel, shape((nodes, TPR * TILE), bf), (nbr_slots.T,), flops=10**9, name="mask"
    )
    kv, q, first_kv = call(
        own_kernel,
        (shape((nodes, 2 * cols), bf), shape((nodes, cols), bf), shape((dp * per_part, 2 * cols), bf)),
        (who, title_nodes, node_table, w_graph, first, *dones),
        smem=(0, 1),
        hbm=(2, 3),
        scratch=[pltpu.VMEM((nodes, width), bf), pltpu.VMEM((dp * per_part, width), f32)],
        flops=2 * nodes * width * 3 * cols,
        name="own",
    )
    keys = nodes + dp * fetch
    graph_out = call(
        graph_kernel,
        shape((cols, nodes), bf),
        (tile_cols, q, kv, first_kv, mask, far),
        smem=(0,),
        scratch=[pltpu.VMEM((keys, cols), bf), pltpu.VMEM((keys, cols), bf)],
        flops=10**9,
        name="graph",
    )
    encoded = call(
        place_kernel, shape((tok_rows, width), bf), (who, *dones), smem=(0,), name="place"
    )
    return (encoded, graph_out.T)


def solution(mesh):
    in_specs = (
        P("dp", None),
        P(None, None, "mp"),
        P("mp", None),
        P(None, "mp"),
        P("mp", None),
        P(),
        P("dp", None),
        P(None, None, "mp"),
        P("dp"),
        P("dp", None, None),
        P("dp", None),
        P("dp", None),
    )
    out_specs = (P("dp", None), P("dp", "mp"))
    return jax.shard_map(
        local, mesh=mesh, in_specs=in_specs, out_specs=out_specs, check_vma=False
    )
```

```python
import jax
import jax.numpy as jnp
from jax import lax
from jax.experimental import pallas as pl
from jax.experimental.pallas import tpu as pltpu
from jax.sharding import PartitionSpec as P

SEQ = 128
TILE = 128
DEG = 16
TPR = 6
HD = 64
GHD = 96

eps_norm = 1e-06
bf = jnp.bfloat16
f32 = jnp.float32

VMEM = pl.BlockSpec(memory_space=pltpu.VMEM)
SMEM = pl.BlockSpec(memory_space=pltpu.SMEM)
HBM = pl.BlockSpec(memory_space=pltpu.HBM)
PAD = 16
NT = (((1,), (1,)), ((), ()))
TN = (((0,), (0,)), ((), ()))


def call(
    kernel, outs, args, smem=(), hbm=(), scalars=(), scratch=(), out_specs=None, flops=0, name=None
):
    count, out_count, own = len(args), len(jax.tree.leaves(outs)), len(scratch)
    specs = [SMEM if i in smem else HBM if i in hbm else VMEM for i in range(count)]
    nbytes = sum(a.size * a.dtype.itemsize for a in args)
    space = [pltpu.SMEM if i in scalars else pltpu.VMEM for i in hbm]
    buffers = [kind(args[i].shape, args[i].dtype) for kind, i in zip(space, hbm)]
    sems = [pltpu.SemaphoreType.DMA((len(hbm),))] if hbm else []

    def body(*refs):
        ins, rest = list(refs[:count]), refs[count:]
        kept, moved = rest[: out_count + own], rest[out_count + own :]
        moves = {}
        for j, i in enumerate(hbm):
            moves[i] = pltpu.make_async_copy(ins[i], moved[j], moved[-1].at[j])
            moves[i].start()
            ins[i] = moved[j]

        def ready(*wanted):
            for i in wanted:
                moves[i].wait()

        kernel(ready, *ins, *kept)

    return pl.pallas_call(
        body,
        out_shape=outs,
        in_specs=specs,
        out_specs=jax.tree.map(lambda _: VMEM, outs) if out_specs is None else out_specs,
        scratch_shapes=list(scratch) + buffers + sems,
        compiler_params=pltpu.CompilerParams(vmem_limit_bytes=(60 if hbm else 40) * 1024 * 1024),
        cost_estimate=pl.CostEstimate(flops=flops, bytes_accessed=nbytes, transcendentals=0),
        name=name,
    )(*args)


def shape(dims, dtype):
    return jax.ShapeDtypeStruct(dims, dtype)


def dot(a, b):
    return jnp.dot(a, b, preferred_element_type=f32)


def dot_nt(a, b):
    return lax.dot_general(a, b, NT, preferred_element_type=f32)


def dot_tn(a, b):
    return lax.dot_general(a, b, TN, preferred_element_type=f32)


def layer_norm(values, gain):
    mean = jnp.mean(values, axis=-1, keepdims=True)
    centred = values - mean
    var = jnp.mean(centred * centred, axis=-1, keepdims=True)
    return centred * lax.rsqrt(var + eps_norm) * gain


def send_kernel(ready, me_ref, at_ref, ids_ref, table_ref, w_ref, sent_ref, rows_ref, sems):
    cols = w_ref.shape[1]
    per_part = at_ref.shape[0]
    fetch, nodes = ids_ref.shape[1], table_ref.shape[0]
    ready(1, 2, 3, 4)
    table = table_ref[...]
    kv = jnp.concatenate([dot_nt(table, w_ref[1]), dot_nt(table, w_ref[2])], axis=1).astype(bf)
    ids = ids_ref[...].astype(f32).T.astype(jnp.int32)
    lanes = lax.broadcasted_iota(jnp.int32, (fetch, nodes), 1)
    lead = lax.broadcasted_iota(jnp.int32, (fetch, 2 * cols), 1) == 0
    moves = []
    for part in range(ids.shape[1]):
        step = me_ref[0] ^ part
        picked = ids[:, part : part + 1]
        hot = jnp.where(lanes == picked, 1.0, 0.0).astype(bf)
        rows = dot(hot, kv)
        code = jnp.full((fetch, 1), -1, jnp.int32)
        for title in range(per_part):
            code = jnp.where(picked == at_ref[title], step * per_part + title, code)
        mark = jnp.where(lead, jnp.nan, code.astype(f32))
        at = pl.ds(part * fetch, fetch)
        rows_ref[at, :] = jnp.where(code >= 0, mark, rows).astype(bf)
        moves.append(pltpu.make_async_copy(rows_ref.at[at, :], sent_ref.at[at, :], sems.at[part]))
        moves[-1].start()
    for move in moves:
        move.wait()


def mask_kernel(ready, slots_ref, mask_ref):
    all_slots = slots_ref[...].astype(f32).T.astype(jnp.int32)
    for tile in range(all_slots.shape[0] // TILE):
        slots = all_slots[tile * TILE : (tile + 1) * TILE, :]
        lanes = lax.broadcasted_iota(jnp.int32, (TILE, TPR * TILE), 1)
        edges = lanes == lax.broadcasted_iota(jnp.int32, (TILE, TPR * TILE), 0)
        for edge in range(DEG):
            edges = edges | (lanes == slots[:, edge : edge + 1])
        mask_ref[tile * TILE : (tile + 1) * TILE, :] = jnp.where(edges, 1.0, 0.0).astype(bf)


def attn_kernel(ready, who_ref, titles_ref, w_in_ref, w_out_ref, *refs):
    outs, total = refs[:-1], refs[-1]
    titles = titles_ref[...]
    q = dot_nt(titles, w_in_ref[0]).astype(bf)
    k = dot_nt(titles, w_in_ref[1]).astype(bf)
    v = dot_nt(titles, w_in_ref[2]).astype(bf)
    cols = q.shape[1]
    heads = cols // HD
    lanes = lax.broadcasted_iota(jnp.int32, (SEQ, cols), 1) // HD
    for title in range(titles.shape[0] // SEQ):
        rows = slice(title * SEQ, (title + 1) * SEQ)
        qt, kt, vt = q[rows], k[rows], v[rows]
        stacked = jnp.concatenate(
            [jnp.where(lanes == h, qt, jnp.zeros_like(qt)) for h in range(heads)], axis=0
        )
        scores = dot_nt(stacked, kt) * (1.0 / HD**0.5)
        expo = jnp.exp(scores - jnp.max(scores, axis=-1, keepdims=True))
        probs = (expo / jnp.sum(expo, axis=-1, keepdims=True)).astype(bf)
        mixed = dot(probs, vt)
        context = mixed[:SEQ]
        for h in range(1, heads):
            context = jnp.where(lanes == h, mixed[h * SEQ : (h + 1) * SEQ], context)
        total[rows, :] = dot(context.astype(bf), w_out_ref[...])
    chunk = outs[0].shape[0] - PAD
    firsts = first_rows(total)
    for step, out in enumerate(outs):
        at = pl.ds(pl.multiple_of(who_ref[step] * chunk, chunk), chunk)
        out[:chunk, :] = total[at, :].astype(out.dtype)
        out[chunk:, :] = firsts.astype(out.dtype)


def first_rows(ref):
    sub = lax.broadcasted_iota(jnp.int32, (PAD, ref.shape[1]), 0)
    rows = jnp.zeros((PAD, ref.shape[1]), f32)
    for title in range(ref.shape[0] // SEQ):
        row = ref[title * SEQ : title * SEQ + 1, :].astype(f32)
        rows = jnp.where(sub == title, row, rows)
    return rows


def norm_one_kernel(
    ready, who_ref, titles_ref, gains_ref, w_in_ref, w_out_ref, own_ref, *refs
):
    *parts, out, first_hidden, first_terms = refs
    chunk = own_ref.shape[0] - PAD
    total = own_ref[...]
    for part in parts:
        total = total + part[...].astype(f32)
    at = pl.ds(pl.multiple_of(who_ref[0] * chunk, chunk), chunk)
    base = jnp.concatenate([titles_ref[at, :].astype(f32), first_rows(titles_ref)], axis=0)
    hidden = layer_norm(base + total, gains_ref[0:1, :]).astype(bf)
    out[:chunk, :] = hidden[:chunk]
    firsts = hidden[chunk:]
    first_hidden[...] = firsts
    terms = dot(gelu(dot(firsts, w_in_ref[...])).astype(bf), w_out_ref[...])
    first_terms[...] = terms
    out[chunk:, :] = terms.astype(bf)


def gelu(x):
    return 0.5 * x * (1.0 + lax.erf(x * (0.5**0.5)))


def ffn_kernel(ready, w_in_ref, w_out_ref, gains_ref, first_hidden, first_terms, *refs):
    *refs, first = refs
    count = len(refs) // 2
    ins, outs = refs[:count], refs[count:]
    chunk = outs[0].shape[0]
    hidden = jnp.concatenate([ref[:chunk, :] for ref in ins], axis=0)
    inner = gelu(dot(hidden, w_in_ref[...])).astype(bf)
    total = dot(inner, w_out_ref[...])
    for step, out in enumerate(outs):
        out[...] = total[step * chunk : (step + 1) * chunk].astype(out.dtype)
    terms = first_terms[...]
    for ref in ins[1:]:
        terms = terms + ref[chunk:, :].astype(f32)
    done = layer_norm(first_hidden[...].astype(f32) + terms, gains_ref[1:2, :])
    first[...] = done[: first.shape[0]].astype(bf)


def norm_two_kernel(ready, hidden_ref, gains_ref, own_ref, *refs):
    *parts, out = refs
    total = own_ref[...]
    for part in parts:
        total = total + part[...].astype(f32)
    hidden = hidden_ref[: out.shape[0], :].astype(f32)
    out[...] = layer_norm(hidden + total, gains_ref[1:2, :]).astype(bf)


def pack_kernel(ready, *refs):
    *parts, out = refs
    per_part = parts[0].shape[0]
    sub = lax.broadcasted_iota(jnp.int32, out.shape, 0)
    rows = jnp.zeros(out.shape, f32)
    for turn, ref in enumerate(parts):
        for title in range(per_part):
            row = ref[title : title + 1, :].astype(f32)
            rows = jnp.where(sub == turn * per_part + title, row, rows)
    out[...] = rows.astype(bf)


def place_kernel(ready, who_ref, *refs):
    *chunks, out = refs
    chunk = out.shape[0] // len(chunks)
    for step, ref in enumerate(chunks):
        out[pl.ds(pl.multiple_of(who_ref[step] * chunk, chunk), chunk), :] = ref[...]


def own_kernel(ready, table_ref, w_ref, kv_ref, q_ref):
    cols = w_ref.shape[1]
    table = table_ref[...]
    kv_ref[:, :cols] = dot_nt(table, w_ref[1]).astype(bf)
    kv_ref[:, cols:] = dot_nt(table, w_ref[2]).astype(bf)
    q_ref[...] = dot_nt(table, w_ref[0]).astype(bf)


def tail_rows(count):
    return -(-count // PAD) * PAD


def graph_kernel(
    ready, who_ref, cols_ref, at_ref, q_ref, kv_ref, w_ref, mask_ref, far_ref, first_ref, *refs
):
    *packs, out_ref, k_all, v_all, firsts = refs
    nodes, cols = q_ref.shape
    row_tiles = nodes // TILE
    per_part = first_ref.shape[0]
    members = len(packs)
    for step, ref in enumerate(packs):
        rows = ref[...].astype(f32)
        for turn in range(firsts.shape[0] // per_part // members):
            for title in range(per_part):
                place = (turn * members + who_ref[step]) * per_part + title
                at = turn * per_part + title
                firsts[pl.ds(place, 1), :] = rows[at : at + 1]
    firsts[0:per_part, :] = first_ref[...].astype(f32)
    first = firsts[...].astype(bf)
    ready(5)
    first_kv = jnp.concatenate([dot_nt(first, w_ref[1]), dot_nt(first, w_ref[2])], axis=1).astype(bf)
    first_q = dot_nt(first, w_ref[0])
    ready(2, 4)
    for tile in range(row_tiles):
        span = slice(tile * TILE, (tile + 1) * TILE)
        rows = kv_ref[span, :].astype(f32)
        sub = lax.broadcasted_iota(jnp.int32, (TILE, 2 * cols), 0) + tile * TILE
        for title in range(per_part):
            row = first_kv[title : title + 1].astype(f32)
            rows = jnp.where(sub == at_ref[title], row, rows)
        rows = rows.astype(bf)
        k_all[span, :] = rows[:, :cols]
        v_all[span, :] = rows[:, cols:]
    ready(7)
    lanes = lax.broadcasted_iota(jnp.int32, (TILE, first_kv.shape[0]), 1).astype(f32)
    for tile in range(far_ref.shape[0] // TILE):
        rows = far_ref[tile * TILE : (tile + 1) * TILE, :].astype(f32)
        code = jnp.where(rows[:, 0:1] != rows[:, 0:1], rows[:, 1:2], -1.0)
        hot = jnp.where(lanes == code, 1.0, 0.0).astype(bf)
        fixed = jnp.where(code >= 0.0, dot(hot, first_kv), rows).astype(bf)
        span = slice(nodes + tile * TILE, nodes + (tile + 1) * TILE)
        k_all[span, :] = fixed[:, :cols]
        v_all[span, :] = fixed[:, cols:]

    ready(1, 3, 6)
    heads = cols // GHD
    head_of = lax.broadcasted_iota(jnp.int32, (TILE, cols), 1) // GHD
    for tile in range(row_tiles):
        q = q_ref[tile * TILE : (tile + 1) * TILE, :].astype(f32)
        sub = lax.broadcasted_iota(jnp.int32, (TILE, cols), 0) + tile * TILE
        for title in range(per_part):
            q = jnp.where(sub == at_ref[title], first_q[title : title + 1], q)
        q = q.astype(bf)
        stacked = jnp.concatenate(
            [jnp.where(head_of == h, q, jnp.zeros_like(q)) for h in range(heads)], axis=0
        )
        starts = [pl.multiple_of(cols_ref[tile, c] * TILE, TILE) for c in range(TPR)]
        keys = jnp.concatenate([k_all[pl.ds(start, TILE), :] for start in starts], axis=0)
        values = jnp.concatenate([v_all[pl.ds(start, TILE), :] for start in starts], axis=0)
        scores = dot_nt(stacked, keys) * (1.0 / GHD**0.5)
        mask = mask_ref[tile * TILE : (tile + 1) * TILE, :].astype(f32)
        mask = jnp.concatenate([mask] * heads, axis=0) > 0.5
        masked = jnp.where(mask, scores, -jnp.inf)
        expo = jnp.exp(masked - jnp.max(masked, axis=-1, keepdims=True))
        scale = 1.0 / jnp.sum(expo, axis=-1, keepdims=True)
        mixed = dot(expo.astype(bf), values) * scale
        out = mixed[:TILE]
        for h in range(1, heads):
            out = jnp.where(head_of == h, mixed[h * TILE : (h + 1) * TILE], out)
        out_ref[:, tile * TILE : (tile + 1) * TILE] = out.T.astype(bf)


def local(

    titles,
    w_attn_in,
    w_attn_out,
    w_ffn_in,
    w_ffn_out,
    gains,
    node_table,
    w_graph,
    title_nodes,
    send_ids,
    tile_cols,
    nbr_slots,
):
    tok_rows, width = titles.shape
    nodes = node_table.shape[0]
    cols = w_graph.shape[2]
    mp = lax.axis_size("mp")
    dp = lax.axis_size("dp")
    me_mp = lax.axis_index("mp").astype(jnp.int32)
    me_dp = lax.axis_index("dp").astype(jnp.int32).reshape(1)
    who = me_mp ^ jnp.arange(mp, dtype=jnp.int32)
    chunk = tok_rows // mp
    per_part = title_nodes.shape[0]
    fetch = send_ids.shape[2]

    def swap(value, step, axis="mp"):
        return lax.ppermute(value, axis, [(i, i ^ step) for i in range(lax.axis_size(axis))])

    w_attn_in = jnp.swapaxes(w_attn_in, 1, 2)
    w_graph = jnp.swapaxes(w_graph, 1, 2)
    sent = call(
        send_kernel,
        shape((dp * fetch, 2 * cols), bf),
        (me_dp, title_nodes, send_ids[0], node_table, w_graph),
        smem=(0,),
        hbm=(4, 3, 2, 1),
        scalars=(1,),
        out_specs=HBM,
        scratch=[pltpu.VMEM((dp * fetch, 2 * cols), bf), pltpu.SemaphoreType.DMA((dp,))],
        flops=2 * nodes * width * 2 * cols + 2 * dp * fetch * nodes * 2 * cols,
        name="send",
    )
    far = lax.all_to_all(
        sent.reshape(dp, fetch, 2 * cols), "dp", split_axis=0, concat_axis=0, tiled=True
    ).reshape(dp * fetch, 2 * cols)
    titles, _ = lax.optimization_barrier((titles, sent))

    terms = call(
        attn_kernel,
        tuple(shape((chunk + PAD, width), bf if step else f32) for step in range(mp)),
        (who, titles, w_attn_in, w_attn_out),
        smem=(0,),
        scratch=[pltpu.VMEM((tok_rows, width), f32)],
        flops=2 * tok_rows * width * 4 * w_attn_in.shape[1],
        name="attn",
    )
    parts = [swap(terms[step], step) for step in range(1, mp)]
    hidden, first_hidden, first_terms = call(
        norm_one_kernel,
        (shape((chunk + PAD, width), bf), shape((PAD, width), bf), shape((PAD, width), f32)),
        (who, titles, gains, w_ffn_in, w_ffn_out, terms[0], *parts),
        smem=(0,),
        name="norm_one",
    )
    hiddens = [hidden] + [swap(hidden, step) for step in range(1, mp)]
    *terms, first = call(
        ffn_kernel,
        tuple(shape((chunk, width), bf if step else f32) for step in range(mp))
        + (shape((per_part, width), bf),),
        (w_ffn_in, w_ffn_out, gains, first_hidden, first_terms, *hiddens),
        flops=4 * tok_rows * width * w_ffn_in.shape[1],
        name="ffn",
    )
    parts = [swap(terms[step], step) for step in range(1, mp)]
    turns = dp // mp
    firsts = [
        lax.ppermute(
            first,
            ("dp", "mp"),
            [
                (p * mp + m, (p ^ (turn * mp + m)) * mp + m)
                for p in range(dp)
                for m in range(mp)
                if turn or m
            ],
        )
        for turn in range(turns)
    ]
    mask = call(
        mask_kernel, shape((nodes, TPR * TILE), bf), (nbr_slots.T,), flops=4 * 10**9, name="mask"
    )
    kv, q = call(
        own_kernel,
        (shape((nodes, 2 * cols), bf), shape((nodes, cols), bf)),
        (node_table, w_graph),
        flops=2 * 10**9,
        name="own",
    )
    hidden, kv, q = lax.optimization_barrier((hidden, kv, q))
    done = call(
        norm_two_kernel,
        shape((chunk, width), bf),
        (hidden, gains, terms[0], *parts),
        name="norm_two",
    )
    dones = [done] + [swap(done, step) for step in range(1, mp)]
    dones, firsts, mask = lax.optimization_barrier((dones, firsts, mask))
    pack = call(pack_kernel, shape((tail_rows(turns * per_part), width), bf), firsts, name="pack")
    packs = [pack] + [swap(pack, step) for step in range(1, mp)]

    keys = nodes + dp * fetch
    graph_out = call(
        graph_kernel,
        shape((cols, nodes), bf),
        (who, tile_cols, title_nodes, q, kv, w_graph, mask, far, first, *packs),
        smem=(0,),
        hbm=(5, 2, 4, 7, 1, 3, 6),
        scalars=(1, 2),
        scratch=[
            pltpu.VMEM((keys, cols), bf),
            pltpu.VMEM((keys, cols), bf),
            pltpu.VMEM((dp * per_part, width), f32),
        ],
        flops=10**9,
        name="graph",
    )
    encoded = call(
        place_kernel, shape((tok_rows, width), bf), (who, *dones), smem=(0,), name="place"
    )
    return (encoded, graph_out.T)


def solution(mesh):
    in_specs = (
        P("dp", None),
        P(None, None, "mp"),
        P("mp", None),
        P(None, "mp"),
        P("mp", None),
        P(),
        P("dp", None),
        P(None, None, "mp"),
        P("dp"),
        P("dp", None, None),
        P("dp", None),
        P("dp", None),
    )
    out_specs = (P("dp", None), P("dp", "mp"))
    return jax.shard_map(
        local, mesh=mesh, in_specs=in_specs, out_specs=out_specs, check_vma=False
    )
```

```python
import functools
import jax
import jax.numpy as jnp
from jax import lax
from jax.experimental import pallas as pl
from jax.experimental.pallas import tpu as pltpu
from jax.sharding import PartitionSpec as P

SEQ = 128
TILE = 128
DEG = 16
TPR = 6
HD = 64
GHD = 96

eps_norm = 1e-06
bf = jnp.bfloat16
f32 = jnp.float32

VMEM = pl.BlockSpec(memory_space=pltpu.VMEM)
SMEM = pl.BlockSpec(memory_space=pltpu.SMEM)
HBM = pl.BlockSpec(memory_space=pltpu.HBM)
PAD = 16
NT = (((1,), (1,)), ((), ()))
TN = (((0,), (0,)), ((), ()))


def call(
    kernel, outs, args, smem=(), hbm=(), scalars=(), scratch=(), out_specs=None, flops=0, name=None
):
    count, out_count, own = len(args), len(jax.tree.leaves(outs)), len(scratch)
    specs = [SMEM if i in smem else HBM if i in hbm else VMEM for i in range(count)]
    nbytes = sum(a.size * a.dtype.itemsize for a in args)
    space = [pltpu.SMEM if i in scalars else pltpu.VMEM for i in hbm]
    buffers = [kind(args[i].shape, args[i].dtype) for kind, i in zip(space, hbm)]
    sems = [pltpu.SemaphoreType.DMA((len(hbm),))] if hbm else []

    def body(*refs):
        ins, rest = list(refs[:count]), refs[count:]
        kept, moved = rest[: out_count + own], rest[out_count + own :]
        moves = {}
        for j, i in enumerate(hbm):
            moves[i] = pltpu.make_async_copy(ins[i], moved[j], moved[-1].at[j])
            moves[i].start()
            ins[i] = moved[j]

        def ready(*wanted):
            for i in wanted:
                moves[i].wait()

        kernel(ready, *ins, *kept)

    return pl.pallas_call(
        body,
        out_shape=outs,
        in_specs=specs,
        out_specs=jax.tree.map(lambda _: VMEM, outs) if out_specs is None else out_specs,
        scratch_shapes=list(scratch) + buffers + sems,
        compiler_params=pltpu.CompilerParams(vmem_limit_bytes=(60 if hbm else 40) * 1024 * 1024),
        cost_estimate=pl.CostEstimate(flops=flops, bytes_accessed=nbytes, transcendentals=0),
        name=name,
    )(*args)


def shape(dims, dtype):
    return jax.ShapeDtypeStruct(dims, dtype)


def dot(a, b):
    return jnp.dot(a, b, preferred_element_type=f32)


def dot_nt(a, b):
    return lax.dot_general(a, b, NT, preferred_element_type=f32)


def dot_tn(a, b):
    return lax.dot_general(a, b, TN, preferred_element_type=f32)


def layer_norm(values, gain):
    mean = jnp.mean(values, axis=-1, keepdims=True)
    centred = values - mean
    var = jnp.mean(centred * centred, axis=-1, keepdims=True)
    return centred * lax.rsqrt(var + eps_norm) * gain


def send_kernel(ready, me_ref, at_ref, ids_ref, table_ref, w_ref, sent_ref, rows_ref, sems):
    cols = w_ref.shape[1]
    per_part = at_ref.shape[0]
    fetch, nodes = ids_ref.shape[1], table_ref.shape[0]
    ready(1, 2, 3, 4)
    table = table_ref[...]
    kv = jnp.concatenate([dot_nt(table, w_ref[1]), dot_nt(table, w_ref[2])], axis=1).astype(bf)
    ids = ids_ref[...].astype(f32).T.astype(jnp.int32)
    lanes = lax.broadcasted_iota(jnp.int32, (fetch, nodes), 1)
    lead = lax.broadcasted_iota(jnp.int32, (fetch, 2 * cols), 1) == 0
    moves = []
    for part in range(ids.shape[1]):
        step = me_ref[0] ^ part
        picked = ids[:, part : part + 1]
        hot = jnp.where(lanes == picked, 1.0, 0.0).astype(bf)
        rows = dot(hot, kv)
        code = jnp.full((fetch, 1), -1, jnp.int32)
        for title in range(per_part):
            code = jnp.where(picked == at_ref[title], step * per_part + title, code)
        mark = jnp.where(lead, jnp.nan, code.astype(f32))
        at = pl.ds(part * fetch, fetch)
        rows_ref[at, :] = jnp.where(code >= 0, mark, rows).astype(bf)
        moves.append(pltpu.make_async_copy(rows_ref.at[at, :], sent_ref.at[at, :], sems.at[part]))
        moves[-1].start()
    for move in moves:
        move.wait()


def mask_kernel(ready, slots_ref, mask_ref):
    all_slots = slots_ref[...].astype(f32).T.astype(jnp.int32)
    for tile in range(all_slots.shape[0] // TILE):
        slots = all_slots[tile * TILE : (tile + 1) * TILE, :]
        lanes = lax.broadcasted_iota(jnp.int32, (TILE, TPR * TILE), 1)
        edges = lanes == lax.broadcasted_iota(jnp.int32, (TILE, TPR * TILE), 0)
        for edge in range(DEG):
            edges = edges | (lanes == slots[:, edge : edge + 1])
        mask_ref[tile * TILE : (tile + 1) * TILE, :] = jnp.where(edges, 1.0, 0.0).astype(bf)


def attn_kernel(ready, who_ref, titles_ref, w_in_ref, w_out_ref, *refs):
    outs, total = refs[:-1], refs[-1]
    ready(1, 2)
    titles = titles_ref[...]
    q = dot_nt(titles, w_in_ref[0]).astype(bf)
    k = dot_nt(titles, w_in_ref[1]).astype(bf)
    v = dot_nt(titles, w_in_ref[2]).astype(bf)
    cols = q.shape[1]
    heads = cols // HD
    lanes = lax.broadcasted_iota(jnp.int32, (SEQ, cols), 1) // HD
    ready(3)
    for title in range(titles.shape[0] // SEQ):
        rows = slice(title * SEQ, (title + 1) * SEQ)
        qt, kt, vt = q[rows], k[rows], v[rows]
        stacked = jnp.concatenate(
            [jnp.where(lanes == h, qt, jnp.zeros_like(qt)) for h in range(heads)], axis=0
        )
        scores = dot_nt(stacked, kt) * (1.0 / HD**0.5)
        expo = jnp.exp(scores - jnp.max(scores, axis=-1, keepdims=True))
        probs = (expo / jnp.sum(expo, axis=-1, keepdims=True)).astype(bf)
        mixed = dot(probs, vt)
        context = mixed[:SEQ]
        for h in range(1, heads):
            context = jnp.where(lanes == h, mixed[h * SEQ : (h + 1) * SEQ], context)
        total[rows, :] = dot(context.astype(bf), w_out_ref[...])
    chunk = outs[0].shape[0] - PAD
    firsts = first_rows(total)
    for step, out in enumerate(outs):
        at = pl.ds(pl.multiple_of(who_ref[step] * chunk, chunk), chunk)
        out[:chunk, :] = total[at, :].astype(out.dtype)
        out[chunk:, :] = firsts.astype(out.dtype)


def first_rows(ref):
    sub = lax.broadcasted_iota(jnp.int32, (PAD, ref.shape[1]), 0)
    rows = jnp.zeros((PAD, ref.shape[1]), f32)
    for title in range(ref.shape[0] // SEQ):
        row = ref[title * SEQ : title * SEQ + 1, :].astype(f32)
        rows = jnp.where(sub == title, row, rows)
    return rows


def norm_one_kernel(
    ready, who_ref, titles_ref, gains_ref, w_in_ref, w_out_ref, own_ref, *refs
):
    *parts, out, first_hidden, first_terms = refs
    chunk = own_ref.shape[0] - PAD
    total = own_ref[...]
    for part in parts:
        total = total + part[...].astype(f32)
    at = pl.ds(pl.multiple_of(who_ref[0] * chunk, chunk), chunk)
    base = jnp.concatenate([titles_ref[at, :].astype(f32), first_rows(titles_ref)], axis=0)
    hidden = layer_norm(base + total, gains_ref[0:1, :]).astype(bf)
    out[:chunk, :] = hidden[:chunk]
    firsts = hidden[chunk:]
    first_hidden[...] = firsts
    terms = dot(gelu(dot(firsts, w_in_ref[...])).astype(bf), w_out_ref[...])
    first_terms[...] = terms
    out[chunk:, :] = terms.astype(bf)


def gelu(x):
    return 0.5 * x * (1.0 + lax.erf(x * (0.5**0.5)))


def ffn_kernel(ready, w_in_ref, w_out_ref, gains_ref, first_hidden, first_terms, *refs):
    *refs, first = refs
    count = len(refs) // 2
    ins, outs = refs[:count], refs[count:]
    chunk = outs[0].shape[0]
    hidden = jnp.concatenate([ref[:chunk, :] for ref in ins], axis=0)
    inner = gelu(dot(hidden, w_in_ref[...])).astype(bf)
    total = dot(inner, w_out_ref[...])
    for step, out in enumerate(outs):
        out[...] = total[step * chunk : (step + 1) * chunk].astype(out.dtype)
    terms = first_terms[...]
    for ref in ins[1:]:
        terms = terms + ref[chunk:, :].astype(f32)
    done = layer_norm(first_hidden[...].astype(f32) + terms, gains_ref[1:2, :])
    first[...] = done[: first.shape[0]].astype(bf)


def norm_two_kernel(ready, hidden_ref, gains_ref, own_ref, *refs):
    *parts, out = refs
    total = own_ref[...]
    for part in parts:
        total = total + part[...].astype(f32)
    hidden = hidden_ref[: out.shape[0], :].astype(f32)
    out[...] = layer_norm(hidden + total, gains_ref[1:2, :]).astype(bf)


def pack_kernel(ready, *refs):
    *parts, out = refs
    per_part = parts[0].shape[0]
    sub = lax.broadcasted_iota(jnp.int32, out.shape, 0)
    rows = jnp.zeros(out.shape, f32)
    for turn, ref in enumerate(parts):
        for title in range(per_part):
            row = ref[title : title + 1, :].astype(f32)
            rows = jnp.where(sub == turn * per_part + title, row, rows)
    out[...] = rows.astype(bf)


def join_kernel(ready, *refs):
    *parts, out = refs
    start = 0
    for part in parts:
        out[start : start + part.shape[0], :] = part[...]
        start += part.shape[0]


def place_kernel(whose, ready, who_ref, *refs):
    *blocks, out = refs
    chunk = out.shape[0] // len(whose)
    pieces = [
        block[start : start + chunk, :] for block in blocks for start in range(0, block.shape[0], chunk)
    ]
    for step, piece in zip(whose, pieces):
        out[pl.ds(pl.multiple_of(who_ref[step] * chunk, chunk), chunk), :] = piece


def own_kernel(ready, table_ref, w_ref, kv_ref, q_ref):
    cols = w_ref.shape[1]
    table = table_ref[...]
    kv_ref[:, :cols] = dot_nt(table, w_ref[1]).astype(bf)
    kv_ref[:, cols:] = dot_nt(table, w_ref[2]).astype(bf)
    q_ref[...] = dot_nt(table, w_ref[0]).astype(bf)


def tail_rows(count):
    return -(-count // PAD) * PAD


def graph_kernel(
    ready, who_ref, cols_ref, at_ref, q_ref, kv_ref, w_ref, mask_ref, far_ref, first_ref, *refs
):
    *packs, out_ref, k_all, v_all, firsts = refs
    nodes, cols = q_ref.shape
    row_tiles = nodes // TILE
    per_part = first_ref.shape[0]
    members = len(packs)
    for step, ref in enumerate(packs):
        rows = ref[...].astype(f32)
        for turn in range(firsts.shape[0] // per_part // members):
            for title in range(per_part):
                place = (turn * members + who_ref[step] % members) * per_part + title
                at = turn * per_part + title
                firsts[pl.ds(place, 1), :] = rows[at : at + 1]
    firsts[0:per_part, :] = first_ref[...].astype(f32)
    first = firsts[...].astype(bf)
    ready(5)
    first_kv = jnp.concatenate([dot_nt(first, w_ref[1]), dot_nt(first, w_ref[2])], axis=1).astype(bf)
    first_q = dot_nt(first, w_ref[0])
    ready(2, 4)
    for tile in range(row_tiles):
        span = slice(tile * TILE, (tile + 1) * TILE)
        rows = kv_ref[span, :].astype(f32)
        sub = lax.broadcasted_iota(jnp.int32, (TILE, 2 * cols), 0) + tile * TILE
        for title in range(per_part):
            row = first_kv[title : title + 1].astype(f32)
            rows = jnp.where(sub == at_ref[title], row, rows)
        rows = rows.astype(bf)
        k_all[span, :] = rows[:, :cols]
        v_all[span, :] = rows[:, cols:]
    ready(7)
    lanes = lax.broadcasted_iota(jnp.int32, (TILE, first_kv.shape[0]), 1).astype(f32)
    for tile in range(far_ref.shape[0] // TILE):
        rows = far_ref[tile * TILE : (tile + 1) * TILE, :].astype(f32)
        code = jnp.where(rows[:, 0:1] != rows[:, 0:1], rows[:, 1:2], -1.0)
        hot = jnp.where(lanes == code, 1.0, 0.0).astype(bf)
        fixed = jnp.where(code >= 0.0, dot(hot, first_kv), rows).astype(bf)
        span = slice(nodes + tile * TILE, nodes + (tile + 1) * TILE)
        k_all[span, :] = fixed[:, :cols]
        v_all[span, :] = fixed[:, cols:]

    ready(1, 3, 6)
    heads = cols // GHD
    head_of = lax.broadcasted_iota(jnp.int32, (TILE, cols), 1) // GHD
    for tile in range(row_tiles):
        q = q_ref[tile * TILE : (tile + 1) * TILE, :].astype(f32)
        sub = lax.broadcasted_iota(jnp.int32, (TILE, cols), 0) + tile * TILE
        for title in range(per_part):
            q = jnp.where(sub == at_ref[title], first_q[title : title + 1], q)
        q = q.astype(bf)
        stacked = jnp.concatenate(
            [jnp.where(head_of == h, q, jnp.zeros_like(q)) for h in range(heads)], axis=0
        )
        starts = [pl.multiple_of(cols_ref[tile, c] * TILE, TILE) for c in range(TPR)]
        keys = jnp.concatenate([k_all[pl.ds(start, TILE), :] for start in starts], axis=0)
        values = jnp.concatenate([v_all[pl.ds(start, TILE), :] for start in starts], axis=0)
        scores = dot_nt(stacked, keys) * (1.0 / GHD**0.5)
        mask = mask_ref[tile * TILE : (tile + 1) * TILE, :].astype(f32)
        mask = jnp.concatenate([mask] * heads, axis=0) > 0.5
        masked = jnp.where(mask, scores, -jnp.inf)
        expo = jnp.exp(masked - jnp.max(masked, axis=-1, keepdims=True))
        scale = 1.0 / jnp.sum(expo, axis=-1, keepdims=True)
        mixed = dot(expo.astype(bf), values) * scale
        out = mixed[:TILE]
        for h in range(1, heads):
            out = jnp.where(head_of == h, mixed[h * TILE : (h + 1) * TILE], out)
        out_ref[:, tile * TILE : (tile + 1) * TILE] = out.T.astype(bf)


def local(

    titles,
    w_attn_in,
    w_attn_out,
    w_ffn_in,
    w_ffn_out,
    gains,
    node_table,
    w_graph,
    title_nodes,
    send_ids,
    tile_cols,
    nbr_slots,
):
    tok_rows, width = titles.shape
    nodes = node_table.shape[0]
    cols = w_graph.shape[2]
    mp = lax.axis_size("mp")
    dp = lax.axis_size("dp")
    me_mp = lax.axis_index("mp").astype(jnp.int32)
    me_dp = lax.axis_index("dp").astype(jnp.int32).reshape(1)
    who = me_mp ^ jnp.arange(mp, dtype=jnp.int32)
    chunk = tok_rows // mp
    per_part = title_nodes.shape[0]
    fetch = send_ids.shape[2]

    def swap(value, step, axis="mp"):
        return lax.ppermute(value, axis, [(i, i ^ step) for i in range(lax.axis_size(axis))])

    w_attn_in = jnp.swapaxes(w_attn_in, 1, 2)
    w_graph = jnp.swapaxes(w_graph, 1, 2)
    sent = call(
        send_kernel,
        shape((dp * fetch, 2 * cols), bf),
        (me_dp, title_nodes, send_ids[0], node_table, w_graph),
        smem=(0,),
        hbm=(4, 3, 2, 1),
        scalars=(1,),
        out_specs=HBM,
        scratch=[pltpu.VMEM((dp * fetch, 2 * cols), bf), pltpu.SemaphoreType.DMA((dp,))],
        flops=2 * nodes * width * 2 * cols + 2 * dp * fetch * nodes * 2 * cols,
        name="send",
    )
    far = lax.all_to_all(
        sent.reshape(dp, fetch, 2 * cols), "dp", split_axis=0, concat_axis=0, tiled=True
    ).reshape(dp * fetch, 2 * cols)
    titles, _ = lax.optimization_barrier((titles, sent))

    terms = call(
        attn_kernel,
        tuple(shape((chunk + PAD, width), bf if step else f32) for step in range(mp)),
        (who, titles, w_attn_in, w_attn_out),
        smem=(0,),
        hbm=(1, 2, 3),
        scratch=[pltpu.VMEM((tok_rows, width), f32)],
        flops=2 * tok_rows * width * 4 * w_attn_in.shape[1],
        name="attn",
    )
    parts = [swap(terms[step], step) for step in range(1, mp)]
    mask = call(
        mask_kernel, shape((nodes, TPR * TILE), bf), (nbr_slots.T,), flops=4 * 10**9, name="mask"
    )
    kv, q = call(
        own_kernel,
        (shape((nodes, 2 * cols), bf), shape((nodes, cols), bf)),
        (node_table, w_graph),
        flops=2 * 10**9,
        name="own",
    )
    parts, mask, kv, q = lax.optimization_barrier((parts, mask, kv, q))
    hidden, first_hidden, first_terms = call(
        norm_one_kernel,
        (shape((chunk + PAD, width), bf), shape((PAD, width), bf), shape((PAD, width), f32)),
        (who, titles, gains, w_ffn_in, w_ffn_out, terms[0], *parts),
        smem=(0,),
        name="norm_one",
    )
    hiddens = [hidden] + [swap(hidden, step) for step in range(1, mp)]
    *terms, first = call(
        ffn_kernel,
        tuple(shape((chunk, width), bf if step else f32) for step in range(mp))
        + (shape((per_part, width), bf),),
        (w_ffn_in, w_ffn_out, gains, first_hidden, first_terms, *hiddens),
        flops=4 * tok_rows * width * w_ffn_in.shape[1],
        name="ffn",
    )
    parts = [swap(terms[step], step) for step in range(1, mp)]
    done = call(
        norm_two_kernel,
        shape((chunk, width), bf),
        (hidden, gains, terms[0], *parts),
        name="norm_two",
    )
    share = 2
    turns = dp // share
    firsts = [
        lax.ppermute(
            first,
            ("dp", "mp"),
            [
                (p * mp + m, (p ^ (turn * share + m % share)) * mp + m)
                for p in range(dp)
                for m in range(mp)
                if turn or m % share
            ],
        )
        for turn in range(turns)
    ]
    whose, blocks, step = [0], [done], mp // 2
    while step:
        rows = blocks[0]
        if len(blocks) > 1:
            dims = (sum(block.shape[0] for block in blocks), width)
            rows = call(join_kernel, shape(dims, bf), blocks, name="join")
        blocks = blocks + [swap(rows, step)]
        whose = whose + [other ^ step for other in whose]
        step //= 2
    encoded = call(
        functools.partial(place_kernel, whose),
        shape((tok_rows, width), bf),
        (who, *blocks),
        smem=(0,),
        name="place",
    )
    encoded, firsts = lax.optimization_barrier((encoded, firsts))
    pack = call(pack_kernel, shape((tail_rows(turns * per_part), width), bf), firsts, name="pack")
    packs = [pack, swap(pack, 1)]

    keys = nodes + dp * fetch
    graph_out = call(
        graph_kernel,
        shape((cols, nodes), bf),
        (who, tile_cols, title_nodes, q, kv, w_graph, mask, far, first, *packs),
        smem=(0,),
        hbm=(5, 2, 4, 7, 1, 3, 6),
        scalars=(1, 2),
        scratch=[
            pltpu.VMEM((keys, cols), bf),
            pltpu.VMEM((keys, cols), bf),
            pltpu.VMEM((dp * per_part, width), f32),
        ],
        flops=10**9,
        name="graph",
    )
    return (encoded, graph_out.T)


def solution(mesh):
    in_specs = (
        P("dp", None),
        P(None, None, "mp"),
        P("mp", None),
        P(None, "mp"),
        P("mp", None),
        P(),
        P("dp", None),
        P(None, None, "mp"),
        P("dp"),
        P("dp", None, None),
        P("dp", None),
        P("dp", None),
    )
    out_specs = (P("dp", None), P("dp", "mp"))
    return jax.shard_map(
        local, mesh=mesh, in_specs=in_specs, out_specs=out_specs, check_vma=False
    )
```

```python
import functools
import jax
import jax.numpy as jnp
from jax import lax
from jax.experimental import pallas as pl
from jax.experimental.pallas import tpu as pltpu
from jax.sharding import PartitionSpec as P

SEQ = 128
TILE = 128
DEG = 16
TPR = 6
HD = 64
GHD = 96

eps_norm = 1e-06
bf = jnp.bfloat16
f32 = jnp.float32

VMEM = pl.BlockSpec(memory_space=pltpu.VMEM)
SMEM = pl.BlockSpec(memory_space=pltpu.SMEM)
HBM = pl.BlockSpec(memory_space=pltpu.HBM)
PAD = 16
NT = (((1,), (1,)), ((), ()))
TN = (((0,), (0,)), ((), ()))


def call(
    kernel, outs, args, smem=(), hbm=(), scalars=(), scratch=(), out_specs=None, flops=0, name=None
):
    count, out_count, own = len(args), len(jax.tree.leaves(outs)), len(scratch)
    specs = [SMEM if i in smem else HBM if i in hbm else VMEM for i in range(count)]
    nbytes = sum(a.size * a.dtype.itemsize for a in args)
    space = [pltpu.SMEM if i in scalars else pltpu.VMEM for i in hbm]
    buffers = [kind(args[i].shape, args[i].dtype) for kind, i in zip(space, hbm)]
    sems = [pltpu.SemaphoreType.DMA((len(hbm),))] if hbm else []

    def body(*refs):
        ins, rest = list(refs[:count]), refs[count:]
        kept, moved = rest[: out_count + own], rest[out_count + own :]
        moves = {}
        for j, i in enumerate(hbm):
            moves[i] = pltpu.make_async_copy(ins[i], moved[j], moved[-1].at[j])
            moves[i].start()
            ins[i] = moved[j]

        def ready(*wanted):
            for i in wanted:
                moves[i].wait()

        kernel(ready, *ins, *kept)

    return pl.pallas_call(
        body,
        out_shape=outs,
        in_specs=specs,
        out_specs=jax.tree.map(lambda _: VMEM, outs) if out_specs is None else out_specs,
        scratch_shapes=list(scratch) + buffers + sems,
        compiler_params=pltpu.CompilerParams(vmem_limit_bytes=(60 if hbm else 40) * 1024 * 1024),
        cost_estimate=pl.CostEstimate(flops=flops, bytes_accessed=nbytes, transcendentals=0),
        name=name,
    )(*args)


def shape(dims, dtype):
    return jax.ShapeDtypeStruct(dims, dtype)


def dot(a, b):
    return jnp.dot(a, b, preferred_element_type=f32)


def dot_nt(a, b):
    return lax.dot_general(a, b, NT, preferred_element_type=f32)


def dot_tn(a, b):
    return lax.dot_general(a, b, TN, preferred_element_type=f32)


def layer_norm(values, gain):
    mean = jnp.mean(values, axis=-1, keepdims=True)
    centred = values - mean
    var = jnp.mean(centred * centred, axis=-1, keepdims=True)
    return centred * lax.rsqrt(var + eps_norm) * gain


def send_kernel(ready, me_ref, at_ref, ids_ref, table_ref, w_ref, sent_ref, rows_ref, sems):
    cols = w_ref.shape[1]
    per_part = at_ref.shape[0]
    fetch, nodes = ids_ref.shape[1], table_ref.shape[0]
    ready(1, 2, 3, 4)
    table = table_ref[...]
    kv = jnp.concatenate([dot_nt(table, w_ref[1]), dot_nt(table, w_ref[2])], axis=1).astype(bf)
    ids = ids_ref[...].astype(f32).T.astype(jnp.int32)
    lanes = lax.broadcasted_iota(jnp.int32, (fetch, nodes), 1)
    lead = lax.broadcasted_iota(jnp.int32, (fetch, 2 * cols), 1) == 0
    moves = []
    for part in range(ids.shape[1]):
        step = me_ref[0] ^ part
        picked = ids[:, part : part + 1]
        hot = jnp.where(lanes == picked, 1.0, 0.0).astype(bf)
        rows = dot(hot, kv)
        code = jnp.full((fetch, 1), -1, jnp.int32)
        for title in range(per_part):
            code = jnp.where(picked == at_ref[title], step * per_part + title, code)
        mark = jnp.where(lead, jnp.nan, code.astype(f32))
        at = pl.ds(part * fetch, fetch)
        rows_ref[at, :] = jnp.where(code >= 0, mark, rows).astype(bf)
        moves.append(pltpu.make_async_copy(rows_ref.at[at, :], sent_ref.at[at, :], sems.at[part]))
        moves[-1].start()
    for move in moves:
        move.wait()


def mask_kernel(ready, slots_ref, mask_ref):
    all_slots = slots_ref[...].astype(f32).T.astype(jnp.int32)
    for tile in range(all_slots.shape[0] // TILE):
        slots = all_slots[tile * TILE : (tile + 1) * TILE, :]
        lanes = lax.broadcasted_iota(jnp.int32, (TILE, TPR * TILE), 1)
        edges = lanes == lax.broadcasted_iota(jnp.int32, (TILE, TPR * TILE), 0)
        for edge in range(DEG):
            edges = edges | (lanes == slots[:, edge : edge + 1])
        mask_ref[tile * TILE : (tile + 1) * TILE, :] = jnp.where(edges, 1.0, 0.0).astype(bf)


def attn_kernel(ready, who_ref, titles_ref, w_in_ref, w_out_ref, *refs):
    outs, total = refs[:-1], refs[-1]
    titles = titles_ref[...]
    q = dot_nt(titles, w_in_ref[0]).astype(bf)
    k = dot_nt(titles, w_in_ref[1]).astype(bf)
    v = dot_nt(titles, w_in_ref[2]).astype(bf)
    cols = q.shape[1]
    heads = cols // HD
    lanes = lax.broadcasted_iota(jnp.int32, (SEQ, cols), 1) // HD
    for title in range(titles.shape[0] // SEQ):
        rows = slice(title * SEQ, (title + 1) * SEQ)
        qt, kt, vt = q[rows], k[rows], v[rows]
        stacked = jnp.concatenate(
            [jnp.where(lanes == h, qt, jnp.zeros_like(qt)) for h in range(heads)], axis=0
        )
        scores = dot_nt(stacked, kt) * (1.0 / HD**0.5)
        expo = jnp.exp(scores - jnp.max(scores, axis=-1, keepdims=True))
        probs = (expo / jnp.sum(expo, axis=-1, keepdims=True)).astype(bf)
        mixed = dot(probs, vt)
        context = mixed[:SEQ]
        for h in range(1, heads):
            context = jnp.where(lanes == h, mixed[h * SEQ : (h + 1) * SEQ], context)
        total[rows, :] = dot(context.astype(bf), w_out_ref[...])
    chunk = outs[0].shape[0] - PAD
    firsts = first_rows(total)
    for step, out in enumerate(outs):
        at = pl.ds(pl.multiple_of(who_ref[step] * chunk, chunk), chunk)
        out[:chunk, :] = total[at, :].astype(out.dtype)
        out[chunk:, :] = firsts.astype(out.dtype)


def first_rows(ref):
    sub = lax.broadcasted_iota(jnp.int32, (PAD, ref.shape[1]), 0)
    rows = jnp.zeros((PAD, ref.shape[1]), f32)
    for title in range(ref.shape[0] // SEQ):
        row = ref[title * SEQ : title * SEQ + 1, :].astype(f32)
        rows = jnp.where(sub == title, row, rows)
    return rows


def norm_one_kernel(
    ready, who_ref, titles_ref, gains_ref, w_in_ref, w_out_ref, own_ref, *refs
):
    *parts, out, first_hidden, first_terms = refs
    chunk = own_ref.shape[0] - PAD
    total = own_ref[...]
    for part in parts:
        total = total + part[...].astype(f32)
    at = pl.ds(pl.multiple_of(who_ref[0] * chunk, chunk), chunk)
    base = jnp.concatenate([titles_ref[at, :].astype(f32), first_rows(titles_ref)], axis=0)
    hidden = layer_norm(base + total, gains_ref[0:1, :]).astype(bf)
    out[:chunk, :] = hidden[:chunk]
    firsts = hidden[chunk:]
    first_hidden[...] = firsts
    terms = dot(gelu(dot(firsts, w_in_ref[...])).astype(bf), w_out_ref[...])
    first_terms[...] = terms
    out[chunk:, :] = terms.astype(bf)


def gelu(x):
    return 0.5 * x * (1.0 + lax.erf(x * (0.5**0.5)))


def ffn_kernel(ready, w_in_ref, w_out_ref, gains_ref, first_hidden, first_terms, *refs):
    *refs, first = refs
    count = len(refs) // 2
    ins, outs = refs[:count], refs[count:]
    chunk = outs[0].shape[0]
    hidden = jnp.concatenate([ref[:chunk, :] for ref in ins], axis=0)
    inner = gelu(dot(hidden, w_in_ref[...])).astype(bf)
    total = dot(inner, w_out_ref[...])
    for step, out in enumerate(outs):
        out[...] = total[step * chunk : (step + 1) * chunk].astype(out.dtype)
    terms = first_terms[...]
    for ref in ins[1:]:
        terms = terms + ref[chunk:, :].astype(f32)
    done = layer_norm(first_hidden[...].astype(f32) + terms, gains_ref[1:2, :])
    first[...] = done[: first.shape[0]].astype(bf)


def norm_two_kernel(ready, hidden_ref, gains_ref, own_ref, *refs):
    *parts, out = refs
    total = own_ref[...]
    for part in parts:
        total = total + part[...].astype(f32)
    hidden = hidden_ref[: out.shape[0], :].astype(f32)
    out[...] = layer_norm(hidden + total, gains_ref[1:2, :]).astype(bf)


def pack_kernel(ready, *refs):
    *parts, out = refs
    per_part = parts[0].shape[0]
    sub = lax.broadcasted_iota(jnp.int32, out.shape, 0)
    rows = jnp.zeros(out.shape, f32)
    for turn, ref in enumerate(parts):
        for title in range(per_part):
            row = ref[title : title + 1, :].astype(f32)
            rows = jnp.where(sub == turn * per_part + title, row, rows)
    out[...] = rows.astype(bf)


def join_kernel(ready, *refs):
    *parts, out = refs
    start = 0
    for part in parts:
        out[start : start + part.shape[0], :] = part[...]
        start += part.shape[0]


def place_kernel(whose, ready, who_ref, *refs):
    *blocks, out = refs
    chunk = out.shape[0] // len(whose)
    pieces = [
        block[start : start + chunk, :] for block in blocks for start in range(0, block.shape[0], chunk)
    ]
    for step, piece in zip(whose, pieces):
        out[pl.ds(pl.multiple_of(who_ref[step] * chunk, chunk), chunk), :] = piece


def own_kernel(ready, table_ref, w_ref, kv_ref, q_ref):
    cols = w_ref.shape[1]
    table = table_ref[...]
    kv_ref[:, :cols] = dot_nt(table, w_ref[1]).astype(bf)
    kv_ref[:, cols:] = dot_nt(table, w_ref[2]).astype(bf)
    q_ref[...] = dot_nt(table, w_ref[0]).astype(bf)


def tail_rows(count):
    return -(-count // PAD) * PAD


def graph_kernel(
    ready, who_ref, cols_ref, at_ref, q_ref, kv_ref, w_ref, mask_ref, far_ref, first_ref, *refs
):
    *packs, out_ref, k_all, v_all, firsts = refs
    nodes, cols = q_ref.shape
    row_tiles = nodes // TILE
    per_part = first_ref.shape[0]
    members = len(packs)
    for step, ref in enumerate(packs):
        rows = ref[...].astype(f32)
        for turn in range(firsts.shape[0] // per_part // members):
            for title in range(per_part):
                place = (turn * members + who_ref[step]) * per_part + title
                at = turn * per_part + title
                firsts[pl.ds(place, 1), :] = rows[at : at + 1]
    firsts[0:per_part, :] = first_ref[...].astype(f32)
    first = firsts[...].astype(bf)
    first_kv = jnp.concatenate([dot_nt(first, w_ref[1]), dot_nt(first, w_ref[2])], axis=1).astype(bf)
    first_q = dot_nt(first, w_ref[0])
    for tile in range(row_tiles):
        span = slice(tile * TILE, (tile + 1) * TILE)
        rows = kv_ref[span, :].astype(f32)
        sub = lax.broadcasted_iota(jnp.int32, (TILE, 2 * cols), 0) + tile * TILE
        for title in range(per_part):
            row = first_kv[title : title + 1].astype(f32)
            rows = jnp.where(sub == at_ref[title], row, rows)
        rows = rows.astype(bf)
        k_all[span, :] = rows[:, :cols]
        v_all[span, :] = rows[:, cols:]
    lanes = lax.broadcasted_iota(jnp.int32, (TILE, first_kv.shape[0]), 1).astype(f32)
    for tile in range(far_ref.shape[0] // TILE):
        rows = far_ref[tile * TILE : (tile + 1) * TILE, :].astype(f32)
        code = jnp.where(rows[:, 0:1] != rows[:, 0:1], rows[:, 1:2], -1.0)
        hot = jnp.where(lanes == code, 1.0, 0.0).astype(bf)
        fixed = jnp.where(code >= 0.0, dot(hot, first_kv), rows).astype(bf)
        span = slice(nodes + tile * TILE, nodes + (tile + 1) * TILE)
        k_all[span, :] = fixed[:, :cols]
        v_all[span, :] = fixed[:, cols:]

    heads = cols // GHD
    head_of = lax.broadcasted_iota(jnp.int32, (TILE, cols), 1) // GHD
    for tile in range(row_tiles):
        q = q_ref[tile * TILE : (tile + 1) * TILE, :].astype(f32)
        sub = lax.broadcasted_iota(jnp.int32, (TILE, cols), 0) + tile * TILE
        for title in range(per_part):
            q = jnp.where(sub == at_ref[title], first_q[title : title + 1], q)
        q = q.astype(bf)
        stacked = jnp.concatenate(
            [jnp.where(head_of == h, q, jnp.zeros_like(q)) for h in range(heads)], axis=0
        )
        starts = [pl.multiple_of(cols_ref[tile, c] * TILE, TILE) for c in range(TPR)]
        keys = jnp.concatenate([k_all[pl.ds(start, TILE), :] for start in starts], axis=0)
        values = jnp.concatenate([v_all[pl.ds(start, TILE), :] for start in starts], axis=0)
        scores = dot_nt(stacked, keys) * (1.0 / GHD**0.5)
        mask = mask_ref[tile * TILE : (tile + 1) * TILE, :].astype(f32)
        mask = jnp.concatenate([mask] * heads, axis=0) > 0.5
        masked = jnp.where(mask, scores, -jnp.inf)
        expo = jnp.exp(masked - jnp.max(masked, axis=-1, keepdims=True))
        scale = 1.0 / jnp.sum(expo, axis=-1, keepdims=True)
        mixed = dot(expo.astype(bf), values) * scale
        out = mixed[:TILE]
        for h in range(1, heads):
            out = jnp.where(head_of == h, mixed[h * TILE : (h + 1) * TILE], out)
        out_ref[:, tile * TILE : (tile + 1) * TILE] = out.T.astype(bf)


def local(

    titles,
    w_attn_in,
    w_attn_out,
    w_ffn_in,
    w_ffn_out,
    gains,
    node_table,
    w_graph,
    title_nodes,
    send_ids,
    tile_cols,
    nbr_slots,
):
    tok_rows, width = titles.shape
    nodes = node_table.shape[0]
    cols = w_graph.shape[2]
    mp = lax.axis_size("mp")
    dp = lax.axis_size("dp")
    me_mp = lax.axis_index("mp").astype(jnp.int32)
    me_dp = lax.axis_index("dp").astype(jnp.int32).reshape(1)
    who = me_mp ^ jnp.arange(mp, dtype=jnp.int32)
    chunk = tok_rows // mp
    per_part = title_nodes.shape[0]
    fetch = send_ids.shape[2]

    def swap(value, step, axis="mp"):
        return lax.ppermute(value, axis, [(i, i ^ step) for i in range(lax.axis_size(axis))])

    w_attn_in = jnp.swapaxes(w_attn_in, 1, 2)
    w_graph = jnp.swapaxes(w_graph, 1, 2)
    sent = call(
        send_kernel,
        shape((dp * fetch, 2 * cols), bf),
        (me_dp, title_nodes, send_ids[0], node_table, w_graph),
        smem=(0,),
        hbm=(4, 3, 2, 1),
        scalars=(1,),
        out_specs=HBM,
        scratch=[pltpu.VMEM((dp * fetch, 2 * cols), bf), pltpu.SemaphoreType.DMA((dp,))],
        flops=2 * nodes * width * 2 * cols + 2 * dp * fetch * nodes * 2 * cols,
        name="send",
    )
    far = lax.all_to_all(
        sent.reshape(dp, fetch, 2 * cols), "dp", split_axis=0, concat_axis=0, tiled=True
    ).reshape(dp * fetch, 2 * cols)
    titles, _ = lax.optimization_barrier((titles, sent))

    terms = call(
        attn_kernel,
        tuple(shape((chunk + PAD, width), bf if step else f32) for step in range(mp)),
        (who, titles, w_attn_in, w_attn_out),
        smem=(0,),
        scratch=[pltpu.VMEM((tok_rows, width), f32)],
        flops=2 * tok_rows * width * 4 * w_attn_in.shape[1],
        name="attn",
    )
    parts = [swap(terms[step], step) for step in range(1, mp)]
    mask = call(
        mask_kernel, shape((nodes, TPR * TILE), bf), (nbr_slots.T,), flops=4 * 10**9, name="mask"
    )
    parts, mask = lax.optimization_barrier((parts, mask))
    hidden, first_hidden, first_terms = call(
        norm_one_kernel,
        (shape((chunk + PAD, width), bf), shape((PAD, width), bf), shape((PAD, width), f32)),
        (who, titles, gains, w_ffn_in, w_ffn_out, terms[0], *parts),
        smem=(0,),
        name="norm_one",
    )
    hiddens = [hidden] + [swap(hidden, step) for step in range(1, mp)]
    *terms, first = call(
        ffn_kernel,
        tuple(shape((chunk, width), bf if step else f32) for step in range(mp))
        + (shape((per_part, width), bf),),
        (w_ffn_in, w_ffn_out, gains, first_hidden, first_terms, *hiddens),
        flops=4 * tok_rows * width * w_ffn_in.shape[1],
        name="ffn",
    )
    parts = [swap(terms[step], step) for step in range(1, mp)]
    turns = dp // mp
    firsts = [
        lax.ppermute(
            first,
            ("dp", "mp"),
            [
                (p * mp + m, (p ^ (turn * mp + m)) * mp + m)
                for p in range(dp)
                for m in range(mp)
                if turn or m
            ],
        )
        for turn in range(turns)
    ]
    kv, q = call(
        own_kernel,
        (shape((nodes, 2 * cols), bf), shape((nodes, cols), bf)),
        (node_table, w_graph),
        flops=2 * 10**9,
        name="own",
    )
    hidden, kv, q = lax.optimization_barrier((hidden, kv, q))
    done = call(
        norm_two_kernel,
        shape((chunk, width), bf),
        (hidden, gains, terms[0], *parts),
        name="norm_two",
    )
    whose, blocks, step = [0], [done], mp // 2
    while step:
        rows = blocks[0]
        if len(blocks) > 1:
            dims = (sum(block.shape[0] for block in blocks), width)
            rows = call(join_kernel, shape(dims, bf), blocks, name="join")
        blocks = blocks + [swap(rows, step)]
        whose = whose + [other ^ step for other in whose]
        step //= 2
    encoded = call(
        functools.partial(place_kernel, whose),
        shape((tok_rows, width), bf),
        (who, *blocks),
        smem=(0,),
        name="place",
    )
    encoded, firsts, far = lax.optimization_barrier((encoded, firsts, far))
    pack = call(pack_kernel, shape((tail_rows(turns * per_part), width), bf), firsts, name="pack")
    packs = [pack] + [swap(pack, step) for step in range(1, mp)]

    keys = nodes + dp * fetch
    graph_out = call(
        graph_kernel,
        shape((cols, nodes), bf),
        (who, tile_cols, title_nodes, q, kv, w_graph, mask, far, first, *packs),
        smem=(0, 1, 2),
        scratch=[
            pltpu.VMEM((keys, cols), bf),
            pltpu.VMEM((keys, cols), bf),
            pltpu.VMEM((dp * per_part, width), f32),
        ],
        flops=10**9,
        name="graph",
    )
    return (encoded, graph_out.T)


def solution(mesh):
    in_specs = (
        P("dp", None),
        P(None, None, "mp"),
        P("mp", None),
        P(None, "mp"),
        P("mp", None),
        P(),
        P("dp", None),
        P(None, None, "mp"),
        P("dp"),
        P("dp", None, None),
        P("dp", None),
        P("dp", None),
    )
    out_specs = (P("dp", None), P("dp", "mp"))
    return jax.shard_map(
        local, mesh=mesh, in_specs=in_specs, out_specs=out_specs, check_vma=False
    )
```

```python
import functools
import jax
import jax.numpy as jnp
from jax import lax
from jax.experimental import pallas as pl
from jax.experimental.pallas import tpu as pltpu
from jax.sharding import PartitionSpec as P

SEQ = 128
TILE = 128
DEG = 16
TPR = 6
HD = 64
GHD = 96

eps_norm = 1e-06
bf = jnp.bfloat16
f32 = jnp.float32

VMEM = pl.BlockSpec(memory_space=pltpu.VMEM)
SMEM = pl.BlockSpec(memory_space=pltpu.SMEM)
HBM = pl.BlockSpec(memory_space=pltpu.HBM)
PAD = 16
NT = (((1,), (1,)), ((), ()))
TN = (((0,), (0,)), ((), ()))


def call(
    kernel,
    outs,
    args,
    smem=(),
    hbm=(),
    held=(),
    scalars=(),
    scratch=(),
    out_specs=None,
    late=False,
    flops=0,
    name=None,
):
    count, out_count, own = len(args), len(jax.tree.leaves(outs)), len(scratch)
    specs = [SMEM if i in smem else HBM if i in hbm or i in held else VMEM for i in range(count)]
    nbytes = sum(a.size * a.dtype.itemsize for a in args)
    space = [pltpu.SMEM if i in scalars else pltpu.VMEM for i in hbm]
    buffers = [kind(args[i].shape, args[i].dtype) for kind, i in zip(space, hbm)]
    sems = [pltpu.SemaphoreType.DMA((len(hbm),))] if hbm else []

    def body(*refs):
        ins, rest = list(refs[:count]), refs[count:]
        kept, moved = rest[: out_count + own], rest[out_count + own :]
        moves = {}
        for j, i in enumerate(hbm):
            moves[i] = pltpu.make_async_copy(ins[i], moved[j], moved[-1].at[j])
            ins[i] = moved[j]

        def start():
            for move in moves.values():
                move.start()

        def ready(*wanted):
            for i in wanted:
                moves[i].wait()

        ready.start = start
        if not late:
            start()
        kernel(ready, *ins, *kept)

    return pl.pallas_call(
        body,
        out_shape=outs,
        in_specs=specs,
        out_specs=jax.tree.map(lambda _: VMEM, outs) if out_specs is None else out_specs,
        scratch_shapes=list(scratch) + buffers + sems,
        compiler_params=pltpu.CompilerParams(vmem_limit_bytes=(60 if hbm else 40) * 1024 * 1024),
        cost_estimate=pl.CostEstimate(flops=flops, bytes_accessed=nbytes, transcendentals=0),
        name=name,
    )(*args)


def shape(dims, dtype):
    return jax.ShapeDtypeStruct(dims, dtype)


def dot(a, b):
    return jnp.dot(a, b, preferred_element_type=f32)


def dot_nt(a, b):
    return lax.dot_general(a, b, NT, preferred_element_type=f32)


def dot_tn(a, b):
    return lax.dot_general(a, b, TN, preferred_element_type=f32)


def layer_norm(values, gain):
    mean = jnp.mean(values, axis=-1, keepdims=True)
    centred = values - mean
    var = jnp.mean(centred * centred, axis=-1, keepdims=True)
    return centred * lax.rsqrt(var + eps_norm) * gain


def send_kernel(ready, me_ref, at_ref, ids_ref, table_ref, w_ref, sent_ref, rows_ref, sems):
    cols = w_ref.shape[1]
    per_part = at_ref.shape[0]
    fetch, nodes = ids_ref.shape[1], table_ref.shape[0]
    ready(1, 2, 3, 4)
    table = table_ref[...]
    kv = jnp.concatenate([dot_nt(table, w_ref[1]), dot_nt(table, w_ref[2])], axis=1).astype(bf)
    ids = ids_ref[...].astype(f32).T.astype(jnp.int32)
    lanes = lax.broadcasted_iota(jnp.int32, (fetch, nodes), 1)
    lead = lax.broadcasted_iota(jnp.int32, (fetch, 2 * cols), 1) == 0
    moves = []
    for part in range(ids.shape[1]):
        step = me_ref[0] ^ part
        picked = ids[:, part : part + 1]
        hot = jnp.where(lanes == picked, 1.0, 0.0).astype(bf)
        rows = dot(hot, kv)
        code = jnp.full((fetch, 1), -1, jnp.int32)
        for title in range(per_part):
            code = jnp.where(picked == at_ref[title], step * per_part + title, code)
        mark = jnp.where(lead, jnp.nan, code.astype(f32))
        at = pl.ds(part * fetch, fetch)
        rows_ref[at, :] = jnp.where(code >= 0, mark, rows).astype(bf)
        moves.append(pltpu.make_async_copy(rows_ref.at[at, :], sent_ref.at[at, :], sems.at[part]))
        moves[-1].start()
    for move in moves:
        move.wait()


def mask_kernel(ready, slots_ref, mask_ref):
    all_slots = slots_ref[...].astype(f32).T.astype(jnp.int32)
    for tile in range(all_slots.shape[0] // TILE):
        slots = all_slots[tile * TILE : (tile + 1) * TILE, :]
        lanes = lax.broadcasted_iota(jnp.int32, (TILE, TPR * TILE), 1)
        edges = lanes == lax.broadcasted_iota(jnp.int32, (TILE, TPR * TILE), 0)
        for edge in range(DEG):
            edges = edges | (lanes == slots[:, edge : edge + 1])
        mask_ref[tile * TILE : (tile + 1) * TILE, :] = jnp.where(edges, 1.0, 0.0).astype(bf)


def attn_kernel(ready, who_ref, titles_ref, w_in_ref, w_out_ref, *refs):
    outs, total = refs[:-1], refs[-1]
    titles = titles_ref[...]
    q = dot_nt(titles, w_in_ref[0]).astype(bf)
    k = dot_nt(titles, w_in_ref[1]).astype(bf)
    v = dot_nt(titles, w_in_ref[2]).astype(bf)
    cols = q.shape[1]
    heads = cols // HD
    lanes = lax.broadcasted_iota(jnp.int32, (SEQ, cols), 1) // HD
    for title in range(titles.shape[0] // SEQ):
        rows = slice(title * SEQ, (title + 1) * SEQ)
        qt, kt, vt = q[rows], k[rows], v[rows]
        stacked = jnp.concatenate(
            [jnp.where(lanes == h, qt, jnp.zeros_like(qt)) for h in range(heads)], axis=0
        )
        scores = dot_nt(stacked, kt) * (1.0 / HD**0.5)
        expo = jnp.exp(scores - jnp.max(scores, axis=-1, keepdims=True))
        probs = (expo / jnp.sum(expo, axis=-1, keepdims=True)).astype(bf)
        mixed = dot(probs, vt)
        context = mixed[:SEQ]
        for h in range(1, heads):
            context = jnp.where(lanes == h, mixed[h * SEQ : (h + 1) * SEQ], context)
        total[rows, :] = dot(context.astype(bf), w_out_ref[...])
    chunk = outs[0].shape[0] - PAD
    firsts = first_rows(total)
    for step, out in enumerate(outs):
        at = pl.ds(pl.multiple_of(who_ref[step] * chunk, chunk), chunk)
        out[:chunk, :] = total[at, :].astype(out.dtype)
        out[chunk:, :] = firsts.astype(out.dtype)


def first_rows(ref):
    sub = lax.broadcasted_iota(jnp.int32, (PAD, ref.shape[1]), 0)
    rows = jnp.zeros((PAD, ref.shape[1]), f32)
    for title in range(ref.shape[0] // SEQ):
        row = ref[title * SEQ : title * SEQ + 1, :].astype(f32)
        rows = jnp.where(sub == title, row, rows)
    return rows


def norm_one_kernel(
    ready, who_ref, titles_ref, gains_ref, w_in_ref, w_out_ref, own_ref, *refs
):
    *parts, out, first_hidden, first_terms = refs
    chunk = own_ref.shape[0] - PAD
    total = own_ref[...]
    for part in parts:
        total = total + part[...].astype(f32)
    at = pl.ds(pl.multiple_of(who_ref[0] * chunk, chunk), chunk)
    base = jnp.concatenate([titles_ref[at, :].astype(f32), first_rows(titles_ref)], axis=0)
    hidden = layer_norm(base + total, gains_ref[0:1, :]).astype(bf)
    out[:chunk, :] = hidden[:chunk]
    firsts = hidden[chunk:]
    first_hidden[...] = firsts
    terms = dot(gelu(dot(firsts, w_in_ref[...])).astype(bf), w_out_ref[...])
    first_terms[...] = terms
    out[chunk:, :] = terms.astype(bf)


def gelu(x):
    return 0.5 * x * (1.0 + lax.erf(x * (0.5**0.5)))


def ffn_kernel(ready, w_in_ref, w_out_ref, gains_ref, first_hidden, first_terms, *refs):
    *refs, first = refs
    count = len(refs) // 2
    ins, outs = refs[:count], refs[count:]
    chunk = outs[0].shape[0]
    hidden = jnp.concatenate([ref[:chunk, :] for ref in ins], axis=0)
    inner = gelu(dot(hidden, w_in_ref[...])).astype(bf)
    total = dot(inner, w_out_ref[...])
    for step, out in enumerate(outs):
        out[...] = total[step * chunk : (step + 1) * chunk].astype(out.dtype)
    terms = first_terms[...]
    for ref in ins[1:]:
        terms = terms + ref[chunk:, :].astype(f32)
    done = layer_norm(first_hidden[...].astype(f32) + terms, gains_ref[1:2, :])
    first[...] = done[: first.shape[0]].astype(bf)


def norm_two_kernel(ready, hidden_ref, gains_ref, own_ref, *refs):
    *parts, out = refs
    total = own_ref[...]
    for part in parts:
        total = total + part[...].astype(f32)
    hidden = hidden_ref[: out.shape[0], :].astype(f32)
    out[...] = layer_norm(hidden + total, gains_ref[1:2, :]).astype(bf)


def pack_kernel(ready, *refs):
    *parts, out = refs
    per_part = parts[0].shape[0]
    sub = lax.broadcasted_iota(jnp.int32, out.shape, 0)
    rows = jnp.zeros(out.shape, f32)
    for turn, ref in enumerate(parts):
        for title in range(per_part):
            row = ref[title : title + 1, :].astype(f32)
            rows = jnp.where(sub == turn * per_part + title, row, rows)
    out[...] = rows.astype(bf)


def join_kernel(ready, *refs):
    *parts, out = refs
    start = 0
    for part in parts:
        out[start : start + part.shape[0], :] = part[...]
        start += part.shape[0]


def place_kernel(whose, ready, who_ref, *refs):
    *blocks, out = refs
    chunk = out.shape[0] // len(whose)
    pieces = [
        block[start : start + chunk, :] for block in blocks for start in range(0, block.shape[0], chunk)
    ]
    for step, piece in zip(whose, pieces):
        out[pl.ds(pl.multiple_of(who_ref[step] * chunk, chunk), chunk), :] = piece


def own_kernel(
    ready, who_ref, at_ref, table_ref, w_ref, first_ref, *refs
):
    *packs, kv_ref, q_ref, first_kv_ref, features, firsts = refs
    members = len(packs)
    per_part, width = first_ref.shape
    cols = w_ref.shape[1]
    for step, ref in enumerate(packs):
        rows = ref[...].astype(f32)
        for turn in range(firsts.shape[0] // per_part // members):
            for title in range(per_part):
                place = (turn * members + who_ref[step]) * per_part + title
                at = turn * per_part + title
                firsts[pl.ds(place, 1), :] = rows[at : at + 1]
    firsts[0:per_part, :] = first_ref[...].astype(f32)
    ready(1, 2)
    for tile in range(features.shape[0] // TILE):
        span = slice(tile * TILE, (tile + 1) * TILE)
        rows = table_ref[span, :].astype(f32)
        sub = lax.broadcasted_iota(jnp.int32, (TILE, width), 0) + tile * TILE
        for title in range(per_part):
            rows = jnp.where(sub == at_ref[title], firsts[title : title + 1, :], rows)
        features[span, :] = rows.astype(bf)
    first = firsts[...].astype(bf)
    table = features[...]
    ready(3)
    for j in (1, 2):
        span = slice((j - 1) * cols, j * cols)
        first_kv_ref[:, span] = dot_nt(first, w_ref[j]).astype(bf)
        kv_ref[:, span] = dot_nt(table, w_ref[j]).astype(bf)
    q_ref[...] = dot_nt(table, w_ref[0]).astype(bf)


def tail_rows(count):
    return -(-count // PAD) * PAD


def graph_kernel(
    ready, cols_ref, q_ref, kv_ref, first_ref, mask_ref, far_hbm, out_ref, k_all, v_all, far_ref, sems
):
    pieces = sems.shape[0]
    size = far_ref.shape[0] // pieces
    moves = []
    for piece in range(pieces):
        at = pl.ds(piece * size, size)
        moves.append(pltpu.make_async_copy(far_hbm.at[at, :], far_ref.at[at, :], sems.at[piece]))
        moves[-1].start()
    ready.start()
    nodes, cols = q_ref.shape
    row_tiles = nodes // TILE
    first_kv = first_ref[...]
    lanes = lax.broadcasted_iota(jnp.int32, (TILE, first_kv.shape[0]), 1).astype(f32)
    for tile in range(far_ref.shape[0] // TILE):
        if tile * TILE % size == 0:
            moves[tile * TILE // size].wait()
        rows = far_ref[tile * TILE : (tile + 1) * TILE, :].astype(f32)
        code = jnp.where(rows[:, 0:1] != rows[:, 0:1], rows[:, 1:2], -1.0)
        hot = jnp.where(lanes == code, 1.0, 0.0).astype(bf)
        fixed = jnp.where(code >= 0.0, dot(hot, first_kv), rows).astype(bf)
        span = slice(nodes + tile * TILE, nodes + (tile + 1) * TILE)
        k_all[span, :] = fixed[:, :cols]
        v_all[span, :] = fixed[:, cols:]

    ready(2)
    k_all[:nodes, :] = kv_ref[:, :cols]
    v_all[:nodes, :] = kv_ref[:, cols:]
    ready(0, 1, 4)
    heads = cols // GHD
    head_of = lax.broadcasted_iota(jnp.int32, (TILE, cols), 1) // GHD
    for tile in range(row_tiles):
        q = q_ref[tile * TILE : (tile + 1) * TILE, :]
        stacked = jnp.concatenate(
            [jnp.where(head_of == h, q, jnp.zeros_like(q)) for h in range(heads)], axis=0
        )
        starts = [pl.multiple_of(cols_ref[tile, c] * TILE, TILE) for c in range(TPR)]
        keys = jnp.concatenate([k_all[pl.ds(start, TILE), :] for start in starts], axis=0)
        values = jnp.concatenate([v_all[pl.ds(start, TILE), :] for start in starts], axis=0)
        scores = dot_nt(stacked, keys) * (1.0 / GHD**0.5)
        mask = mask_ref[tile * TILE : (tile + 1) * TILE, :].astype(f32)
        mask = jnp.concatenate([mask] * heads, axis=0) > 0.5
        masked = jnp.where(mask, scores, -jnp.inf)
        expo = jnp.exp(masked - jnp.max(masked, axis=-1, keepdims=True))
        scale = 1.0 / jnp.sum(expo, axis=-1, keepdims=True)
        mixed = dot(expo.astype(bf), values) * scale
        out = mixed[:TILE]
        for h in range(1, heads):
            out = jnp.where(head_of == h, mixed[h * TILE : (h + 1) * TILE], out)
        out_ref[:, tile * TILE : (tile + 1) * TILE] = out.T.astype(bf)


def local(

    titles,
    w_attn_in,
    w_attn_out,
    w_ffn_in,
    w_ffn_out,
    gains,
    node_table,
    w_graph,
    title_nodes,
    send_ids,
    tile_cols,
    nbr_slots,
):
    tok_rows, width = titles.shape
    nodes = node_table.shape[0]
    cols = w_graph.shape[2]
    mp = lax.axis_size("mp")
    dp = lax.axis_size("dp")
    me_mp = lax.axis_index("mp").astype(jnp.int32)
    me_dp = lax.axis_index("dp").astype(jnp.int32).reshape(1)
    who = me_mp ^ jnp.arange(mp, dtype=jnp.int32)
    chunk = tok_rows // mp
    per_part = title_nodes.shape[0]
    fetch = send_ids.shape[2]

    def swap(value, step, axis="mp"):
        return lax.ppermute(value, axis, [(i, i ^ step) for i in range(lax.axis_size(axis))])

    w_attn_in = jnp.swapaxes(w_attn_in, 1, 2)
    w_graph = jnp.swapaxes(w_graph, 1, 2)
    sent = call(
        send_kernel,
        shape((dp * fetch, 2 * cols), bf),
        (me_dp, title_nodes, send_ids[0], node_table, w_graph),
        smem=(0,),
        hbm=(4, 3, 2, 1),
        scalars=(1,),
        out_specs=HBM,
        scratch=[pltpu.VMEM((dp * fetch, 2 * cols), bf), pltpu.SemaphoreType.DMA((dp,))],
        flops=2 * nodes * width * 2 * cols + 2 * dp * fetch * nodes * 2 * cols,
        name="send",
    )
    far = lax.all_to_all(
        sent.reshape(dp, fetch, 2 * cols), "dp", split_axis=0, concat_axis=0, tiled=True
    ).reshape(dp * fetch, 2 * cols)
    titles, _ = lax.optimization_barrier((titles, sent))

    terms = call(
        attn_kernel,
        tuple(shape((chunk + PAD, width), bf if step else f32) for step in range(mp)),
        (who, titles, w_attn_in, w_attn_out),
        smem=(0,),
        scratch=[pltpu.VMEM((tok_rows, width), f32)],
        flops=2 * tok_rows * width * 4 * w_attn_in.shape[1],
        name="attn",
    )
    parts = [swap(terms[step], step) for step in range(1, mp)]
    mask = call(
        mask_kernel, shape((nodes, TPR * TILE), bf), (nbr_slots.T,), flops=4 * 10**9, name="mask"
    )
    parts, mask = lax.optimization_barrier((parts, mask))
    hidden, first_hidden, first_terms = call(
        norm_one_kernel,
        (shape((chunk + PAD, width), bf), shape((PAD, width), bf), shape((PAD, width), f32)),
        (who, titles, gains, w_ffn_in, w_ffn_out, terms[0], *parts),
        smem=(0,),
        name="norm_one",
    )
    hiddens = [hidden] + [swap(hidden, step) for step in range(1, mp)]
    *terms, first = call(
        ffn_kernel,
        tuple(shape((chunk, width), bf if step else f32) for step in range(mp))
        + (shape((per_part, width), bf),),
        (w_ffn_in, w_ffn_out, gains, first_hidden, first_terms, *hiddens),
        flops=4 * tok_rows * width * w_ffn_in.shape[1],
        name="ffn",
    )
    parts = [swap(terms[step], step) for step in range(1, mp)]
    turns = dp // mp
    firsts = [
        lax.ppermute(
            first,
            ("dp", "mp"),
            [
                (p * mp + m, (p ^ (turn * mp + m)) * mp + m)
                for p in range(dp)
                for m in range(mp)
                if turn or m
            ],
        )
        for turn in range(turns)
    ]
    parts, firsts = lax.optimization_barrier((parts, firsts))
    done = call(
        norm_two_kernel,
        shape((chunk, width), bf),
        (hidden, gains, terms[0], *parts),
        name="norm_two",
    )
    pack = call(pack_kernel, shape((tail_rows(turns * per_part), width), bf), firsts, name="pack")
    packs = [pack] + [swap(pack, step) for step in range(1, mp)]
    whose, blocks, step = [0], [done], mp // 2
    while step:
        rows = blocks[0]
        if len(blocks) > 1:
            dims = (sum(block.shape[0] for block in blocks), width)
            rows = call(join_kernel, shape(dims, bf), blocks, name="join")
        blocks = blocks + [swap(rows, step)]
        whose = whose + [other ^ step for other in whose]
        step //= 2
    encoded = call(
        functools.partial(place_kernel, whose),
        shape((tok_rows, width), bf),
        (who, *blocks),
        smem=(0,),
        name="place",
    )
    encoded, far = lax.optimization_barrier((encoded, far))

    kv, q, first_kv = call(
        own_kernel,
        (shape((nodes, 2 * cols), bf), shape((nodes, cols), bf), shape((dp * per_part, 2 * cols), bf)),
        (who, title_nodes, node_table, w_graph, first, *packs),
        smem=(0,),
        hbm=(1, 2, 3),
        scalars=(1,),
        scratch=[pltpu.VMEM((nodes, width), bf), pltpu.VMEM((dp * per_part, width), f32)],
        flops=2 * 10**9,
        name="own",
    )
    keys = nodes + dp * fetch
    graph_out = call(
        graph_kernel,
        shape((cols, nodes), bf),
        (tile_cols, q, kv, first_kv, mask, far),
        hbm=(2, 1, 4, 0),
        held=(5,),
        scalars=(0,),
        late=True,
        scratch=[
            pltpu.VMEM((keys, cols), bf),
            pltpu.VMEM((keys, cols), bf),
            pltpu.VMEM(far.shape, bf),
            pltpu.SemaphoreType.DMA((4,)),
        ],
        flops=10**9,
        name="graph",
    )
    return (encoded, graph_out.T)


def solution(mesh):
    in_specs = (
        P("dp", None),
        P(None, None, "mp"),
        P("mp", None),
        P(None, "mp"),
        P("mp", None),
        P(),
        P("dp", None),
        P(None, None, "mp"),
        P("dp"),
        P("dp", None, None),
        P("dp", None),
        P("dp", None),
    )
    out_specs = (P("dp", None), P("dp", "mp"))
    return jax.shard_map(
        local, mesh=mesh, in_specs=in_specs, out_specs=out_specs, check_vma=False
    )
```

```python
import functools
import jax
import jax.numpy as jnp
from jax import lax
from jax.experimental import pallas as pl
from jax.experimental.pallas import tpu as pltpu
from jax.sharding import PartitionSpec as P

SEQ = 128
TILE = 128
DEG = 16
TPR = 6
HD = 64
GHD = 96

eps_norm = 1e-06
bf = jnp.bfloat16
f32 = jnp.float32

VMEM = pl.BlockSpec(memory_space=pltpu.VMEM)
SMEM = pl.BlockSpec(memory_space=pltpu.SMEM)
HBM = pl.BlockSpec(memory_space=pltpu.HBM)
PAD = 16
NT = (((1,), (1,)), ((), ()))
TN = (((0,), (0,)), ((), ()))


def call(
    kernel,
    outs,
    args,
    smem=(),
    hbm=(),
    scalars=(),
    scratch=(),
    out_specs=None,
    flops=0,
    name=None,
):
    count, out_count, own = len(args), len(jax.tree.leaves(outs)), len(scratch)
    specs = [SMEM if i in smem else HBM if i in hbm else VMEM for i in range(count)]
    nbytes = sum(a.size * a.dtype.itemsize for a in args)
    space = [pltpu.SMEM if i in scalars else pltpu.VMEM for i in hbm]
    buffers = [kind(args[i].shape, args[i].dtype) for kind, i in zip(space, hbm)]
    sems = [pltpu.SemaphoreType.DMA((len(hbm),))] if hbm else []

    def body(*refs):
        ins, rest = list(refs[:count]), refs[count:]
        kept, moved = rest[: out_count + own], rest[out_count + own :]
        moves = {}
        for j, i in enumerate(hbm):
            moves[i] = pltpu.make_async_copy(ins[i], moved[j], moved[-1].at[j])
            moves[i].start()
            ins[i] = moved[j]

        def ready(*wanted):
            for i in wanted:
                moves[i].wait()

        kernel(ready, *ins, *kept)

    return pl.pallas_call(
        body,
        out_shape=outs,
        in_specs=specs,
        out_specs=jax.tree.map(lambda _: VMEM, outs) if out_specs is None else out_specs,
        scratch_shapes=list(scratch) + buffers + sems,
        compiler_params=pltpu.CompilerParams(vmem_limit_bytes=(60 if hbm else 40) * 1024 * 1024),
        cost_estimate=pl.CostEstimate(flops=flops, bytes_accessed=nbytes, transcendentals=0),
        name=name,
    )(*args)


def shape(dims, dtype):
    return jax.ShapeDtypeStruct(dims, dtype)


def dot(a, b):
    return jnp.dot(a, b, preferred_element_type=f32)


def dot_nt(a, b):
    return lax.dot_general(a, b, NT, preferred_element_type=f32)


def dot_tn(a, b):
    return lax.dot_general(a, b, TN, preferred_element_type=f32)


def layer_norm(values, gain):
    mean = jnp.mean(values, axis=-1, keepdims=True)
    centred = values - mean
    var = jnp.mean(centred * centred, axis=-1, keepdims=True)
    return centred * lax.rsqrt(var + eps_norm) * gain


def one_hot(picked, nodes):
    lanes = lax.broadcasted_iota(jnp.int32, (picked.shape[0], nodes), 1)
    return jnp.where(lanes == picked, 1.0, 0.0).astype(bf)


def mark(rows, picked, at_ref, step):
    per_part = at_ref.shape[0]
    code = jnp.full(picked.shape, -1, jnp.int32)
    for title in range(per_part):
        code = jnp.where(picked == at_ref[title], step * per_part + title, code)
    lead = lax.broadcasted_iota(jnp.int32, rows.shape, 1) == 0
    return jnp.where(code >= 0, jnp.where(lead, jnp.nan, code.astype(f32)), rows)


def send_kernel(ready, me_ref, who_ref, at_ref, ids_ref, table_ref, w_ref, sent_ref, ids_t):
    cols = w_ref.shape[1]
    nodes, width = table_ref.shape
    parts, fetch = ids_ref.shape
    half, share = parts // 2, fetch // who_ref.shape[0]
    size = sent_ref.shape[0] // parts
    side, low = me_ref[1], me_ref[0] % half
    ready(2, 3)
    ids_t[...] = ids_ref[...].astype(f32).T

    def picks(ids, this, count):
        first = [ids[:, part : part + 1] for part in range(half)]
        second = [ids[:, half + part : half + part + 1] for part in range(half)]
        both = [jnp.where(this == 0, x, y).astype(jnp.int32) for x, y in zip(first, second)]
        return both, one_hot(jnp.concatenate(both, axis=0), nodes)

    def target(this, part):
        return pl.ds(pl.multiple_of((this * half + part) * size, size), size)

    mine = ids_t[pl.ds(pl.multiple_of(who_ref[0] * share, share), share), :]
    picked, hot = picks(mine, 1 - side, share)
    ready(4)
    rows = dot(hot, table_ref[...])
    for part in range(half):
        step = half + (low ^ part)
        raw = mark(rows[part * share : (part + 1) * share], picked[part], at_ref, step)
        raw = jnp.concatenate([raw[:, : width // 2], raw[:, width // 2 :]], axis=0)
        sent_ref[target(1 - side, part), :] = raw.astype(bf)
    picked, hot = picks(ids_t[:size, :], side, size)
    ready(5)
    table = table_ref[...]
    kv = jnp.concatenate([dot_nt(table, w_ref[1]), dot_nt(table, w_ref[2])], axis=1).astype(bf)
    rows = dot(hot, kv)
    for part in range(half):
        near = mark(rows[part * size : (part + 1) * size], picked[part], at_ref, low ^ part)
        sent_ref[target(side, part), :] = near.astype(bf)


def rest_kernel(ready, me_ref, at_ref, ids_ref, table_ref, w_ref, *refs):
    *outs, ids_t = refs
    size = outs[0].shape[0]
    table = table_ref[...]
    kv = jnp.concatenate([dot_nt(table, w_ref[1]), dot_nt(table, w_ref[2])], axis=1).astype(bf)
    ids_t[...] = ids_ref[...].astype(f32).T
    ids = ids_t[ids_t.shape[0] - size :, :]
    part = lax.broadcasted_iota(jnp.int32, ids.shape, 1)
    for step, out in enumerate(outs):
        picked = jnp.sum(jnp.where(part == me_ref[0] ^ step, ids, 0.0), axis=1, keepdims=True)
        picked = picked.astype(jnp.int32)
        rows = dot(one_hot(picked, table.shape[0]), kv)
        out[...] = mark(rows, picked, at_ref, step).astype(bf)


def pick_kernel(ready, me_ref, far_ref, out_ref):
    size = out_ref.shape[0]
    out_ref[...] = far_ref[pl.ds(pl.multiple_of((1 - me_ref[1]) * size, size), size), :]


def raw_kernel(half, whose, ready, me_ref, who_ref, w_ref, *refs):
    *blocks, out = refs
    cols = w_ref.shape[1]
    share = blocks[0].shape[0] // (2 * half)
    fetch = share * len(blocks)
    for step, block in zip(whose, blocks):
        spans = [slice(i * share, (i + 1) * share) for i in range(2 * half)]
        left = jnp.concatenate([block[span, :].astype(f32) for span in spans[::2]], axis=0)
        right = jnp.concatenate([block[span, :].astype(f32) for span in spans[1::2]], axis=0)
        marked = left[:, 0:1] != left[:, 0:1]
        code = left[:, 1:2]
        clean = jnp.concatenate([left, right], axis=1)
        clean = jnp.where(marked, 0.0, clean).astype(bf)
        kv = jnp.concatenate([dot_nt(clean, w_ref[1]), dot_nt(clean, w_ref[2])], axis=1)
        lead = lax.broadcasted_iota(jnp.int32, kv.shape, 1) == 0
        kv = jnp.where(marked, jnp.where(lead, jnp.nan, code), kv).astype(out.dtype)
        for part in range(half):
            at = pl.multiple_of(part * fetch + who_ref[step] * share, share)
            out[pl.ds(at, share), :] = kv[part * share : (part + 1) * share]


def mask_kernel(ready, slots_ref, mask_ref):
    all_slots = slots_ref[...].astype(f32).T.astype(jnp.int32)
    for tile in range(all_slots.shape[0] // TILE):
        slots = all_slots[tile * TILE : (tile + 1) * TILE, :]
        lanes = lax.broadcasted_iota(jnp.int32, (TILE, TPR * TILE), 1)
        edges = lanes == lax.broadcasted_iota(jnp.int32, (TILE, TPR * TILE), 0)
        for edge in range(DEG):
            edges = edges | (lanes == slots[:, edge : edge + 1])
        mask_ref[tile * TILE : (tile + 1) * TILE, :] = jnp.where(edges, 1.0, 0.0).astype(bf)


def attn_kernel(ready, who_ref, titles_ref, w_in_ref, w_out_ref, *refs):
    outs, total = refs[:-1], refs[-1]
    titles = titles_ref[...]
    q = dot_nt(titles, w_in_ref[0]).astype(bf)
    k = dot_nt(titles, w_in_ref[1]).astype(bf)
    v = dot_nt(titles, w_in_ref[2]).astype(bf)
    cols = q.shape[1]
    heads = cols // HD
    lanes = lax.broadcasted_iota(jnp.int32, (SEQ, cols), 1) // HD
    for title in range(titles.shape[0] // SEQ):
        rows = slice(title * SEQ, (title + 1) * SEQ)
        qt, kt, vt = q[rows], k[rows], v[rows]
        stacked = jnp.concatenate(
            [jnp.where(lanes == h, qt, jnp.zeros_like(qt)) for h in range(heads)], axis=0
        )
        scores = dot_nt(stacked, kt) * (1.0 / HD**0.5)
        expo = jnp.exp(scores - jnp.max(scores, axis=-1, keepdims=True))
        probs = (expo / jnp.sum(expo, axis=-1, keepdims=True)).astype(bf)
        mixed = dot(probs, vt)
        context = mixed[:SEQ]
        for h in range(1, heads):
            context = jnp.where(lanes == h, mixed[h * SEQ : (h + 1) * SEQ], context)
        total[rows, :] = dot(context.astype(bf), w_out_ref[...])
    chunk = (outs[0].shape[0] - PAD) // 2
    firsts = first_rows(total)
    for out, pair in zip(outs, ((0, 2), (1, 3))):
        for j, step in enumerate(pair):
            at = pl.ds(pl.multiple_of(who_ref[step] * chunk, chunk), chunk)
            out[j * chunk : (j + 1) * chunk, :] = total[at, :].astype(out.dtype)
        out[2 * chunk :, :] = firsts.astype(out.dtype)


def half_kernel(chunk, ready, kept_ref, came_ref, keep_ref, give_ref):
    total = kept_ref[...] + came_ref[...].astype(f32)
    keep_ref[:chunk, :] = total[:chunk]
    give_ref[:chunk, :] = total[chunk : 2 * chunk].astype(bf)
    if keep_ref.shape[0] > chunk:
        keep_ref[chunk:, :] = total[2 * chunk :]
        give_ref[chunk:, :] = total[2 * chunk :].astype(bf)


def first_rows(ref):
    sub = lax.broadcasted_iota(jnp.int32, (PAD, ref.shape[1]), 0)
    rows = jnp.zeros((PAD, ref.shape[1]), f32)
    for title in range(ref.shape[0] // SEQ):
        row = ref[title * SEQ : title * SEQ + 1, :].astype(f32)
        rows = jnp.where(sub == title, row, rows)
    return rows


def norm_one_kernel(
    ready, who_ref, titles_ref, gains_ref, w_in_ref, w_out_ref, own_ref, *refs
):
    *parts, out, first_hidden, first_terms = refs
    chunk = own_ref.shape[0] - PAD
    total = own_ref[...]
    for part in parts:
        total = total + part[...].astype(f32)
    at = pl.ds(pl.multiple_of(who_ref[0] * chunk, chunk), chunk)
    base = jnp.concatenate([titles_ref[at, :].astype(f32), first_rows(titles_ref)], axis=0)
    hidden = layer_norm(base + total, gains_ref[0:1, :]).astype(bf)
    out[:chunk, :] = hidden[:chunk]
    firsts = hidden[chunk:]
    first_hidden[...] = firsts
    terms = dot(gelu(dot(firsts, w_in_ref[...])).astype(bf), w_out_ref[...])
    first_terms[...] = terms
    out[chunk:, :] = terms.astype(bf)


def gelu(x):
    return 0.5 * x * (1.0 + lax.erf(x * (0.5**0.5)))


def ffn_kernel(ready, w_in_ref, w_out_ref, gains_ref, first_hidden, first_terms, *refs):
    *ins, kept, sent, first = refs
    chunk = kept.shape[0] // 2
    hidden = jnp.concatenate([ref[:chunk, :] for ref in ins], axis=0)
    inner = gelu(dot(hidden, w_in_ref[...])).astype(bf)
    total = dot(inner, w_out_ref[...])
    kept[...] = total[: 2 * chunk]
    sent[...] = total[2 * chunk :].astype(bf)
    terms = first_terms[...]
    for ref in ins[1:]:
        terms = terms + ref[chunk:, :].astype(f32)
    done = layer_norm(first_hidden[...].astype(f32) + terms, gains_ref[1:2, :])
    first[...] = done[: first.shape[0]].astype(bf)


def norm_two_kernel(ready, hidden_ref, gains_ref, own_ref, *refs):
    *parts, out = refs
    total = own_ref[...]
    for part in parts:
        total = total + part[...].astype(f32)
    hidden = hidden_ref[: out.shape[0], :].astype(f32)
    out[...] = layer_norm(hidden + total, gains_ref[1:2, :]).astype(bf)


def pack_kernel(ready, *refs):
    *parts, out = refs
    per_part = parts[0].shape[0]
    sub = lax.broadcasted_iota(jnp.int32, out.shape, 0)
    rows = jnp.zeros(out.shape, f32)
    for turn, ref in enumerate(parts):
        for title in range(per_part):
            row = ref[title : title + 1, :].astype(f32)
            rows = jnp.where(sub == turn * per_part + title, row, rows)
    out[...] = rows.astype(bf)


def place_kernel(whose, ready, who_ref, *refs):
    *blocks, out = refs
    chunk = out.shape[0] // len(whose)
    pieces = [
        block[start : start + chunk, :] for block in blocks for start in range(0, block.shape[0], chunk)
    ]
    for step, piece in zip(whose, pieces):
        out[pl.ds(pl.multiple_of(who_ref[step] * chunk, chunk), chunk), :] = piece


def own_kernel(
    ready, who_ref, at_ref, table_ref, w_ref, first_ref, *refs
):
    *packs, kv_ref, q_ref, first_kv_ref, features, firsts = refs
    members = len(packs)
    per_part, width = first_ref.shape
    cols = w_ref.shape[1]
    for step, ref in enumerate(packs):
        rows = ref[...].astype(f32)
        for turn in range(firsts.shape[0] // per_part // members):
            for title in range(per_part):
                place = (turn * members + who_ref[step]) * per_part + title
                at = turn * per_part + title
                firsts[pl.ds(place, 1), :] = rows[at : at + 1]
    firsts[0:per_part, :] = first_ref[...].astype(f32)
    for tile in range(features.shape[0] // TILE):
        span = slice(tile * TILE, (tile + 1) * TILE)
        rows = table_ref[span, :].astype(f32)
        sub = lax.broadcasted_iota(jnp.int32, (TILE, width), 0) + tile * TILE
        for title in range(per_part):
            rows = jnp.where(sub == at_ref[title], firsts[title : title + 1, :], rows)
        features[span, :] = rows.astype(bf)
    first = firsts[...].astype(bf)
    table = features[...]
    for j in (1, 2):
        span = slice((j - 1) * cols, j * cols)
        first_kv_ref[:, span] = dot_nt(first, w_ref[j]).astype(bf)
        kv_ref[:, span] = dot_nt(table, w_ref[j]).astype(bf)
    q_ref[...] = dot_nt(table, w_ref[0]).astype(bf)


def tail_rows(count):
    return -(-count // PAD) * PAD


def graph_kernel(
    ready, me_ref, cols_ref, q_ref, kv_ref, first_ref, mask_ref, far_ref, cross_ref, *refs
):
    *rest, out_ref, k_all, v_all = refs
    nodes, cols = q_ref.shape
    row_tiles = nodes // TILE
    first_kv = first_ref[...]
    k_all[:nodes, :] = kv_ref[:, :cols]
    v_all[:nodes, :] = kv_ref[:, cols:]

    def fix(rows, start):
        count = rows.shape[0]
        rows = rows.astype(f32)
        lanes = lax.broadcasted_iota(jnp.int32, (count, first_kv.shape[0]), 1).astype(f32)
        code = jnp.where(rows[:, 0:1] != rows[:, 0:1], rows[:, 1:2], -1.0)
        hot = jnp.where(lanes == code, 1.0, 0.0).astype(bf)
        fixed = jnp.where(code >= 0.0, dot(hot, first_kv), rows).astype(bf)
        at = pl.ds(pl.multiple_of(start, count), count)
        k_all[at, :] = fixed[:, :cols]
        v_all[at, :] = fixed[:, cols:]

    half = len(rest)
    size = rest[0].shape[0]
    side, low = me_ref[1], me_ref[0] % half
    for start in range(0, cross_ref.shape[0], TILE):
        fix(cross_ref[start : start + TILE, :], nodes + (1 - side) * cross_ref.shape[0] + start)
    for part in range(half):
        at = pl.ds(pl.multiple_of((side * half + part) * size, size), size)
        fix(far_ref[at, :], nodes + (side * half + part) * 2 * size)
    for step, ref in enumerate(rest):
        fix(ref[...], nodes + (side * half + (low ^ step)) * 2 * size + size)

    heads = cols // GHD
    head_of = lax.broadcasted_iota(jnp.int32, (TILE, cols), 1) // GHD
    for tile in range(row_tiles):
        q = q_ref[tile * TILE : (tile + 1) * TILE, :]
        stacked = jnp.concatenate(
            [jnp.where(head_of == h, q, jnp.zeros_like(q)) for h in range(heads)], axis=0
        )
        starts = [pl.multiple_of(cols_ref[tile, c] * TILE, TILE) for c in range(TPR)]
        keys = jnp.concatenate([k_all[pl.ds(start, TILE), :] for start in starts], axis=0)
        values = jnp.concatenate([v_all[pl.ds(start, TILE), :] for start in starts], axis=0)
        scores = dot_nt(stacked, keys) * (1.0 / GHD**0.5)
        mask = mask_ref[tile * TILE : (tile + 1) * TILE, :].astype(f32)
        mask = jnp.concatenate([mask] * heads, axis=0) > 0.5
        masked = jnp.where(mask, scores, -jnp.inf)
        expo = jnp.exp(masked - jnp.max(masked, axis=-1, keepdims=True))
        scale = 1.0 / jnp.sum(expo, axis=-1, keepdims=True)
        mixed = dot(expo.astype(bf), values) * scale
        out = mixed[:TILE]
        for h in range(1, heads):
            out = jnp.where(head_of == h, mixed[h * TILE : (h + 1) * TILE], out)
        out_ref[:, tile * TILE : (tile + 1) * TILE] = out.T.astype(bf)


def local(

    titles,
    w_attn_in,
    w_attn_out,
    w_ffn_in,
    w_ffn_out,
    gains,
    node_table,
    w_graph,
    title_nodes,
    send_ids,
    tile_cols,
    nbr_slots,
):
    tok_rows, width = titles.shape
    nodes = node_table.shape[0]
    cols = w_graph.shape[2]
    mp = lax.axis_size("mp")
    dp = lax.axis_size("dp")
    half = dp // 2
    me_mp = lax.axis_index("mp").astype(jnp.int32)
    me_dp = lax.axis_index("dp").astype(jnp.int32)
    me = jnp.stack([me_dp, me_dp // half])
    who = me_mp ^ jnp.arange(mp, dtype=jnp.int32)
    chunk = tok_rows // mp
    per_part = title_nodes.shape[0]
    fetch = send_ids.shape[2]
    share = fetch // mp

    def swap(value, step, axis="mp"):
        return lax.ppermute(value, axis, [(i, i ^ step) for i in range(lax.axis_size(axis))])

    def gather(value):
        whose, blocks, step = [0], [value], mp // 2
        while step:
            blocks = blocks + [swap(block, step) for block in blocks]
            whose = whose + [other ^ step for other in whose]
            step //= 2
        return whose, blocks

    def halves(kept, came, pad):
        dims = (chunk + pad, width)
        return call(
            functools.partial(half_kernel, chunk),
            (shape(dims, f32), shape(dims, bf)),
            (kept, came),
            name="half",
        )

    w_attn_in = jnp.swapaxes(w_attn_in, 1, 2)
    w_graph = jnp.swapaxes(w_graph, 1, 2)
    size = 2 * share
    sent = call(
        send_kernel,
        shape((dp * size, 2 * cols), bf),
        (me, who, title_nodes, send_ids[0], node_table, w_graph),
        smem=(0, 1),
        hbm=(4, 3, 5, 2),
        scalars=(2,),
        scratch=[pltpu.VMEM((fetch, dp), f32)],
        flops=3 * 10**9,
        name="send",
    )
    far = lax.all_to_all(
        sent.reshape(dp, size, 2 * cols), "dp", split_axis=0, concat_axis=0, tiled=True
    ).reshape(dp * size, 2 * cols)
    titles, _ = lax.optimization_barrier((titles, sent))

    kept, given = call(
        attn_kernel,
        (shape((2 * chunk + PAD, width), f32), shape((2 * chunk + PAD, width), bf)),
        (who, titles, w_attn_in, w_attn_out),
        smem=(0,),
        scratch=[pltpu.VMEM((tok_rows, width), f32)],
        flops=2 * tok_rows * width * 4 * w_attn_in.shape[1],
        name="attn",
    )
    keep, give = halves(kept, swap(given, 1), PAD)
    part = swap(give, 2)
    mask = call(
        mask_kernel, shape((nodes, TPR * TILE), bf), (nbr_slots.T,), flops=4 * 10**9, name="mask"
    )
    rest = call(
        rest_kernel,
        (shape((size, 2 * cols), bf),) * half,
        (me, title_nodes, send_ids[0], node_table, w_graph),
        smem=(0, 1),
        scratch=[pltpu.VMEM((fetch, dp), f32)],
        flops=2 * 10**9,
        name="rest",
    )
    part, mask = lax.optimization_barrier((part, mask))
    hidden, first_hidden, first_terms = call(
        norm_one_kernel,
        (shape((chunk + PAD, width), bf), shape((PAD, width), bf), shape((PAD, width), f32)),
        (who, titles, gains, w_ffn_in, w_ffn_out, keep, part),
        smem=(0,),
        name="norm_one",
    )
    whose, hiddens = gather(hidden)
    hiddens, rest = lax.optimization_barrier((hiddens, rest))
    kept, given, first = call(
        ffn_kernel,
        (
            shape((2 * chunk, width), f32),
            shape((2 * chunk, width), bf),
            shape((per_part, width), bf),
        ),
        (w_ffn_in, w_ffn_out, gains, first_hidden, first_terms, *hiddens),
        flops=4 * tok_rows * width * w_ffn_in.shape[1],
        name="ffn",
    )
    turns = dp // mp
    firsts = [
        lax.ppermute(
            first,
            ("dp", "mp"),
            [
                (p * mp + m, (p ^ (turn * mp + m)) * mp + m)
                for p in range(dp)
                for m in range(mp)
                if turn or m
            ],
        )
        for turn in range(turns)
    ]
    recv, far = lax.optimization_barrier((swap(given, 1), far))
    keep, give = halves(kept, recv, 0)
    give, far = lax.optimization_barrier((give, far))
    raw = call(pick_kernel, shape((half * size, 2 * cols), bf), (me, far), smem=(0,), name="pick")
    part = swap(give, 2)
    across = swap(raw, 2)
    rest = [rest[0]] + [swap(rest[step], step, "dp") for step in range(1, half)]
    part, firsts, across, rest = lax.optimization_barrier((part, firsts, across, rest))
    blocks = [raw, across, swap(raw, 1), swap(across, 1)]
    done = call(
        norm_two_kernel, shape((chunk, width), bf), (hidden, gains, keep, part), name="norm_two"
    )
    pack = call(pack_kernel, shape((tail_rows(turns * per_part), width), bf), firsts, name="pack")
    packs = [pack] + [swap(pack, step) for step in range(1, mp)]
    _, dones = gather(done)
    encoded = call(
        functools.partial(place_kernel, whose),
        shape((tok_rows, width), bf),
        (who, *dones),
        smem=(0,),
        name="place",
    )

    cross = call(
        functools.partial(raw_kernel, half, whose),
        shape((half * fetch, 2 * cols), bf if share % 16 == 0 else f32),
        (me, who, w_graph, *blocks),
        smem=(0, 1),
        flops=2 * 10**9,
        name="raw",
    )
    kv, q, first_kv = call(
        own_kernel,
        (shape((nodes, 2 * cols), bf), shape((nodes, cols), bf), shape((dp * per_part, 2 * cols), bf)),
        (who, title_nodes, node_table, w_graph, first, *packs),
        smem=(0, 1),
        scratch=[pltpu.VMEM((nodes, width), bf), pltpu.VMEM((dp * per_part, width), f32)],
        flops=2 * 10**9,
        name="own",
    )
    keys = nodes + dp * fetch
    graph_out = call(
        graph_kernel,
        shape((cols, nodes), bf),
        (me, tile_cols, q, kv, first_kv, mask, far, cross, *rest),
        smem=(0, 1),
        scratch=[pltpu.VMEM((keys, cols), bf), pltpu.VMEM((keys, cols), bf)],
        flops=4 * 10**9,
        name="graph",
    )
    return (encoded, graph_out.T)


def solution(mesh):
    in_specs = (
        P("dp", None),
        P(None, None, "mp"),
        P("mp", None),
        P(None, "mp"),
        P("mp", None),
        P(),
        P("dp", None),
        P(None, None, "mp"),
        P("dp"),
        P("dp", None, None),
        P("dp", None),
        P("dp", None),
    )
    out_specs = (P("dp", None), P("dp", "mp"))
    return jax.shard_map(
        local, mesh=mesh, in_specs=in_specs, out_specs=out_specs, check_vma=False
    )
```

```python
import functools
import jax
import jax.numpy as jnp
from jax import lax
from jax.experimental import pallas as pl
from jax.experimental.pallas import tpu as pltpu
from jax.sharding import PartitionSpec as P

SEQ = 128
TILE = 128
DEG = 16
TPR = 6
HD = 64
GHD = 96

eps_norm = 1e-06
bf = jnp.bfloat16
f32 = jnp.float32

VMEM = pl.BlockSpec(memory_space=pltpu.VMEM)
SMEM = pl.BlockSpec(memory_space=pltpu.SMEM)
HBM = pl.BlockSpec(memory_space=pltpu.HBM)
PAD = 16
NT = (((1,), (1,)), ((), ()))
TN = (((0,), (0,)), ((), ()))


def call(
    kernel,
    outs,
    args,
    smem=(),
    hbm=(),
    scalars=(),
    scratch=(),
    out_specs=None,
    flops=0,
    name=None,
):
    count, out_count, own = len(args), len(jax.tree.leaves(outs)), len(scratch)
    specs = [SMEM if i in smem else HBM if i in hbm else VMEM for i in range(count)]
    nbytes = sum(a.size * a.dtype.itemsize for a in args)
    space = [pltpu.SMEM if i in scalars else pltpu.VMEM for i in hbm]
    buffers = [kind(args[i].shape, args[i].dtype) for kind, i in zip(space, hbm)]
    sems = [pltpu.SemaphoreType.DMA((len(hbm),))] if hbm else []

    def body(*refs):
        ins, rest = list(refs[:count]), refs[count:]
        kept, moved = rest[: out_count + own], rest[out_count + own :]
        moves = {}
        for j, i in enumerate(hbm):
            moves[i] = pltpu.make_async_copy(ins[i], moved[j], moved[-1].at[j])
            moves[i].start()
            ins[i] = moved[j]

        def ready(*wanted):
            for i in wanted:
                moves[i].wait()

        kernel(ready, *ins, *kept)

    return pl.pallas_call(
        body,
        out_shape=outs,
        in_specs=specs,
        out_specs=jax.tree.map(lambda _: VMEM, outs) if out_specs is None else out_specs,
        scratch_shapes=list(scratch) + buffers + sems,
        compiler_params=pltpu.CompilerParams(vmem_limit_bytes=(60 if hbm else 40) * 1024 * 1024),
        cost_estimate=pl.CostEstimate(flops=flops, bytes_accessed=nbytes, transcendentals=0),
        name=name,
    )(*args)


def shape(dims, dtype):
    return jax.ShapeDtypeStruct(dims, dtype)


def dot(a, b):
    return jnp.dot(a, b, preferred_element_type=f32)


def dot_nt(a, b):
    return lax.dot_general(a, b, NT, preferred_element_type=f32)


def dot_tn(a, b):
    return lax.dot_general(a, b, TN, preferred_element_type=f32)


def layer_norm(values, gain):
    mean = jnp.mean(values, axis=-1, keepdims=True)
    centred = values - mean
    var = jnp.mean(centred * centred, axis=-1, keepdims=True)
    return centred * lax.rsqrt(var + eps_norm) * gain


def one_hot(picked, nodes):
    lanes = lax.broadcasted_iota(jnp.int32, (picked.shape[0], nodes), 1)
    return jnp.where(lanes == picked, 1.0, 0.0).astype(bf)


def mark(rows, picked, at_ref, step):
    per_part = at_ref.shape[0]
    code = jnp.full(picked.shape, -1, jnp.int32)
    for title in range(per_part):
        code = jnp.where(picked == at_ref[title], step * per_part + title, code)
    lead = lax.broadcasted_iota(jnp.int32, rows.shape, 1) == 0
    return jnp.where(code >= 0, jnp.where(lead, jnp.nan, code.astype(f32)), rows)


def send_kernel(ready, me_ref, who_ref, at_ref, ids_ref, table_ref, w_ref, sent_ref, ids_t):
    cols = w_ref.shape[1]
    nodes, width = table_ref.shape
    parts, fetch = ids_ref.shape
    half = parts // 2
    size = sent_ref.shape[0] // parts
    share = size // 2
    side, low = lax.div(me_ref[0], half), lax.rem(me_ref[0], half)
    ready(2, 3)
    ids_t[...] = ids_ref[...].astype(f32).T

    def picks(ids, this, count):
        first = [ids[:, part : part + 1] for part in range(half)]
        second = [ids[:, half + part : half + part + 1] for part in range(half)]
        both = [jnp.where(this == 0, x, y).astype(jnp.int32) for x, y in zip(first, second)]
        return both, one_hot(jnp.concatenate(both, axis=0), nodes)

    def target(this, part):
        return pl.ds(pl.multiple_of((this * half + part) * size, size), size)

    mine = ids_t[pl.ds(pl.multiple_of(who_ref[0] * share, share), share), :]
    picked, hot = picks(mine, 1 - side, share)
    ready(4)
    rows = dot(hot, table_ref[...])
    for part in range(half):
        step = half + (low ^ part)
        raw = mark(rows[part * share : (part + 1) * share], picked[part], at_ref, step)
        raw = jnp.concatenate([raw[:, : width // 2], raw[:, width // 2 :]], axis=0)
        sent_ref[target(1 - side, part), :] = raw.astype(bf)
    picked, hot = picks(ids_t[:size, :], side, size)
    ready(5)
    table = table_ref[...]
    kv = jnp.concatenate([dot_nt(table, w_ref[1]), dot_nt(table, w_ref[2])], axis=1).astype(bf)
    rows = dot(hot, kv)
    for part in range(half):
        near = mark(rows[part * size : (part + 1) * size], picked[part], at_ref, low ^ part)
        sent_ref[target(side, part), :] = near.astype(bf)


def rest_kernel(ready, me_ref, at_ref, ids_ref, table_ref, w_ref, *refs):
    *outs, ids_t = refs
    size = outs[0].shape[0]
    table = table_ref[...]
    kv = jnp.concatenate([dot_nt(table, w_ref[1]), dot_nt(table, w_ref[2])], axis=1).astype(bf)
    ids_t[...] = ids_ref[...].astype(f32).T
    ids = ids_t[ids_t.shape[0] - size :, :]
    part = lax.broadcasted_iota(jnp.int32, ids.shape, 1)
    for step, out in enumerate(outs):
        picked = jnp.sum(jnp.where(part == me_ref[0] ^ step, ids, 0.0), axis=1, keepdims=True)
        picked = picked.astype(jnp.int32)
        rows = dot(one_hot(picked, table.shape[0]), kv)
        out[...] = mark(rows, picked, at_ref, step).astype(bf)


def pick_kernel(half, ready, me_ref, far_ref, out_ref):
    size = out_ref.shape[0]
    start = (1 - lax.div(me_ref[0], half)) * size
    out_ref[...] = far_ref[pl.ds(pl.multiple_of(start, size), size), :]


def raw_kernel(half, whose, ready, me_ref, who_ref, w_ref, *refs):
    *blocks, out = refs
    cols = w_ref.shape[1]
    share = blocks[0].shape[0] // (2 * half)
    fetch = share * len(blocks)
    for step, block in zip(whose, blocks):
        spans = [slice(i * share, (i + 1) * share) for i in range(2 * half)]
        left = jnp.concatenate([block[span, :].astype(f32) for span in spans[::2]], axis=0)
        right = jnp.concatenate([block[span, :].astype(f32) for span in spans[1::2]], axis=0)
        marked = left[:, 0:1] != left[:, 0:1]
        code = left[:, 1:2]
        clean = jnp.concatenate([left, right], axis=1)
        clean = jnp.where(marked, 0.0, clean).astype(bf)
        kv = jnp.concatenate([dot_nt(clean, w_ref[1]), dot_nt(clean, w_ref[2])], axis=1)
        lead = lax.broadcasted_iota(jnp.int32, kv.shape, 1) == 0
        kv = jnp.where(marked, jnp.where(lead, jnp.nan, code), kv).astype(out.dtype)
        for part in range(half):
            at = pl.multiple_of(part * fetch + (who_ref[0] ^ step) * share, share)
            out[pl.ds(at, share), :] = kv[part * share : (part + 1) * share]


def mask_kernel(ready, slots_ref, mask_ref):
    all_slots = slots_ref[...].astype(f32).T.astype(jnp.int32)
    for tile in range(all_slots.shape[0] // TILE):
        slots = all_slots[tile * TILE : (tile + 1) * TILE, :]
        lanes = lax.broadcasted_iota(jnp.int32, (TILE, TPR * TILE), 1)
        edges = lanes == lax.broadcasted_iota(jnp.int32, (TILE, TPR * TILE), 0)
        for edge in range(DEG):
            edges = edges | (lanes == slots[:, edge : edge + 1])
        mask_ref[tile * TILE : (tile + 1) * TILE, :] = jnp.where(edges, 1.0, 0.0).astype(bf)


def attn_kernel(ready, who_ref, titles_ref, w_in_ref, w_out_ref, *refs):
    outs, total = refs[:-1], refs[-1]
    titles = titles_ref[...]
    q = dot_nt(titles, w_in_ref[0]).astype(bf)
    k = dot_nt(titles, w_in_ref[1]).astype(bf)
    v = dot_nt(titles, w_in_ref[2]).astype(bf)
    cols = q.shape[1]
    heads = cols // HD
    lanes = lax.broadcasted_iota(jnp.int32, (SEQ, cols), 1) // HD
    for title in range(titles.shape[0] // SEQ):
        rows = slice(title * SEQ, (title + 1) * SEQ)
        qt, kt, vt = q[rows], k[rows], v[rows]
        stacked = jnp.concatenate(
            [jnp.where(lanes == h, qt, jnp.zeros_like(qt)) for h in range(heads)], axis=0
        )
        scores = dot_nt(stacked, kt) * (1.0 / HD**0.5)
        expo = jnp.exp(scores - jnp.max(scores, axis=-1, keepdims=True))
        probs = (expo / jnp.sum(expo, axis=-1, keepdims=True)).astype(bf)
        mixed = dot(probs, vt)
        context = mixed[:SEQ]
        for h in range(1, heads):
            context = jnp.where(lanes == h, mixed[h * SEQ : (h + 1) * SEQ], context)
        total[rows, :] = dot(context.astype(bf), w_out_ref[...])
    chunk = (outs[0].shape[0] - PAD) // 2
    firsts = first_rows(total)
    for out, pair in zip(outs, ((0, 2), (1, 3))):
        for j, step in enumerate(pair):
            at = pl.ds(pl.multiple_of((who_ref[0] ^ step) * chunk, chunk), chunk)
            out[j * chunk : (j + 1) * chunk, :] = total[at, :].astype(out.dtype)
        out[2 * chunk :, :] = firsts.astype(out.dtype)


def half_kernel(chunk, ready, kept_ref, came_ref, keep_ref, give_ref):
    total = kept_ref[...] + came_ref[...].astype(f32)
    keep_ref[:chunk, :] = total[:chunk]
    give_ref[:chunk, :] = total[chunk : 2 * chunk].astype(bf)
    if keep_ref.shape[0] > chunk:
        keep_ref[chunk:, :] = total[2 * chunk :]
        give_ref[chunk:, :] = total[2 * chunk :].astype(bf)


def first_rows(ref):
    sub = lax.broadcasted_iota(jnp.int32, (PAD, ref.shape[1]), 0)
    rows = jnp.zeros((PAD, ref.shape[1]), f32)
    for title in range(ref.shape[0] // SEQ):
        row = ref[title * SEQ : title * SEQ + 1, :].astype(f32)
        rows = jnp.where(sub == title, row, rows)
    return rows


def norm_one_kernel(
    ready, who_ref, titles_ref, gains_ref, w_in_ref, w_out_ref, own_ref, *refs
):
    *parts, out, first_hidden, first_terms = refs
    chunk = own_ref.shape[0] - PAD
    total = own_ref[...]
    for part in parts:
        total = total + part[...].astype(f32)
    at = pl.ds(pl.multiple_of(who_ref[0] * chunk, chunk), chunk)
    base = jnp.concatenate([titles_ref[at, :].astype(f32), first_rows(titles_ref)], axis=0)
    hidden = layer_norm(base + total, gains_ref[0:1, :]).astype(bf)
    out[:chunk, :] = hidden[:chunk]
    firsts = hidden[chunk:]
    first_hidden[...] = firsts
    terms = dot(gelu(dot(firsts, w_in_ref[...])).astype(bf), w_out_ref[...])
    first_terms[...] = terms
    out[chunk:, :] = terms.astype(bf)


def gelu(x):
    return 0.5 * x * (1.0 + lax.erf(x * (0.5**0.5)))


def ffn_kernel(ready, w_in_ref, w_out_ref, gains_ref, first_hidden, first_terms, *refs):
    *ins, kept, sent, first = refs
    chunk = kept.shape[0] // 2
    hidden = jnp.concatenate([ref[:chunk, :] for ref in ins], axis=0)
    inner = gelu(dot(hidden, w_in_ref[...])).astype(bf)
    total = dot(inner, w_out_ref[...])
    kept[...] = total[: 2 * chunk]
    sent[...] = total[2 * chunk :].astype(bf)
    terms = first_terms[...]
    for ref in ins[1:]:
        terms = terms + ref[chunk:, :].astype(f32)
    done = layer_norm(first_hidden[...].astype(f32) + terms, gains_ref[1:2, :])
    first[...] = done[: first.shape[0]].astype(bf)


def norm_two_kernel(ready, hidden_ref, gains_ref, own_ref, *refs):
    *parts, out = refs
    total = own_ref[...]
    for part in parts:
        total = total + part[...].astype(f32)
    hidden = hidden_ref[: out.shape[0], :].astype(f32)
    out[...] = layer_norm(hidden + total, gains_ref[1:2, :]).astype(bf)


def pack_kernel(ready, *refs):
    *parts, out = refs
    per_part = parts[0].shape[0]
    sub = lax.broadcasted_iota(jnp.int32, out.shape, 0)
    rows = jnp.zeros(out.shape, f32)
    for turn, ref in enumerate(parts):
        for title in range(per_part):
            row = ref[title : title + 1, :].astype(f32)
            rows = jnp.where(sub == turn * per_part + title, row, rows)
    out[...] = rows.astype(bf)


def own_kernel(
    ready, who_ref, at_ref, table_ref, w_ref, first_ref, *refs
):
    *packs, kv_ref, q_ref, first_kv_ref, features, firsts = refs
    members = len(packs)
    per_part, width = first_ref.shape
    cols = w_ref.shape[1]
    for step, ref in enumerate(packs):
        rows = ref[...].astype(f32)
        for turn in range(firsts.shape[0] // per_part // members):
            for title in range(per_part):
                place = (turn * members + (who_ref[0] ^ step)) * per_part + title
                at = turn * per_part + title
                firsts[pl.ds(place, 1), :] = rows[at : at + 1]
    firsts[0:per_part, :] = first_ref[...].astype(f32)
    for tile in range(features.shape[0] // TILE):
        span = slice(tile * TILE, (tile + 1) * TILE)
        rows = table_ref[span, :].astype(f32)
        sub = lax.broadcasted_iota(jnp.int32, (TILE, width), 0) + tile * TILE
        for title in range(per_part):
            rows = jnp.where(sub == at_ref[title], firsts[title : title + 1, :], rows)
        features[span, :] = rows.astype(bf)
    first = firsts[...].astype(bf)
    table = features[...]
    for j in (1, 2):
        span = slice((j - 1) * cols, j * cols)
        first_kv_ref[:, span] = dot_nt(first, w_ref[j]).astype(bf)
        kv_ref[:, span] = dot_nt(table, w_ref[j]).astype(bf)
    q_ref[...] = dot_nt(table, w_ref[0]).astype(bf)


def tail_rows(count):
    return -(-count // PAD) * PAD


def graph_kernel(
    whose, ready, me_ref, who_ref, cols_ref, q_ref, kv_ref, first_ref, mask_ref, far_ref, cross_ref, *refs
):
    *rest, out_ref, encoded_ref, k_all, v_all = refs
    dones, rest = rest[: len(whose)], rest[len(whose) :]
    chunk = dones[0].shape[0]
    for step, ref in zip(whose, dones):
        at = pl.multiple_of((who_ref[0] ^ step) * chunk, chunk)
        encoded_ref[pl.ds(at, chunk), :] = ref[...]
    nodes, cols = q_ref.shape
    row_tiles = nodes // TILE
    first_kv = first_ref[...]
    k_all[:nodes, :] = kv_ref[:, :cols]
    v_all[:nodes, :] = kv_ref[:, cols:]

    def fix(rows, start):
        count = rows.shape[0]
        rows = rows.astype(f32)
        lanes = lax.broadcasted_iota(jnp.int32, (count, first_kv.shape[0]), 1).astype(f32)
        code = jnp.where(rows[:, 0:1] != rows[:, 0:1], rows[:, 1:2], -1.0)
        hot = jnp.where(lanes == code, 1.0, 0.0).astype(bf)
        fixed = jnp.where(code >= 0.0, dot(hot, first_kv), rows).astype(bf)
        at = pl.ds(pl.multiple_of(start, count), count)
        k_all[at, :] = fixed[:, :cols]
        v_all[at, :] = fixed[:, cols:]

    half = len(rest)
    size = rest[0].shape[0]
    side, low = lax.div(me_ref[0], half), lax.rem(me_ref[0], half)
    for start in range(0, cross_ref.shape[0], TILE):
        fix(cross_ref[start : start + TILE, :], nodes + (1 - side) * cross_ref.shape[0] + start)
    for part in range(half):
        at = pl.ds(pl.multiple_of((side * half + part) * size, size), size)
        fix(far_ref[at, :], nodes + (side * half + part) * 2 * size)
    for step, ref in enumerate(rest):
        fix(ref[...], nodes + (side * half + (low ^ step)) * 2 * size + size)

    heads = cols // GHD
    head_of = lax.broadcasted_iota(jnp.int32, (TILE, cols), 1) // GHD
    for tile in range(row_tiles):
        q = q_ref[tile * TILE : (tile + 1) * TILE, :]
        stacked = jnp.concatenate(
            [jnp.where(head_of == h, q, jnp.zeros_like(q)) for h in range(heads)], axis=0
        )
        starts = [pl.multiple_of(cols_ref[tile, c] * TILE, TILE) for c in range(TPR)]
        keys = jnp.concatenate([k_all[pl.ds(start, TILE), :] for start in starts], axis=0)
        values = jnp.concatenate([v_all[pl.ds(start, TILE), :] for start in starts], axis=0)
        scores = dot_nt(stacked, keys) * (1.0 / GHD**0.5)
        mask = mask_ref[tile * TILE : (tile + 1) * TILE, :].astype(f32)
        mask = jnp.concatenate([mask] * heads, axis=0) > 0.5
        masked = jnp.where(mask, scores, -jnp.inf)
        expo = jnp.exp(masked - jnp.max(masked, axis=-1, keepdims=True))
        scale = 1.0 / jnp.sum(expo, axis=-1, keepdims=True)
        mixed = dot(expo.astype(bf), values) * scale
        out = mixed[:TILE]
        for h in range(1, heads):
            out = jnp.where(head_of == h, mixed[h * TILE : (h + 1) * TILE], out)
        out_ref[:, tile * TILE : (tile + 1) * TILE] = out.T.astype(bf)


def local(

    titles,
    w_attn_in,
    w_attn_out,
    w_ffn_in,
    w_ffn_out,
    gains,
    node_table,
    w_graph,
    title_nodes,
    send_ids,
    tile_cols,
    nbr_slots,
):
    tok_rows, width = titles.shape
    nodes = node_table.shape[0]
    cols = w_graph.shape[2]
    mp = lax.axis_size("mp")
    dp = lax.axis_size("dp")
    half = dp // 2
    me_mp = lax.axis_index("mp").astype(jnp.int32)
    me_dp = lax.axis_index("dp").astype(jnp.int32)
    me, who = me_dp.reshape(1), me_mp.reshape(1)
    chunk = tok_rows // mp
    per_part = title_nodes.shape[0]
    fetch = send_ids.shape[2]
    share = fetch // mp

    def swap(value, step, axis="mp"):
        return lax.ppermute(value, axis, [(i, i ^ step) for i in range(lax.axis_size(axis))])

    def gather(value):
        whose, blocks, step = [0], [value], mp // 2
        while step:
            blocks = blocks + [swap(block, step) for block in blocks]
            whose = whose + [other ^ step for other in whose]
            step //= 2
        return whose, blocks

    def halves(kept, came, pad):
        dims = (chunk + pad, width)
        return call(
            functools.partial(half_kernel, chunk),
            (shape(dims, f32), shape(dims, bf)),
            (kept, came),
            name="half",
        )

    w_attn_in = jnp.swapaxes(w_attn_in, 1, 2)
    w_graph = jnp.swapaxes(w_graph, 1, 2)
    size = 2 * share
    sent = call(
        send_kernel,
        shape((dp * size, 2 * cols), bf),
        (me, who, title_nodes, send_ids[0], node_table, w_graph),
        smem=(0, 1),
        hbm=(4, 3, 5, 2),
        scalars=(2,),
        scratch=[pltpu.VMEM((fetch, dp), f32)],
        flops=3 * 10**9,
        name="send",
    )
    far = lax.all_to_all(
        sent.reshape(dp, size, 2 * cols), "dp", split_axis=0, concat_axis=0, tiled=True
    ).reshape(dp * size, 2 * cols)
    titles, _ = lax.optimization_barrier((titles, sent))

    kept, given = call(
        attn_kernel,
        (shape((2 * chunk + PAD, width), f32), shape((2 * chunk + PAD, width), bf)),
        (who, titles, w_attn_in, w_attn_out),
        smem=(0,),
        scratch=[pltpu.VMEM((tok_rows, width), f32)],
        flops=2 * tok_rows * width * 4 * w_attn_in.shape[1],
        name="attn",
    )
    rest = call(
        rest_kernel,
        (shape((size, 2 * cols), bf),) * half,
        (me, title_nodes, send_ids[0], node_table, w_graph),
        smem=(0, 1),
        scratch=[pltpu.VMEM((fetch, dp), f32)],
        flops=2 * 10**9,
        name="rest",
    )
    recv, rest = lax.optimization_barrier((swap(given, 1), rest))
    keep, give = halves(kept, recv, PAD)
    part = swap(give, 2)
    mask = call(
        mask_kernel, shape((nodes, TPR * TILE), bf), (nbr_slots.T,), flops=4 * 10**9, name="mask"
    )
    part, mask = lax.optimization_barrier((part, mask))
    hidden, first_hidden, first_terms = call(
        norm_one_kernel,
        (shape((chunk + PAD, width), bf), shape((PAD, width), bf), shape((PAD, width), f32)),
        (who, titles, gains, w_ffn_in, w_ffn_out, keep, part),
        smem=(0,),
        name="norm_one",
    )
    whose, hiddens = gather(hidden)
    raw = call(
        functools.partial(pick_kernel, half),
        shape((half * size, 2 * cols), bf),
        (me, far),
        smem=(0,),
        name="pick",
    )
    rest = [rest[0]] + [swap(rest[step], step, "dp") for step in range(1, half)]
    hiddens, raw, rest = lax.optimization_barrier((hiddens, raw, rest))
    across = swap(raw, 2)
    kept, given, first = call(
        ffn_kernel,
        (
            shape((2 * chunk, width), f32),
            shape((2 * chunk, width), bf),
            shape((per_part, width), bf),
        ),
        (w_ffn_in, w_ffn_out, gains, first_hidden, first_terms, *hiddens),
        flops=4 * tok_rows * width * w_ffn_in.shape[1],
        name="ffn",
    )
    turns = dp // mp
    firsts = [
        lax.ppermute(
            first,
            ("dp", "mp"),
            [
                (p * mp + m, (p ^ (turn * mp + m)) * mp + m)
                for p in range(dp)
                for m in range(mp)
                if turn or m
            ],
        )
        for turn in range(turns)
    ]
    keep, give = halves(kept, swap(given, 1), 0)
    part = swap(give, 2)
    part, firsts, across = lax.optimization_barrier((part, firsts, across))
    blocks = [raw, across, swap(raw, 1), swap(across, 1)]
    done = call(
        norm_two_kernel, shape((chunk, width), bf), (hidden, gains, keep, part), name="norm_two"
    )
    pack = call(pack_kernel, shape((tail_rows(turns * per_part), width), bf), firsts, name="pack")
    packs = [pack] + [swap(pack, step) for step in range(1, mp)]
    _, dones = gather(done)
    cross = call(
        functools.partial(raw_kernel, half, whose),
        shape((half * fetch, 2 * cols), bf if share % 16 == 0 else f32),
        (me, who, w_graph, *blocks),
        smem=(0, 1),
        flops=2 * 10**9,
        name="raw",
    )
    kv, q, first_kv = call(
        own_kernel,
        (shape((nodes, 2 * cols), bf), shape((nodes, cols), bf), shape((dp * per_part, 2 * cols), bf)),
        (who, title_nodes, node_table, w_graph, first, *packs),
        smem=(0, 1),
        scratch=[pltpu.VMEM((nodes, width), bf), pltpu.VMEM((dp * per_part, width), f32)],
        flops=2 * 10**9,
        name="own",
    )
    keys = nodes + dp * fetch
    graph_out, encoded = call(
        functools.partial(graph_kernel, whose),
        (shape((cols, nodes), bf), shape((tok_rows, width), bf)),
        (me, who, tile_cols, q, kv, first_kv, mask, far, cross, *dones, *rest),
        smem=(0, 1, 2),
        scratch=[pltpu.VMEM((keys, cols), bf), pltpu.VMEM((keys, cols), bf)],
        flops=4 * 10**9,
        name="graph",
    )
    return (encoded, graph_out.T)


def solution(mesh):
    in_specs = (
        P("dp", None),
        P(None, None, "mp"),
        P("mp", None),
        P(None, "mp"),
        P("mp", None),
        P(),
        P("dp", None),
        P(None, None, "mp"),
        P("dp"),
        P("dp", None, None),
        P("dp", None),
        P("dp", None),
    )
    out_specs = (P("dp", None), P("dp", "mp"))
    return jax.shard_map(
        local, mesh=mesh, in_specs=in_specs, out_specs=out_specs, check_vma=False
    )
```

```python
import functools
import jax
import jax.numpy as jnp
from jax import lax
from jax.experimental import pallas as pl
from jax.experimental.pallas import tpu as pltpu
from jax.sharding import PartitionSpec as P

SEQ = 128
TILE = 128
DEG = 16
TPR = 6
HD = 64
GHD = 96

eps_norm = 1e-06
bf = jnp.bfloat16
f32 = jnp.float32

VMEM = pl.BlockSpec(memory_space=pltpu.VMEM)
SMEM = pl.BlockSpec(memory_space=pltpu.SMEM)
HBM = pl.BlockSpec(memory_space=pltpu.HBM)
PAD = 16
NT = (((1,), (1,)), ((), ()))
TN = (((0,), (0,)), ((), ()))


def call(
    kernel,
    outs,
    args,
    smem=(),
    hbm=(),
    scalars=(),
    scratch=(),
    out_specs=None,
    flops=0,
    name=None,
):
    count, out_count, own = len(args), len(jax.tree.leaves(outs)), len(scratch)
    specs = [SMEM if i in smem else HBM if i in hbm else VMEM for i in range(count)]
    nbytes = sum(a.size * a.dtype.itemsize for a in args)
    space = [pltpu.SMEM if i in scalars else pltpu.VMEM for i in hbm]
    buffers = [kind(args[i].shape, args[i].dtype) for kind, i in zip(space, hbm)]
    sems = [pltpu.SemaphoreType.DMA((len(hbm),))] if hbm else []

    def body(*refs):
        ins, rest = list(refs[:count]), refs[count:]
        kept, moved = rest[: out_count + own], rest[out_count + own :]
        moves = {}
        for j, i in enumerate(hbm):
            moves[i] = pltpu.make_async_copy(ins[i], moved[j], moved[-1].at[j])
            moves[i].start()
            ins[i] = moved[j]

        def ready(*wanted):
            for i in wanted:
                moves[i].wait()

        kernel(ready, *ins, *kept)

    return pl.pallas_call(
        body,
        out_shape=outs,
        in_specs=specs,
        out_specs=jax.tree.map(lambda _: VMEM, outs) if out_specs is None else out_specs,
        scratch_shapes=list(scratch) + buffers + sems,
        compiler_params=pltpu.CompilerParams(vmem_limit_bytes=(60 if hbm else 40) * 1024 * 1024),
        cost_estimate=pl.CostEstimate(flops=flops, bytes_accessed=nbytes, transcendentals=0),
        name=name,
    )(*args)


def shape(dims, dtype):
    return jax.ShapeDtypeStruct(dims, dtype)


def dot(a, b):
    return jnp.dot(a, b, preferred_element_type=f32)


def dot_nt(a, b):
    return lax.dot_general(a, b, NT, preferred_element_type=f32)


def dot_tn(a, b):
    return lax.dot_general(a, b, TN, preferred_element_type=f32)


def layer_norm(values, gain):
    mean = jnp.mean(values, axis=-1, keepdims=True)
    centred = values - mean
    var = jnp.mean(centred * centred, axis=-1, keepdims=True)
    return centred * lax.rsqrt(var + eps_norm) * gain


def one_hot(picked, nodes):
    lanes = lax.broadcasted_iota(jnp.int32, (picked.shape[0], nodes), 1)
    return jnp.where(lanes == picked, 1.0, 0.0).astype(bf)


def mark(rows, picked, at_ref, step):
    per_part = at_ref.shape[0]
    code = jnp.full(picked.shape, -1, jnp.int32)
    for title in range(per_part):
        code = jnp.where(picked == at_ref[title], step * per_part + title, code)
    lead = lax.broadcasted_iota(jnp.int32, rows.shape, 1) == 0
    return jnp.where(code >= 0, jnp.where(lead, jnp.nan, code.astype(f32)), rows)


def send_kernel(ready, me_ref, at_ref, ids_ref, table_ref, w_ref, sent_ref, rows_ref, sems):
    cols = w_ref.shape[1]
    fetch, nodes = ids_ref.shape[1], table_ref.shape[0]
    ready(2)
    ids = ids_ref[...].astype(f32).T.astype(jnp.int32)
    ready(1, 3, 4)
    table = table_ref[...]
    kv = jnp.concatenate([dot_nt(table, w_ref[1]), dot_nt(table, w_ref[2])], axis=1).astype(bf)
    moves = []
    for part in range(ids.shape[1]):
        picked = ids[:, part : part + 1]
        rows = mark(dot(one_hot(picked, nodes), kv), picked, at_ref, me_ref[0] ^ part)
        at = pl.ds(part * fetch, fetch)
        rows_ref[at, :] = rows.astype(bf)
        moves.append(pltpu.make_async_copy(rows_ref.at[at, :], sent_ref.at[at, :], sems.at[part]))
        moves[-1].start()
    for move in moves:
        move.wait()


def mask_kernel(ready, slots_ref, mask_ref):
    all_slots = slots_ref[...].astype(f32).T.astype(jnp.int32)
    for tile in range(all_slots.shape[0] // TILE):
        slots = all_slots[tile * TILE : (tile + 1) * TILE, :]
        lanes = lax.broadcasted_iota(jnp.int32, (TILE, TPR * TILE), 1)
        edges = lanes == lax.broadcasted_iota(jnp.int32, (TILE, TPR * TILE), 0)
        for edge in range(DEG):
            edges = edges | (lanes == slots[:, edge : edge + 1])
        mask_ref[tile * TILE : (tile + 1) * TILE, :] = jnp.where(edges, 1.0, 0.0).astype(bf)


def attn_kernel(ready, who_ref, titles_ref, w_in_ref, w_out_ref, *refs):
    outs, total = refs[:-1], refs[-1]
    titles = titles_ref[...]
    q = dot_nt(titles, w_in_ref[0]).astype(bf)
    k = dot_nt(titles, w_in_ref[1]).astype(bf)
    v = dot_nt(titles, w_in_ref[2]).astype(bf)
    cols = q.shape[1]
    heads = cols // HD
    lanes = lax.broadcasted_iota(jnp.int32, (SEQ, cols), 1) // HD
    for title in range(titles.shape[0] // SEQ):
        rows = slice(title * SEQ, (title + 1) * SEQ)
        qt, kt, vt = q[rows], k[rows], v[rows]
        stacked = jnp.concatenate(
            [jnp.where(lanes == h, qt, jnp.zeros_like(qt)) for h in range(heads)], axis=0
        )
        scores = dot_nt(stacked, kt) * (1.0 / HD**0.5)
        expo = jnp.exp(scores - jnp.max(scores, axis=-1, keepdims=True))
        probs = (expo / jnp.sum(expo, axis=-1, keepdims=True)).astype(bf)
        mixed = dot(probs, vt)
        context = mixed[:SEQ]
        for h in range(1, heads):
            context = jnp.where(lanes == h, mixed[h * SEQ : (h + 1) * SEQ], context)
        total[rows, :] = dot(context.astype(bf), w_out_ref[...])
    chunk = (outs[0].shape[0] - PAD) // 2
    firsts = first_rows(total)
    for out, pair in zip(outs, ((0, 2), (1, 3))):
        for j, step in enumerate(pair):
            at = pl.ds(pl.multiple_of((who_ref[0] ^ step) * chunk, chunk), chunk)
            out[j * chunk : (j + 1) * chunk, :] = total[at, :].astype(out.dtype)
        out[2 * chunk :, :] = firsts.astype(out.dtype)


def half_kernel(chunk, ready, kept_ref, came_ref, keep_ref, give_ref):
    total = kept_ref[...] + came_ref[...].astype(f32)
    keep_ref[:chunk, :] = total[:chunk]
    give_ref[:chunk, :] = total[chunk : 2 * chunk].astype(bf)
    if keep_ref.shape[0] > chunk:
        keep_ref[chunk:, :] = total[2 * chunk :]
        give_ref[chunk:, :] = total[2 * chunk :].astype(bf)


def first_rows(ref):
    sub = lax.broadcasted_iota(jnp.int32, (PAD, ref.shape[1]), 0)
    rows = jnp.zeros((PAD, ref.shape[1]), f32)
    for title in range(ref.shape[0] // SEQ):
        row = ref[title * SEQ : title * SEQ + 1, :].astype(f32)
        rows = jnp.where(sub == title, row, rows)
    return rows


def norm_one_kernel(
    ready, who_ref, titles_ref, gains_ref, w_in_ref, w_out_ref, own_ref, *refs
):
    *parts, out, first_hidden, first_terms = refs
    chunk = own_ref.shape[0] - PAD
    total = own_ref[...]
    for part in parts:
        total = total + part[...].astype(f32)
    at = pl.ds(pl.multiple_of(who_ref[0] * chunk, chunk), chunk)
    base = jnp.concatenate([titles_ref[at, :].astype(f32), first_rows(titles_ref)], axis=0)
    hidden = layer_norm(base + total, gains_ref[0:1, :]).astype(bf)
    out[:chunk, :] = hidden[:chunk]
    firsts = hidden[chunk:]
    first_hidden[...] = firsts
    terms = dot(gelu(dot(firsts, w_in_ref[...])).astype(bf), w_out_ref[...])
    first_terms[...] = terms
    out[chunk:, :] = terms.astype(bf)


def gelu(x):
    return 0.5 * x * (1.0 + lax.erf(x * (0.5**0.5)))


def ffn_kernel(ready, w_in_ref, w_out_ref, gains_ref, first_hidden, first_terms, *refs):
    *ins, kept, sent, first = refs
    chunk = kept.shape[0] // 2
    hidden = jnp.concatenate([ref[:chunk, :] for ref in ins], axis=0)
    inner = gelu(dot(hidden, w_in_ref[...])).astype(bf)
    total = dot(inner, w_out_ref[...])
    kept[...] = total[: 2 * chunk]
    sent[...] = total[2 * chunk :].astype(bf)
    terms = first_terms[...]
    for ref in ins[1:]:
        terms = terms + ref[chunk:, :].astype(f32)
    done = layer_norm(first_hidden[...].astype(f32) + terms, gains_ref[1:2, :])
    first[...] = done[: first.shape[0]].astype(bf)


def norm_two_kernel(ready, hidden_ref, gains_ref, own_ref, *refs):
    *parts, out = refs
    total = own_ref[...]
    for part in parts:
        total = total + part[...].astype(f32)
    hidden = hidden_ref[: out.shape[0], :].astype(f32)
    out[...] = layer_norm(hidden + total, gains_ref[1:2, :]).astype(bf)


def pack_kernel(ready, *refs):
    *parts, out = refs
    per_part = parts[0].shape[0]
    sub = lax.broadcasted_iota(jnp.int32, out.shape, 0)
    rows = jnp.zeros(out.shape, f32)
    for turn, ref in enumerate(parts):
        for title in range(per_part):
            row = ref[title : title + 1, :].astype(f32)
            rows = jnp.where(sub == turn * per_part + title, row, rows)
    out[...] = rows.astype(bf)


def own_kernel(ready, table_ref, w_ref, kv_ref, q_ref):
    cols = w_ref.shape[1]
    table = table_ref[...]
    kv_ref[:, :cols] = dot_nt(table, w_ref[1]).astype(bf)
    kv_ref[:, cols:] = dot_nt(table, w_ref[2]).astype(bf)
    q_ref[...] = dot_nt(table, w_ref[0]).astype(bf)


def tail_rows(count):
    return -(-count // PAD) * PAD


def graph_kernel(
    whose, ready, who_ref, cols_ref, at_ref, q_ref, kv_ref, w_ref, mask_ref, far_ref, first_ref, *refs
):
    *packs, out_ref, encoded_ref, k_all, v_all, firsts = refs
    dones, packs = packs[: len(whose)], packs[len(whose) :]
    chunk = dones[0].shape[0]
    for step, ref in zip(whose, dones):
        at = pl.multiple_of((who_ref[0] ^ step) * chunk, chunk)
        encoded_ref[pl.ds(at, chunk), :] = ref[...]
    nodes, cols = q_ref.shape
    row_tiles = nodes // TILE
    per_part = first_ref.shape[0]
    members = len(packs)
    for step, ref in enumerate(packs):
        rows = ref[...].astype(f32)
        for turn in range(firsts.shape[0] // per_part // members):
            for title in range(per_part):
                place = (turn * members + (who_ref[0] ^ step)) * per_part + title
                at = turn * per_part + title
                firsts[pl.ds(place, 1), :] = rows[at : at + 1]
    firsts[0:per_part, :] = first_ref[...].astype(f32)
    first = firsts[...].astype(bf)
    first_kv = jnp.concatenate([dot_nt(first, w_ref[1]), dot_nt(first, w_ref[2])], axis=1).astype(bf)
    first_q = dot_nt(first, w_ref[0])
    for tile in range(row_tiles):
        span = slice(tile * TILE, (tile + 1) * TILE)
        rows = kv_ref[span, :].astype(f32)
        sub = lax.broadcasted_iota(jnp.int32, (TILE, 2 * cols), 0) + tile * TILE
        for title in range(per_part):
            row = first_kv[title : title + 1].astype(f32)
            rows = jnp.where(sub == at_ref[title], row, rows)
        rows = rows.astype(bf)
        k_all[span, :] = rows[:, :cols]
        v_all[span, :] = rows[:, cols:]
    lanes = lax.broadcasted_iota(jnp.int32, (TILE, first_kv.shape[0]), 1).astype(f32)
    for tile in range(far_ref.shape[0] // TILE):
        rows = far_ref[tile * TILE : (tile + 1) * TILE, :].astype(f32)
        code = jnp.where(rows[:, 0:1] != rows[:, 0:1], rows[:, 1:2], -1.0)
        hot = jnp.where(lanes == code, 1.0, 0.0).astype(bf)
        fixed = jnp.where(code >= 0.0, dot(hot, first_kv), rows).astype(bf)
        span = slice(nodes + tile * TILE, nodes + (tile + 1) * TILE)
        k_all[span, :] = fixed[:, :cols]
        v_all[span, :] = fixed[:, cols:]

    heads = cols // GHD
    head_of = lax.broadcasted_iota(jnp.int32, (TILE, cols), 1) // GHD
    for tile in range(row_tiles):
        q = q_ref[tile * TILE : (tile + 1) * TILE, :].astype(f32)
        sub = lax.broadcasted_iota(jnp.int32, (TILE, cols), 0) + tile * TILE
        for title in range(per_part):
            q = jnp.where(sub == at_ref[title], first_q[title : title + 1], q)
        q = q.astype(bf)
        stacked = jnp.concatenate(
            [jnp.where(head_of == h, q, jnp.zeros_like(q)) for h in range(heads)], axis=0
        )
        starts = [pl.multiple_of(cols_ref[tile, c] * TILE, TILE) for c in range(TPR)]
        keys = jnp.concatenate([k_all[pl.ds(start, TILE), :] for start in starts], axis=0)
        values = jnp.concatenate([v_all[pl.ds(start, TILE), :] for start in starts], axis=0)
        scores = dot_nt(stacked, keys) * (1.0 / GHD**0.5)
        mask = mask_ref[tile * TILE : (tile + 1) * TILE, :].astype(f32)
        mask = jnp.concatenate([mask] * heads, axis=0) > 0.5
        masked = jnp.where(mask, scores, -jnp.inf)
        expo = jnp.exp(masked - jnp.max(masked, axis=-1, keepdims=True))
        scale = 1.0 / jnp.sum(expo, axis=-1, keepdims=True)
        mixed = dot(expo.astype(bf), values) * scale
        out = mixed[:TILE]
        for h in range(1, heads):
            out = jnp.where(head_of == h, mixed[h * TILE : (h + 1) * TILE], out)
        out_ref[:, tile * TILE : (tile + 1) * TILE] = out.T.astype(bf)


def local(

    titles,
    w_attn_in,
    w_attn_out,
    w_ffn_in,
    w_ffn_out,
    gains,
    node_table,
    w_graph,
    title_nodes,
    send_ids,
    tile_cols,
    nbr_slots,
):
    tok_rows, width = titles.shape
    nodes = node_table.shape[0]
    cols = w_graph.shape[2]
    mp = lax.axis_size("mp")
    dp = lax.axis_size("dp")
    me_mp = lax.axis_index("mp").astype(jnp.int32)
    me_dp = lax.axis_index("dp").astype(jnp.int32)
    me, who = me_dp.reshape(1), me_mp.reshape(1)
    chunk = tok_rows // mp
    per_part = title_nodes.shape[0]
    fetch = send_ids.shape[2]

    def swap(value, step, axis="mp"):
        return lax.ppermute(value, axis, [(i, i ^ step) for i in range(lax.axis_size(axis))])

    def gather(value):
        whose, blocks, step = [0], [value], mp // 2
        while step:
            blocks = blocks + [swap(block, step) for block in blocks]
            whose = whose + [other ^ step for other in whose]
            step //= 2
        return whose, blocks

    def halves(kept, came, pad):
        dims = (chunk + pad, width)
        return call(
            functools.partial(half_kernel, chunk),
            (shape(dims, f32), shape(dims, bf)),
            (kept, came),
            name="half",
        )

    w_attn_in = jnp.swapaxes(w_attn_in, 1, 2)
    w_graph = jnp.swapaxes(w_graph, 1, 2)
    sent = call(
        send_kernel,
        shape((dp * fetch, 2 * cols), bf),
        (me, title_nodes, send_ids[0], node_table, w_graph),
        smem=(0,),
        hbm=(4, 3, 2, 1),
        scalars=(1,),
        out_specs=HBM,
        scratch=[pltpu.VMEM((dp * fetch, 2 * cols), bf), pltpu.SemaphoreType.DMA((dp,))],
        flops=2 * nodes * width * 2 * cols + 2 * dp * fetch * nodes * 2 * cols,
        name="send",
    )
    far = lax.all_to_all(
        sent.reshape(dp, fetch, 2 * cols), "dp", split_axis=0, concat_axis=0, tiled=True
    ).reshape(dp * fetch, 2 * cols)
    titles, _ = lax.optimization_barrier((titles, sent))

    kept, given = call(
        attn_kernel,
        (shape((2 * chunk + PAD, width), f32), shape((2 * chunk + PAD, width), bf)),
        (who, titles, w_attn_in, w_attn_out),
        smem=(0,),
        scratch=[pltpu.VMEM((tok_rows, width), f32)],
        flops=2 * tok_rows * width * 4 * w_attn_in.shape[1],
        name="attn",
    )
    keep, give = halves(kept, swap(given, 1), PAD)
    part = swap(give, 2)
    mask = call(
        mask_kernel, shape((nodes, TPR * TILE), bf), (nbr_slots.T,), flops=4 * 10**9, name="mask"
    )
    part, mask = lax.optimization_barrier((part, mask))
    hidden, first_hidden, first_terms = call(
        norm_one_kernel,
        (shape((chunk + PAD, width), bf), shape((PAD, width), bf), shape((PAD, width), f32)),
        (who, titles, gains, w_ffn_in, w_ffn_out, keep, part),
        smem=(0,),
        name="norm_one",
    )
    whose, hiddens = gather(hidden)
    kept, given, first = call(
        ffn_kernel,
        (
            shape((2 * chunk, width), f32),
            shape((2 * chunk, width), bf),
            shape((per_part, width), bf),
        ),
        (w_ffn_in, w_ffn_out, gains, first_hidden, first_terms, *hiddens),
        flops=4 * tok_rows * width * w_ffn_in.shape[1],
        name="ffn",
    )
    turns = dp // mp
    firsts = [
        lax.ppermute(
            first,
            ("dp", "mp"),
            [
                (p * mp + m, (p ^ (turn * mp + m)) * mp + m)
                for p in range(dp)
                for m in range(mp)
                if turn or m
            ],
        )
        for turn in range(turns)
    ]
    keep, give = halves(kept, swap(given, 1), 0)
    part = swap(give, 2)
    kv, q = call(
        own_kernel,
        (shape((nodes, 2 * cols), bf), shape((nodes, cols), bf)),
        (node_table, w_graph),
        flops=2 * 10**9,
        name="own",
    )
    part, firsts, kv, q = lax.optimization_barrier((part, firsts, kv, q))
    done = call(
        norm_two_kernel, shape((chunk, width), bf), (hidden, gains, keep, part), name="norm_two"
    )
    pack = call(pack_kernel, shape((tail_rows(turns * per_part), width), bf), firsts, name="pack")
    packs = [pack] + [swap(pack, step) for step in range(1, mp)]
    _, dones = gather(done)
    keys = nodes + dp * fetch
    graph_out, encoded = call(
        functools.partial(graph_kernel, whose),
        (shape((cols, nodes), bf), shape((tok_rows, width), bf)),
        (who, tile_cols, title_nodes, q, kv, w_graph, mask, far, first, *dones, *packs),
        smem=(0, 1, 2),
        scratch=[
            pltpu.VMEM((keys, cols), bf),
            pltpu.VMEM((keys, cols), bf),
            pltpu.VMEM((dp * per_part, width), f32),
        ],
        flops=4 * 10**9,
        name="graph",
    )
    return (encoded, graph_out.T)


def solution(mesh):
    in_specs = (
        P("dp", None),
        P(None, None, "mp"),
        P("mp", None),
        P(None, "mp"),
        P("mp", None),
        P(),
        P("dp", None),
        P(None, None, "mp"),
        P("dp"),
        P("dp", None, None),
        P("dp", None),
        P("dp", None),
    )
    out_specs = (P("dp", None), P("dp", "mp"))
    return jax.shard_map(
        local, mesh=mesh, in_specs=in_specs, out_specs=out_specs, check_vma=False
    )
```

```python
import functools
import jax
import jax.numpy as jnp
from jax import lax
from jax.experimental import pallas as pl
from jax.experimental.pallas import tpu as pltpu
from jax.sharding import PartitionSpec as P

SEQ = 128
TILE = 128
DEG = 16
TPR = 6
HD = 64
GHD = 96

eps_norm = 1e-06
bf = jnp.bfloat16
f32 = jnp.float32

VMEM = pl.BlockSpec(memory_space=pltpu.VMEM)
SMEM = pl.BlockSpec(memory_space=pltpu.SMEM)
HBM = pl.BlockSpec(memory_space=pltpu.HBM)
PAD = 16
NT = (((1,), (1,)), ((), ()))
TN = (((0,), (0,)), ((), ()))


def call(
    kernel,
    outs,
    args,
    smem=(),
    hbm=(),
    scalars=(),
    scratch=(),
    out_specs=None,
    flops=0,
    name=None,
):
    count, out_count, own = len(args), len(jax.tree.leaves(outs)), len(scratch)
    specs = [SMEM if i in smem else HBM if i in hbm else VMEM for i in range(count)]
    nbytes = sum(a.size * a.dtype.itemsize for a in args)
    space = [pltpu.SMEM if i in scalars else pltpu.VMEM for i in hbm]
    buffers = [kind(args[i].shape, args[i].dtype) for kind, i in zip(space, hbm)]
    sems = [pltpu.SemaphoreType.DMA((len(hbm),))] if hbm else []

    def body(*refs):
        ins, rest = list(refs[:count]), refs[count:]
        kept, moved = rest[: out_count + own], rest[out_count + own :]
        moves = {}
        for j, i in enumerate(hbm):
            moves[i] = pltpu.make_async_copy(ins[i], moved[j], moved[-1].at[j])
            moves[i].start()
            ins[i] = moved[j]

        def ready(*wanted):
            for i in wanted:
                moves[i].wait()

        kernel(ready, *ins, *kept)

    return pl.pallas_call(
        body,
        out_shape=outs,
        in_specs=specs,
        out_specs=jax.tree.map(lambda _: VMEM, outs) if out_specs is None else out_specs,
        scratch_shapes=list(scratch) + buffers + sems,
        compiler_params=pltpu.CompilerParams(vmem_limit_bytes=(60 if hbm else 40) * 1024 * 1024),
        cost_estimate=pl.CostEstimate(flops=flops, bytes_accessed=nbytes, transcendentals=0),
        name=name,
    )(*args)


def shape(dims, dtype):
    return jax.ShapeDtypeStruct(dims, dtype)


def dot(a, b):
    return jnp.dot(a, b, preferred_element_type=f32)


def dot_nt(a, b):
    return lax.dot_general(a, b, NT, preferred_element_type=f32)


def dot_tn(a, b):
    return lax.dot_general(a, b, TN, preferred_element_type=f32)


def layer_norm(values, gain):
    mean = jnp.mean(values, axis=-1, keepdims=True)
    centred = values - mean
    var = jnp.mean(centred * centred, axis=-1, keepdims=True)
    return centred * lax.rsqrt(var + eps_norm) * gain


def one_hot(picked, nodes):
    lanes = lax.broadcasted_iota(jnp.int32, (picked.shape[0], nodes), 1)
    return jnp.where(lanes == picked, 1.0, 0.0).astype(bf)


def mark(rows, picked, at_ref, step):
    per_part = at_ref.shape[0]
    code = jnp.full(picked.shape, -1, jnp.int32)
    for title in range(per_part):
        code = jnp.where(picked == at_ref[title], step * per_part + title, code)
    lead = lax.broadcasted_iota(jnp.int32, rows.shape, 1) == 0
    return jnp.where(code >= 0, jnp.where(lead, jnp.nan, code.astype(f32)), rows)


def send_kernel(ready, me_ref, at_ref, ids_ref, table_ref, w_ref, sent_ref, rows_ref, sems):
    cols = w_ref.shape[1]
    fetch, nodes = ids_ref.shape[1], table_ref.shape[0]
    ready(2)
    ids = ids_ref[...].astype(f32).T.astype(jnp.int32)
    ready(1, 3, 4)
    table = table_ref[...]
    kv = jnp.concatenate([dot_nt(table, w_ref[1]), dot_nt(table, w_ref[2])], axis=1).astype(bf)
    moves = []
    for part in range(ids.shape[1]):
        picked = ids[:, part : part + 1]
        rows = mark(dot(one_hot(picked, nodes), kv), picked, at_ref, me_ref[0] ^ part)
        at = pl.ds(part * fetch, fetch)
        rows_ref[at, :] = rows.astype(bf)
        moves.append(pltpu.make_async_copy(rows_ref.at[at, :], sent_ref.at[at, :], sems.at[part]))
        moves[-1].start()
    for move in moves:
        move.wait()


def mask_kernel(ready, slots_ref, mask_ref):
    all_slots = slots_ref[...].astype(f32).T.astype(jnp.int32)
    for tile in range(all_slots.shape[0] // TILE):
        slots = all_slots[tile * TILE : (tile + 1) * TILE, :]
        lanes = lax.broadcasted_iota(jnp.int32, (TILE, TPR * TILE), 1)
        edges = lanes == lax.broadcasted_iota(jnp.int32, (TILE, TPR * TILE), 0)
        for edge in range(DEG):
            edges = edges | (lanes == slots[:, edge : edge + 1])
        mask_ref[tile * TILE : (tile + 1) * TILE, :] = jnp.where(edges, 1.0, 0.0).astype(bf)


def attn_kernel(ready, who_ref, titles_ref, w_in_ref, w_out_ref, *refs):
    outs, total = refs[:-1], refs[-1]
    titles = titles_ref[...]
    q = dot_nt(titles, w_in_ref[0]).astype(bf)
    k = dot_nt(titles, w_in_ref[1]).astype(bf)
    v = dot_nt(titles, w_in_ref[2]).astype(bf)
    cols = q.shape[1]
    heads = cols // HD
    lanes = lax.broadcasted_iota(jnp.int32, (SEQ, cols), 1) // HD
    for title in range(titles.shape[0] // SEQ):
        rows = slice(title * SEQ, (title + 1) * SEQ)
        qt, kt, vt = q[rows], k[rows], v[rows]
        stacked = jnp.concatenate(
            [jnp.where(lanes == h, qt, jnp.zeros_like(qt)) for h in range(heads)], axis=0
        )
        scores = dot_nt(stacked, kt) * (1.0 / HD**0.5)
        expo = jnp.exp(scores - jnp.max(scores, axis=-1, keepdims=True))
        probs = (expo / jnp.sum(expo, axis=-1, keepdims=True)).astype(bf)
        mixed = dot(probs, vt)
        context = mixed[:SEQ]
        for h in range(1, heads):
            context = jnp.where(lanes == h, mixed[h * SEQ : (h + 1) * SEQ], context)
        total[rows, :] = dot(context.astype(bf), w_out_ref[...])
    chunk = (outs[0].shape[0] - PAD) // 2
    firsts = first_rows(total)
    for out, pair in zip(outs, ((0, 2), (1, 3))):
        for j, step in enumerate(pair):
            at = pl.ds(pl.multiple_of((who_ref[0] ^ step) * chunk, chunk), chunk)
            out[j * chunk : (j + 1) * chunk, :] = total[at, :].astype(out.dtype)
        out[2 * chunk :, :] = firsts.astype(out.dtype)


def half_kernel(chunk, ready, kept_ref, came_ref, keep_ref, give_ref):
    total = kept_ref[...] + came_ref[...].astype(f32)
    keep_ref[:chunk, :] = total[:chunk]
    give_ref[:chunk, :] = total[chunk : 2 * chunk].astype(bf)
    if keep_ref.shape[0] > chunk:
        keep_ref[chunk:, :] = total[2 * chunk :]
        give_ref[chunk:, :] = total[2 * chunk :].astype(bf)


def first_rows(ref):
    sub = lax.broadcasted_iota(jnp.int32, (PAD, ref.shape[1]), 0)
    rows = jnp.zeros((PAD, ref.shape[1]), f32)
    for title in range(ref.shape[0] // SEQ):
        row = ref[title * SEQ : title * SEQ + 1, :].astype(f32)
        rows = jnp.where(sub == title, row, rows)
    return rows


def norm_one_kernel(
    ready, who_ref, titles_ref, gains_ref, w_in_ref, w_out_ref, own_ref, *refs
):
    *parts, out, first_hidden, first_terms = refs
    chunk = own_ref.shape[0] - PAD
    total = own_ref[...]
    for part in parts:
        total = total + part[...].astype(f32)
    at = pl.ds(pl.multiple_of(who_ref[0] * chunk, chunk), chunk)
    base = jnp.concatenate([titles_ref[at, :].astype(f32), first_rows(titles_ref)], axis=0)
    hidden = layer_norm(base + total, gains_ref[0:1, :]).astype(bf)
    out[:chunk, :] = hidden[:chunk]
    firsts = hidden[chunk:]
    first_hidden[...] = firsts
    terms = dot(gelu(dot(firsts, w_in_ref[...])).astype(bf), w_out_ref[...])
    first_terms[...] = terms
    out[chunk:, :] = terms.astype(bf)


def gelu(x):
    return 0.5 * x * (1.0 + lax.erf(x * (0.5**0.5)))


def ffn_kernel(ready, w_in_ref, w_out_ref, gains_ref, first_hidden, first_terms, *refs):
    *ins, kept, sent, first = refs
    chunk = kept.shape[0] // 2
    hidden = jnp.concatenate([ref[:chunk, :] for ref in ins], axis=0)
    inner = gelu(dot(hidden, w_in_ref[...])).astype(bf)
    total = dot(inner, w_out_ref[...])
    kept[...] = total[: 2 * chunk]
    sent[...] = total[2 * chunk :].astype(bf)
    terms = first_terms[...]
    for ref in ins[1:]:
        terms = terms + ref[chunk:, :].astype(f32)
    done = layer_norm(first_hidden[...].astype(f32) + terms, gains_ref[1:2, :])
    first[...] = done[: first.shape[0]].astype(bf)


def norm_two_kernel(ready, hidden_ref, gains_ref, own_ref, *refs):
    *parts, out = refs
    total = own_ref[...]
    for part in parts:
        total = total + part[...].astype(f32)
    hidden = hidden_ref[: out.shape[0], :].astype(f32)
    out[...] = layer_norm(hidden + total, gains_ref[1:2, :]).astype(bf)


def pack_kernel(ready, *refs):
    *parts, out = refs
    per_part = parts[0].shape[0]
    sub = lax.broadcasted_iota(jnp.int32, out.shape, 0)
    rows = jnp.zeros(out.shape, f32)
    for turn, ref in enumerate(parts):
        for title in range(per_part):
            row = ref[title : title + 1, :].astype(f32)
            rows = jnp.where(sub == turn * per_part + title, row, rows)
    out[...] = rows.astype(bf)


def own_kernel(ready, table_ref, w_ref, kv_ref, q_ref):
    cols = w_ref.shape[1]
    table = table_ref[...]
    kv_ref[:, :cols] = dot_nt(table, w_ref[1]).astype(bf)
    kv_ref[:, cols:] = dot_nt(table, w_ref[2]).astype(bf)
    q_ref[...] = dot_nt(table, w_ref[0]).astype(bf)


def tail_rows(count):
    return -(-count // PAD) * PAD


def graph_kernel(
    whose, ready, who_ref, cols_ref, at_ref, q_ref, kv_ref, w_ref, mask_ref, far_ref, first_ref, *refs
):
    *packs, out_ref, encoded_ref, k_all, v_all, firsts = refs
    dones, packs = packs[: len(whose)], packs[len(whose) :]
    chunk = dones[0].shape[0]
    for step, ref in zip(whose, dones):
        at = pl.multiple_of((who_ref[0] ^ step) * chunk, chunk)
        encoded_ref[pl.ds(at, chunk), :] = ref[...]
    nodes, cols = q_ref.shape
    row_tiles = nodes // TILE
    per_part = first_ref.shape[0]
    members = len(packs)
    for step, ref in enumerate(packs):
        rows = ref[...].astype(f32)
        for turn in range(firsts.shape[0] // per_part // members):
            for title in range(per_part):
                place = (turn * members + (who_ref[0] ^ step)) * per_part + title
                at = turn * per_part + title
                firsts[pl.ds(place, 1), :] = rows[at : at + 1]
    firsts[0:per_part, :] = first_ref[...].astype(f32)
    first = firsts[...].astype(bf)
    first_kv = jnp.concatenate([dot_nt(first, w_ref[1]), dot_nt(first, w_ref[2])], axis=1).astype(bf)
    first_q = dot_nt(first, w_ref[0])
    for tile in range(row_tiles):
        span = slice(tile * TILE, (tile + 1) * TILE)
        rows = kv_ref[span, :].astype(f32)
        sub = lax.broadcasted_iota(jnp.int32, (TILE, 2 * cols), 0) + tile * TILE
        for title in range(per_part):
            row = first_kv[title : title + 1].astype(f32)
            rows = jnp.where(sub == at_ref[title], row, rows)
        rows = rows.astype(bf)
        k_all[span, :] = rows[:, :cols]
        v_all[span, :] = rows[:, cols:]
    lanes = lax.broadcasted_iota(jnp.int32, (TILE, first_kv.shape[0]), 1).astype(f32)
    for tile in range(far_ref.shape[0] // TILE):
        rows = far_ref[tile * TILE : (tile + 1) * TILE, :].astype(f32)
        code = jnp.where(rows[:, 0:1] != rows[:, 0:1], rows[:, 1:2], -1.0)
        hot = jnp.where(lanes == code, 1.0, 0.0).astype(bf)
        fixed = jnp.where(code >= 0.0, dot(hot, first_kv), rows).astype(bf)
        span = slice(nodes + tile * TILE, nodes + (tile + 1) * TILE)
        k_all[span, :] = fixed[:, :cols]
        v_all[span, :] = fixed[:, cols:]

    heads = cols // GHD
    head_of = lax.broadcasted_iota(jnp.int32, (TILE, cols), 1) // GHD
    for tile in range(row_tiles):
        q = q_ref[tile * TILE : (tile + 1) * TILE, :].astype(f32)
        sub = lax.broadcasted_iota(jnp.int32, (TILE, cols), 0) + tile * TILE
        for title in range(per_part):
            q = jnp.where(sub == at_ref[title], first_q[title : title + 1], q)
        q = q.astype(bf)
        stacked = jnp.concatenate(
            [jnp.where(head_of == h, q, jnp.zeros_like(q)) for h in range(heads)], axis=0
        )
        starts = [pl.multiple_of(cols_ref[tile, c] * TILE, TILE) for c in range(TPR)]
        keys = jnp.concatenate([k_all[pl.ds(start, TILE), :] for start in starts], axis=0)
        values = jnp.concatenate([v_all[pl.ds(start, TILE), :] for start in starts], axis=0)
        scores = dot_nt(stacked, keys) * (1.0 / GHD**0.5)
        mask = mask_ref[tile * TILE : (tile + 1) * TILE, :].astype(f32)
        mask = jnp.concatenate([mask] * heads, axis=0) > 0.5
        masked = jnp.where(mask, scores, -jnp.inf)
        expo = jnp.exp(masked - jnp.max(masked, axis=-1, keepdims=True))
        scale = 1.0 / jnp.sum(expo, axis=-1, keepdims=True)
        mixed = dot(expo.astype(bf), values) * scale
        out = mixed[:TILE]
        for h in range(1, heads):
            out = jnp.where(head_of == h, mixed[h * TILE : (h + 1) * TILE], out)
        out_ref[:, tile * TILE : (tile + 1) * TILE] = out.T.astype(bf)


def local(

    titles,
    w_attn_in,
    w_attn_out,
    w_ffn_in,
    w_ffn_out,
    gains,
    node_table,
    w_graph,
    title_nodes,
    send_ids,
    tile_cols,
    nbr_slots,
):
    tok_rows, width = titles.shape
    nodes = node_table.shape[0]
    cols = w_graph.shape[2]
    mp = lax.axis_size("mp")
    dp = lax.axis_size("dp")
    me_mp = lax.axis_index("mp").astype(jnp.int32)
    me_dp = lax.axis_index("dp").astype(jnp.int32)
    me, who = me_dp.reshape(1), me_mp.reshape(1)
    chunk = tok_rows // mp
    per_part = title_nodes.shape[0]
    fetch = send_ids.shape[2]

    def swap(value, step, axis="mp"):
        return lax.ppermute(value, axis, [(i, i ^ step) for i in range(lax.axis_size(axis))])

    def gather(value):
        whose, blocks, step = [0], [value], mp // 2
        while step:
            blocks = blocks + [swap(block, step) for block in blocks]
            whose = whose + [other ^ step for other in whose]
            step //= 2
        return whose, blocks

    def halves(kept, came, pad):
        dims = (chunk + pad, width)
        return call(
            functools.partial(half_kernel, chunk),
            (shape(dims, f32), shape(dims, bf)),
            (kept, came),
            name="half",
        )

    w_attn_in = jnp.swapaxes(w_attn_in, 1, 2)
    w_graph = jnp.swapaxes(w_graph, 1, 2)
    sent = call(
        send_kernel,
        shape((dp * fetch, 2 * cols), bf),
        (me, title_nodes, send_ids[0], node_table, w_graph),
        smem=(0,),
        hbm=(4, 3, 2, 1),
        scalars=(1,),
        out_specs=HBM,
        scratch=[pltpu.VMEM((dp * fetch, 2 * cols), bf), pltpu.SemaphoreType.DMA((dp,))],
        flops=2 * nodes * width * 2 * cols + 2 * dp * fetch * nodes * 2 * cols,
        name="send",
    )
    far = lax.all_to_all(
        sent.reshape(dp, fetch, 2 * cols), "dp", split_axis=0, concat_axis=0, tiled=True
    ).reshape(dp * fetch, 2 * cols)
    titles, _ = lax.optimization_barrier((titles, sent))

    kept, given = call(
        attn_kernel,
        (shape((2 * chunk + PAD, width), f32), shape((2 * chunk + PAD, width), bf)),
        (who, titles, w_attn_in, w_attn_out),
        smem=(0,),
        scratch=[pltpu.VMEM((tok_rows, width), f32)],
        flops=2 * tok_rows * width * 4 * w_attn_in.shape[1],
        name="attn",
    )
    keep, give = halves(kept, swap(given, 1), PAD)
    part = swap(give, 2)
    hidden, first_hidden, first_terms = call(
        norm_one_kernel,
        (shape((chunk + PAD, width), bf), shape((PAD, width), bf), shape((PAD, width), f32)),
        (who, titles, gains, w_ffn_in, w_ffn_out, keep, part),
        smem=(0,),
        name="norm_one",
    )
    whose, hiddens = gather(hidden)
    kept, given, first = call(
        ffn_kernel,
        (
            shape((2 * chunk, width), f32),
            shape((2 * chunk, width), bf),
            shape((per_part, width), bf),
        ),
        (w_ffn_in, w_ffn_out, gains, first_hidden, first_terms, *hiddens),
        flops=4 * tok_rows * width * w_ffn_in.shape[1],
        name="ffn",
    )
    turns = dp // mp
    firsts = [
        lax.ppermute(
            first,
            ("dp", "mp"),
            [
                (p * mp + m, (p ^ (turn * mp + m)) * mp + m)
                for p in range(dp)
                for m in range(mp)
                if turn or m
            ],
        )
        for turn in range(turns)
    ]
    keep, give = halves(kept, swap(given, 1), 0)
    part = swap(give, 2)
    kv, q = call(
        own_kernel,
        (shape((nodes, 2 * cols), bf), shape((nodes, cols), bf)),
        (node_table, w_graph),
        flops=2 * 10**9,
        name="own",
    )
    mask = call(
        mask_kernel, shape((nodes, TPR * TILE), bf), (nbr_slots.T,), flops=4 * 10**9, name="mask"
    )
    part, firsts, kv, q, mask = lax.optimization_barrier((part, firsts, kv, q, mask))
    done = call(
        norm_two_kernel, shape((chunk, width), bf), (hidden, gains, keep, part), name="norm_two"
    )
    pack = call(pack_kernel, shape((tail_rows(turns * per_part), width), bf), firsts, name="pack")
    packs = [pack] + [swap(pack, step) for step in range(1, mp)]
    across = swap(done, 2)
    across, packs, far = lax.optimization_barrier((across, packs, far))
    dones = [done, across, swap(done, 1), swap(across, 1)]
    keys = nodes + dp * fetch
    graph_out, encoded = call(
        functools.partial(graph_kernel, whose),
        (shape((cols, nodes), bf), shape((tok_rows, width), bf)),
        (who, tile_cols, title_nodes, q, kv, w_graph, mask, far, first, *dones, *packs),
        smem=(0, 1, 2),
        scratch=[
            pltpu.VMEM((keys, cols), bf),
            pltpu.VMEM((keys, cols), bf),
            pltpu.VMEM((dp * per_part, width), f32),
        ],
        flops=4 * 10**9,
        name="graph",
    )
    return (encoded, graph_out.T)


def solution(mesh):
    in_specs = (
        P("dp", None),
        P(None, None, "mp"),
        P("mp", None),
        P(None, "mp"),
        P("mp", None),
        P(),
        P("dp", None),
        P(None, None, "mp"),
        P("dp"),
        P("dp", None, None),
        P("dp", None),
        P("dp", None),
    )
    out_specs = (P("dp", None), P("dp", "mp"))
    return jax.shard_map(
        local, mesh=mesh, in_specs=in_specs, out_specs=out_specs, check_vma=False
    )
```

```python
import functools
import jax
import jax.numpy as jnp
from jax import lax
from jax.experimental import pallas as pl
from jax.experimental.pallas import tpu as pltpu
from jax.sharding import PartitionSpec as P

SEQ = 128
TILE = 128
DEG = 16
TPR = 6
HD = 64
GHD = 96

eps_norm = 1e-06
bf = jnp.bfloat16
f32 = jnp.float32

VMEM = pl.BlockSpec(memory_space=pltpu.VMEM)
SMEM = pl.BlockSpec(memory_space=pltpu.SMEM)
HBM = pl.BlockSpec(memory_space=pltpu.HBM)
PAD = 16
NT = (((1,), (1,)), ((), ()))
TN = (((0,), (0,)), ((), ()))


def call(
    kernel,
    outs,
    args,
    smem=(),
    hbm=(),
    scalars=(),
    scratch=(),
    out_specs=None,
    flops=0,
    name=None,
):
    count, out_count, own = len(args), len(jax.tree.leaves(outs)), len(scratch)
    specs = [SMEM if i in smem else HBM if i in hbm else VMEM for i in range(count)]
    nbytes = sum(a.size * a.dtype.itemsize for a in args)
    space = [pltpu.SMEM if i in scalars else pltpu.VMEM for i in hbm]
    buffers = [kind(args[i].shape, args[i].dtype) for kind, i in zip(space, hbm)]
    sems = [pltpu.SemaphoreType.DMA((len(hbm),))] if hbm else []

    def body(*refs):
        ins, rest = list(refs[:count]), refs[count:]
        kept, moved = rest[: out_count + own], rest[out_count + own :]
        moves = {}
        for j, i in enumerate(hbm):
            moves[i] = pltpu.make_async_copy(ins[i], moved[j], moved[-1].at[j])
            moves[i].start()
            ins[i] = moved[j]

        def ready(*wanted):
            for i in wanted:
                moves[i].wait()

        kernel(ready, *ins, *kept)

    return pl.pallas_call(
        body,
        out_shape=outs,
        in_specs=specs,
        out_specs=jax.tree.map(lambda _: VMEM, outs) if out_specs is None else out_specs,
        scratch_shapes=list(scratch) + buffers + sems,
        compiler_params=pltpu.CompilerParams(vmem_limit_bytes=(60 if hbm else 40) * 1024 * 1024),
        cost_estimate=pl.CostEstimate(flops=flops, bytes_accessed=nbytes, transcendentals=0),
        name=name,
    )(*args)


def shape(dims, dtype):
    return jax.ShapeDtypeStruct(dims, dtype)


def dot(a, b):
    return jnp.dot(a, b, preferred_element_type=f32)


def dot_nt(a, b):
    return lax.dot_general(a, b, NT, preferred_element_type=f32)


def dot_tn(a, b):
    return lax.dot_general(a, b, TN, preferred_element_type=f32)


def layer_norm(values, gain):
    mean = jnp.mean(values, axis=-1, keepdims=True)
    centred = values - mean
    var = jnp.mean(centred * centred, axis=-1, keepdims=True)
    return centred * lax.rsqrt(var + eps_norm) * gain


def one_hot(picked, nodes):
    lanes = lax.broadcasted_iota(jnp.int32, (picked.shape[0], nodes), 1)
    return jnp.where(lanes == picked, 1.0, 0.0).astype(bf)


def mark(rows, picked, at_ref, step):
    per_part = at_ref.shape[0]
    code = jnp.full(picked.shape, -1, jnp.int32)
    for title in range(per_part):
        code = jnp.where(picked == at_ref[title], step * per_part + title, code)
    lead = lax.broadcasted_iota(jnp.int32, rows.shape, 1) == 0
    return jnp.where(code >= 0, jnp.where(lead, jnp.nan, code.astype(f32)), rows)


def send_kernel(ready, me_ref, at_ref, ids_ref, table_ref, w_ref, sent_ref, rows_ref, sems):
    cols = w_ref.shape[1]
    fetch, nodes = ids_ref.shape[1], table_ref.shape[0]
    ready(2)
    ids = ids_ref[...].astype(f32).T.astype(jnp.int32)
    ready(1, 3, 4)
    table = table_ref[...]
    kv = jnp.concatenate([dot_nt(table, w_ref[1]), dot_nt(table, w_ref[2])], axis=1).astype(bf)
    moves = []
    for part in range(ids.shape[1]):
        picked = ids[:, part : part + 1]
        rows = mark(dot(one_hot(picked, nodes), kv), picked, at_ref, me_ref[0] ^ part)
        at = pl.ds(part * fetch, fetch)
        rows_ref[at, :] = rows.astype(bf)
        moves.append(pltpu.make_async_copy(rows_ref.at[at, :], sent_ref.at[at, :], sems.at[part]))
        moves[-1].start()
    for move in moves:
        move.wait()


def mask_kernel(ready, slots_ref, mask_ref):
    all_slots = slots_ref[...].astype(f32).T.astype(jnp.int32)
    for tile in range(all_slots.shape[0] // TILE):
        slots = all_slots[tile * TILE : (tile + 1) * TILE, :]
        lanes = lax.broadcasted_iota(jnp.int32, (TILE, TPR * TILE), 1)
        edges = lanes == lax.broadcasted_iota(jnp.int32, (TILE, TPR * TILE), 0)
        for edge in range(DEG):
            edges = edges | (lanes == slots[:, edge : edge + 1])
        mask_ref[tile * TILE : (tile + 1) * TILE, :] = jnp.where(edges, 1.0, 0.0).astype(bf)


def attn_kernel(ready, who_ref, titles_ref, w_in_ref, w_out_ref, *refs):
    outs, total = refs[:-1], refs[-1]
    titles = titles_ref[...]
    q = dot_nt(titles, w_in_ref[0]).astype(bf)
    k = dot_nt(titles, w_in_ref[1]).astype(bf)
    v = dot_nt(titles, w_in_ref[2]).astype(bf)
    cols = q.shape[1]
    heads = cols // HD
    lanes = lax.broadcasted_iota(jnp.int32, (SEQ, cols), 1) // HD
    for title in range(titles.shape[0] // SEQ):
        rows = slice(title * SEQ, (title + 1) * SEQ)
        qt, kt, vt = q[rows], k[rows], v[rows]
        stacked = jnp.concatenate(
            [jnp.where(lanes == h, qt, jnp.zeros_like(qt)) for h in range(heads)], axis=0
        )
        scores = dot_nt(stacked, kt) * (1.0 / HD**0.5)
        expo = jnp.exp(scores - jnp.max(scores, axis=-1, keepdims=True))
        probs = (expo / jnp.sum(expo, axis=-1, keepdims=True)).astype(bf)
        mixed = dot(probs, vt)
        context = mixed[:SEQ]
        for h in range(1, heads):
            context = jnp.where(lanes == h, mixed[h * SEQ : (h + 1) * SEQ], context)
        total[rows, :] = dot(context.astype(bf), w_out_ref[...])
    chunk = (outs[0].shape[0] - PAD) // 2
    firsts = first_rows(total)
    for out, pair in zip(outs, ((0, 2), (1, 3))):
        for j, step in enumerate(pair):
            at = pl.ds(pl.multiple_of((who_ref[0] ^ step) * chunk, chunk), chunk)
            out[j * chunk : (j + 1) * chunk, :] = total[at, :].astype(out.dtype)
        out[2 * chunk :, :] = firsts.astype(out.dtype)


def half_kernel(chunk, ready, kept_ref, came_ref, keep_ref, give_ref):
    total = kept_ref[...] + came_ref[...].astype(f32)
    keep_ref[:chunk, :] = total[:chunk]
    give_ref[:chunk, :] = total[chunk : 2 * chunk].astype(bf)
    if keep_ref.shape[0] > chunk:
        keep_ref[chunk:, :] = total[2 * chunk :]
        give_ref[chunk:, :] = total[2 * chunk :].astype(bf)


def first_rows(ref):
    sub = lax.broadcasted_iota(jnp.int32, (PAD, ref.shape[1]), 0)
    rows = jnp.zeros((PAD, ref.shape[1]), f32)
    for title in range(ref.shape[0] // SEQ):
        row = ref[title * SEQ : title * SEQ + 1, :].astype(f32)
        rows = jnp.where(sub == title, row, rows)
    return rows


def norm_one_kernel(
    ready, who_ref, titles_ref, gains_ref, w_in_ref, w_out_ref, own_ref, *refs
):
    *parts, out, first_hidden, first_terms = refs
    chunk = own_ref.shape[0] - PAD
    total = own_ref[...]
    for part in parts:
        total = total + part[...].astype(f32)
    at = pl.ds(pl.multiple_of(who_ref[0] * chunk, chunk), chunk)
    base = jnp.concatenate([titles_ref[at, :].astype(f32), first_rows(titles_ref)], axis=0)
    hidden = layer_norm(base + total, gains_ref[0:1, :]).astype(bf)
    out[:chunk, :] = hidden[:chunk]
    firsts = hidden[chunk:]
    first_hidden[...] = firsts
    terms = dot(gelu(dot(firsts, w_in_ref[...])).astype(bf), w_out_ref[...])
    first_terms[...] = terms
    out[chunk:, :] = terms.astype(bf)


def gelu(x):
    return 0.5 * x * (1.0 + lax.erf(x * (0.5**0.5)))


def ffn_kernel(ready, w_in_ref, w_out_ref, gains_ref, first_hidden, first_terms, *refs):
    *ins, kept, sent, first = refs
    chunk = kept.shape[0] // 2
    hidden = jnp.concatenate([ref[:chunk, :] for ref in ins], axis=0)
    inner = gelu(dot(hidden, w_in_ref[...])).astype(bf)
    total = dot(inner, w_out_ref[...])
    kept[...] = total[: 2 * chunk]
    sent[...] = total[2 * chunk :].astype(bf)
    terms = first_terms[...]
    for ref in ins[1:]:
        terms = terms + ref[chunk:, :].astype(f32)
    done = layer_norm(first_hidden[...].astype(f32) + terms, gains_ref[1:2, :])
    first[...] = done[: first.shape[0]].astype(bf)


def norm_two_kernel(ready, hidden_ref, gains_ref, own_ref, *refs):
    *parts, out = refs
    total = own_ref[...]
    for part in parts:
        total = total + part[...].astype(f32)
    hidden = hidden_ref[: out.shape[0], :].astype(f32)
    out[...] = layer_norm(hidden + total, gains_ref[1:2, :]).astype(bf)


def pack_kernel(ready, *refs):
    *parts, out = refs
    per_part = parts[0].shape[0]
    sub = lax.broadcasted_iota(jnp.int32, out.shape, 0)
    rows = jnp.zeros(out.shape, f32)
    for turn, ref in enumerate(parts):
        for title in range(per_part):
            row = ref[title : title + 1, :].astype(f32)
            rows = jnp.where(sub == turn * per_part + title, row, rows)
    out[...] = rows.astype(bf)


def own_kernel(ready, table_ref, w_ref, kv_ref, q_ref):
    cols = w_ref.shape[1]
    table = table_ref[...]
    kv_ref[:, :cols] = dot_nt(table, w_ref[1]).astype(bf)
    kv_ref[:, cols:] = dot_nt(table, w_ref[2]).astype(bf)
    q_ref[...] = dot_nt(table, w_ref[0]).astype(bf)


def tail_rows(count):
    return -(-count // PAD) * PAD


def graph_kernel(
    whose, ready, who_ref, cols_ref, at_ref, q_ref, kv_ref, w_ref, mask_ref, far_ref, first_ref, *refs
):
    *packs, out_ref, encoded_ref, k_all, v_all, firsts = refs
    dones, packs = packs[: len(whose)], packs[len(whose) :]
    chunk = dones[0].shape[0]
    for step, ref in zip(whose, dones):
        at = pl.multiple_of((who_ref[0] ^ step) * chunk, chunk)
        encoded_ref[pl.ds(at, chunk), :] = ref[...]
    nodes, cols = q_ref.shape
    row_tiles = nodes // TILE
    per_part = first_ref.shape[0]
    members = len(packs)
    for step, ref in enumerate(packs):
        rows = ref[...].astype(f32)
        for turn in range(firsts.shape[0] // per_part // members):
            for title in range(per_part):
                place = (turn * members + lax.rem(who_ref[0] ^ step, members)) * per_part + title
                at = turn * per_part + title
                firsts[pl.ds(place, 1), :] = rows[at : at + 1]
    firsts[0:per_part, :] = first_ref[...].astype(f32)
    first = firsts[...].astype(bf)
    first_kv = jnp.concatenate([dot_nt(first, w_ref[1]), dot_nt(first, w_ref[2])], axis=1).astype(bf)
    first_q = dot_nt(first, w_ref[0])
    for tile in range(row_tiles):
        span = slice(tile * TILE, (tile + 1) * TILE)
        rows = kv_ref[span, :].astype(f32)
        sub = lax.broadcasted_iota(jnp.int32, (TILE, 2 * cols), 0) + tile * TILE
        for title in range(per_part):
            row = first_kv[title : title + 1].astype(f32)
            rows = jnp.where(sub == at_ref[title], row, rows)
        rows = rows.astype(bf)
        k_all[span, :] = rows[:, :cols]
        v_all[span, :] = rows[:, cols:]
    lanes = lax.broadcasted_iota(jnp.int32, (TILE, first_kv.shape[0]), 1).astype(f32)
    for tile in range(far_ref.shape[0] // TILE):
        rows = far_ref[tile * TILE : (tile + 1) * TILE, :].astype(f32)
        code = jnp.where(rows[:, 0:1] != rows[:, 0:1], rows[:, 1:2], -1.0)
        hot = jnp.where(lanes == code, 1.0, 0.0).astype(bf)
        fixed = jnp.where(code >= 0.0, dot(hot, first_kv), rows).astype(bf)
        span = slice(nodes + tile * TILE, nodes + (tile + 1) * TILE)
        k_all[span, :] = fixed[:, :cols]
        v_all[span, :] = fixed[:, cols:]

    heads = cols // GHD
    head_of = lax.broadcasted_iota(jnp.int32, (TILE, cols), 1) // GHD
    for tile in range(row_tiles):
        q = q_ref[tile * TILE : (tile + 1) * TILE, :].astype(f32)
        sub = lax.broadcasted_iota(jnp.int32, (TILE, cols), 0) + tile * TILE
        for title in range(per_part):
            q = jnp.where(sub == at_ref[title], first_q[title : title + 1], q)
        q = q.astype(bf)
        stacked = jnp.concatenate(
            [jnp.where(head_of == h, q, jnp.zeros_like(q)) for h in range(heads)], axis=0
        )
        starts = [pl.multiple_of(cols_ref[tile, c] * TILE, TILE) for c in range(TPR)]
        keys = jnp.concatenate([k_all[pl.ds(start, TILE), :] for start in starts], axis=0)
        values = jnp.concatenate([v_all[pl.ds(start, TILE), :] for start in starts], axis=0)
        scores = dot_nt(stacked, keys) * (1.0 / GHD**0.5)
        mask = mask_ref[tile * TILE : (tile + 1) * TILE, :].astype(f32)
        mask = jnp.concatenate([mask] * heads, axis=0) > 0.5
        masked = jnp.where(mask, scores, -jnp.inf)
        expo = jnp.exp(masked - jnp.max(masked, axis=-1, keepdims=True))
        scale = 1.0 / jnp.sum(expo, axis=-1, keepdims=True)
        mixed = dot(expo.astype(bf), values) * scale
        out = mixed[:TILE]
        for h in range(1, heads):
            out = jnp.where(head_of == h, mixed[h * TILE : (h + 1) * TILE], out)
        out_ref[:, tile * TILE : (tile + 1) * TILE] = out.T.astype(bf)


def local(

    titles,
    w_attn_in,
    w_attn_out,
    w_ffn_in,
    w_ffn_out,
    gains,
    node_table,
    w_graph,
    title_nodes,
    send_ids,
    tile_cols,
    nbr_slots,
):
    tok_rows, width = titles.shape
    nodes = node_table.shape[0]
    cols = w_graph.shape[2]
    mp = lax.axis_size("mp")
    dp = lax.axis_size("dp")
    me_mp = lax.axis_index("mp").astype(jnp.int32)
    me_dp = lax.axis_index("dp").astype(jnp.int32)
    me, who = me_dp.reshape(1), me_mp.reshape(1)
    chunk = tok_rows // mp
    per_part = title_nodes.shape[0]
    fetch = send_ids.shape[2]

    def swap(value, step, axis="mp"):
        return lax.ppermute(value, axis, [(i, i ^ step) for i in range(lax.axis_size(axis))])

    def gather(value):
        whose, blocks, step = [0], [value], mp // 2
        while step:
            blocks = blocks + [swap(block, step) for block in blocks]
            whose = whose + [other ^ step for other in whose]
            step //= 2
        return whose, blocks

    def halves(kept, came, pad):
        dims = (chunk + pad, width)
        return call(
            functools.partial(half_kernel, chunk),
            (shape(dims, f32), shape(dims, bf)),
            (kept, came),
            name="half",
        )

    w_attn_in = jnp.swapaxes(w_attn_in, 1, 2)
    w_graph = jnp.swapaxes(w_graph, 1, 2)
    sent = call(
        send_kernel,
        shape((dp * fetch, 2 * cols), bf),
        (me, title_nodes, send_ids[0], node_table, w_graph),
        smem=(0,),
        hbm=(4, 3, 2, 1),
        scalars=(1,),
        out_specs=HBM,
        scratch=[pltpu.VMEM((dp * fetch, 2 * cols), bf), pltpu.SemaphoreType.DMA((dp,))],
        flops=2 * nodes * width * 2 * cols + 2 * dp * fetch * nodes * 2 * cols,
        name="send",
    )
    far = lax.all_to_all(
        sent.reshape(dp, fetch, 2 * cols), "dp", split_axis=0, concat_axis=0, tiled=True
    ).reshape(dp * fetch, 2 * cols)
    titles, _ = lax.optimization_barrier((titles, sent))

    kept, given = call(
        attn_kernel,
        (shape((2 * chunk + PAD, width), f32), shape((2 * chunk + PAD, width), bf)),
        (who, titles, w_attn_in, w_attn_out),
        smem=(0,),
        scratch=[pltpu.VMEM((tok_rows, width), f32)],
        flops=2 * tok_rows * width * 4 * w_attn_in.shape[1],
        name="attn",
    )
    keep, give = halves(kept, swap(given, 1), PAD)
    part = swap(give, 2)
    kv, q = call(
        own_kernel,
        (shape((nodes, 2 * cols), bf), shape((nodes, cols), bf)),
        (node_table, w_graph),
        flops=2 * 10**9,
        name="own",
    )
    part, kv, q = lax.optimization_barrier((part, kv, q))
    hidden, first_hidden, first_terms = call(
        norm_one_kernel,
        (shape((chunk + PAD, width), bf), shape((PAD, width), bf), shape((PAD, width), f32)),
        (who, titles, gains, w_ffn_in, w_ffn_out, keep, part),
        smem=(0,),
        name="norm_one",
    )
    whose, hiddens = gather(hidden)
    kept, given, first = call(
        ffn_kernel,
        (
            shape((2 * chunk, width), f32),
            shape((2 * chunk, width), bf),
            shape((per_part, width), bf),
        ),
        (w_ffn_in, w_ffn_out, gains, first_hidden, first_terms, *hiddens),
        flops=4 * tok_rows * width * w_ffn_in.shape[1],
        name="ffn",
    )
    pair = 2
    turns = dp // pair
    firsts = [
        lax.ppermute(
            first,
            ("dp", "mp"),
            [
                (p * mp + m, (p ^ (turn * pair + m % pair)) * mp + m)
                for p in range(dp)
                for m in range(mp)
                if turn or m % pair
            ],
        )
        for turn in range(turns)
    ]
    keep, give = halves(kept, swap(given, 1), 0)
    give, slots = lax.optimization_barrier((give, nbr_slots))
    part = swap(give, 2)
    mask = call(
        mask_kernel, shape((nodes, TPR * TILE), bf), (slots.T,), flops=4 * 10**9, name="mask"
    )
    part, mask = lax.optimization_barrier((part, mask))
    done = call(
        norm_two_kernel, shape((chunk, width), bf), (hidden, gains, keep, part), name="norm_two"
    )
    across = swap(done, 2)
    across, firsts = lax.optimization_barrier((across, firsts))
    pack = call(pack_kernel, shape((tail_rows(turns * per_part), width), bf), firsts, name="pack")
    packs = [pack, swap(pack, 1)]
    dones = [done, across, swap(done, 1), swap(across, 1)]
    keys = nodes + dp * fetch
    graph_out, encoded = call(
        functools.partial(graph_kernel, whose),
        (shape((cols, nodes), bf), shape((tok_rows, width), bf)),
        (who, tile_cols, title_nodes, q, kv, w_graph, mask, far, first, *dones, *packs),
        smem=(0, 1, 2),
        scratch=[
            pltpu.VMEM((keys, cols), bf),
            pltpu.VMEM((keys, cols), bf),
            pltpu.VMEM((dp * per_part, width), f32),
        ],
        flops=4 * 10**9,
        name="graph",
    )
    return (encoded, graph_out.T)


def solution(mesh):
    in_specs = (
        P("dp", None),
        P(None, None, "mp"),
        P("mp", None),
        P(None, "mp"),
        P("mp", None),
        P(),
        P("dp", None),
        P(None, None, "mp"),
        P("dp"),
        P("dp", None, None),
        P("dp", None),
        P("dp", None),
    )
    out_specs = (P("dp", None), P("dp", "mp"))
    return jax.shard_map(
        local, mesh=mesh, in_specs=in_specs, out_specs=out_specs, check_vma=False
    )
```

```python
import functools
import jax
import jax.numpy as jnp
from jax import lax
from jax.experimental import pallas as pl
from jax.experimental.pallas import tpu as pltpu
from jax.sharding import PartitionSpec as P

SEQ = 128
TILE = 128
DEG = 16
TPR = 6
HD = 64
GHD = 96

eps_norm = 1e-06
bf = jnp.bfloat16
f32 = jnp.float32

VMEM = pl.BlockSpec(memory_space=pltpu.VMEM)
SMEM = pl.BlockSpec(memory_space=pltpu.SMEM)
HBM = pl.BlockSpec(memory_space=pltpu.HBM)
PAD = 16
NT = (((1,), (1,)), ((), ()))
TN = (((0,), (0,)), ((), ()))


def call(
    kernel,
    outs,
    args,
    smem=(),
    hbm=(),
    pieces=None,
    scalars=(),
    scratch=(),
    out_specs=None,
    flops=0,
    name=None,
):
    count, out_count, own = len(args), len(jax.tree.leaves(outs)), len(scratch)
    specs = [SMEM if i in smem else HBM if i in hbm else VMEM for i in range(count)]
    nbytes = sum(a.size * a.dtype.itemsize for a in args)
    space = [pltpu.SMEM if i in scalars else pltpu.VMEM for i in hbm]
    buffers = [kind(args[i].shape, args[i].dtype) for kind, i in zip(space, hbm)]
    spans = {i: (pieces or {}).get(i, ((0, args[i].shape[0]),)) for i in hbm}
    sems = [pltpu.SemaphoreType.DMA((len(spans[i]),)) for i in hbm]

    def body(*refs):
        ins, rest = list(refs[:count]), refs[count:]
        kept, moved = rest[: out_count + own], rest[out_count + own :]
        moves = {}
        for j, i in enumerate(hbm):
            moves[i] = []
            for k, (start, size) in enumerate(spans[i]):
                at = pl.ds(start, size)
                move = pltpu.make_async_copy(
                    ins[i].at[at], moved[j].at[at], moved[len(hbm) + j].at[k]
                )
                move.start()
                moves[i].append(move)
            ins[i] = moved[j]

        def ready(*wanted):
            for i in wanted:
                for move in moves[i]:
                    move.wait()

        kernel(ready, *ins, *kept)

    return pl.pallas_call(
        body,
        out_shape=outs,
        in_specs=specs,
        out_specs=jax.tree.map(lambda _: VMEM, outs) if out_specs is None else out_specs,
        scratch_shapes=list(scratch) + buffers + sems,
        compiler_params=pltpu.CompilerParams(vmem_limit_bytes=(60 if hbm else 40) * 1024 * 1024),
        cost_estimate=pl.CostEstimate(flops=flops, bytes_accessed=nbytes, transcendentals=0),
        name=name,
    )(*args)


def shape(dims, dtype):
    return jax.ShapeDtypeStruct(dims, dtype)


def dot(a, b):
    return jnp.dot(a, b, preferred_element_type=f32)


def dot_nt(a, b):
    return lax.dot_general(a, b, NT, preferred_element_type=f32)


def dot_tn(a, b):
    return lax.dot_general(a, b, TN, preferred_element_type=f32)


def layer_norm(values, gain):
    mean = jnp.mean(values, axis=-1, keepdims=True)
    centred = values - mean
    var = jnp.mean(centred * centred, axis=-1, keepdims=True)
    return centred * lax.rsqrt(var + eps_norm) * gain


def one_hot(picked, nodes):
    lanes = lax.broadcasted_iota(jnp.int32, (picked.shape[0], nodes), 1)
    return jnp.where(lanes == picked, 1.0, 0.0).astype(bf)


def mark(rows, picked, at_ref, step):
    per_part = at_ref.shape[0]
    code = jnp.full(picked.shape, -1, jnp.int32)
    for title in range(per_part):
        code = jnp.where(picked == at_ref[title], step * per_part + title, code)
    lead = lax.broadcasted_iota(jnp.int32, rows.shape, 1) == 0
    return jnp.where(code >= 0, jnp.where(lead, jnp.nan, code.astype(f32)), rows)


def send_kernel(ready, me_ref, at_ref, ids_ref, table_ref, w_ref, sent_ref, rows_ref, sems):
    cols = w_ref.shape[1]
    fetch, nodes = ids_ref.shape[1], table_ref.shape[0]
    ready(2)
    ids = ids_ref[...].astype(f32).T.astype(jnp.int32)
    ready(1, 3, 4)
    table = table_ref[...]
    kv = jnp.concatenate([dot_nt(table, w_ref[1]), dot_nt(table, w_ref[2])], axis=1).astype(bf)
    moves = []
    for part in range(ids.shape[1]):
        picked = ids[:, part : part + 1]
        rows = mark(dot(one_hot(picked, nodes), kv), picked, at_ref, me_ref[0] ^ part)
        at = pl.ds(part * fetch, fetch)
        rows_ref[at, :] = rows.astype(bf)
        moves.append(pltpu.make_async_copy(rows_ref.at[at, :], sent_ref.at[at, :], sems.at[part]))
        moves[-1].start()
    for move in moves:
        move.wait()


def mask_kernel(ready, slots_ref, mask_ref):
    all_slots = slots_ref[...].astype(f32).T.astype(jnp.int32)
    for tile in range(all_slots.shape[0] // TILE):
        slots = all_slots[tile * TILE : (tile + 1) * TILE, :]
        lanes = lax.broadcasted_iota(jnp.int32, (TILE, TPR * TILE), 1)
        edges = lanes == lax.broadcasted_iota(jnp.int32, (TILE, TPR * TILE), 0)
        for edge in range(DEG):
            edges = edges | (lanes == slots[:, edge : edge + 1])
        mask_ref[tile * TILE : (tile + 1) * TILE, :] = jnp.where(edges, 1.0, 0.0).astype(bf)


def attn_kernel(ready, who_ref, titles_ref, w_in_ref, w_out_ref, *refs):
    outs, total = refs[:-1], refs[-1]
    titles = titles_ref[...]
    q = dot_nt(titles, w_in_ref[0]).astype(bf)
    k = dot_nt(titles, w_in_ref[1]).astype(bf)
    v = dot_nt(titles, w_in_ref[2]).astype(bf)
    cols = q.shape[1]
    heads = cols // HD
    lanes = lax.broadcasted_iota(jnp.int32, (SEQ, cols), 1) // HD
    for title in range(titles.shape[0] // SEQ):
        rows = slice(title * SEQ, (title + 1) * SEQ)
        qt, kt, vt = q[rows], k[rows], v[rows]
        stacked = jnp.concatenate(
            [jnp.where(lanes == h, qt, jnp.zeros_like(qt)) for h in range(heads)], axis=0
        )
        scores = dot_nt(stacked, kt) * (1.0 / HD**0.5)
        expo = jnp.exp(scores - jnp.max(scores, axis=-1, keepdims=True))
        probs = (expo / jnp.sum(expo, axis=-1, keepdims=True)).astype(bf)
        mixed = dot(probs, vt)
        context = mixed[:SEQ]
        for h in range(1, heads):
            context = jnp.where(lanes == h, mixed[h * SEQ : (h + 1) * SEQ], context)
        total[rows, :] = dot(context.astype(bf), w_out_ref[...])
    chunk = (outs[0].shape[0] - PAD) // 2
    firsts = first_rows(total)
    for out, pair in zip(outs, ((0, 2), (1, 3))):
        for j, step in enumerate(pair):
            at = pl.ds(pl.multiple_of((who_ref[0] ^ step) * chunk, chunk), chunk)
            out[j * chunk : (j + 1) * chunk, :] = total[at, :].astype(out.dtype)
        out[2 * chunk :, :] = firsts.astype(out.dtype)


def half_kernel(chunk, ready, kept_ref, came_ref, keep_ref, give_ref):
    total = kept_ref[...] + came_ref[...].astype(f32)
    keep_ref[:chunk, :] = total[:chunk]
    give_ref[:chunk, :] = total[chunk : 2 * chunk].astype(bf)
    if keep_ref.shape[0] > chunk:
        keep_ref[chunk:, :] = total[2 * chunk :]
        give_ref[chunk:, :] = total[2 * chunk :].astype(bf)


def first_rows(ref):
    sub = lax.broadcasted_iota(jnp.int32, (PAD, ref.shape[1]), 0)
    rows = jnp.zeros((PAD, ref.shape[1]), f32)
    for title in range(ref.shape[0] // SEQ):
        row = ref[title * SEQ : title * SEQ + 1, :].astype(f32)
        rows = jnp.where(sub == title, row, rows)
    return rows


def norm_one_kernel(
    ready, who_ref, titles_ref, gains_ref, w_in_ref, w_out_ref, own_ref, *refs
):
    *parts, out, first_hidden, first_terms = refs
    chunk = own_ref.shape[0] - PAD
    total = own_ref[...]
    for part in parts:
        total = total + part[...].astype(f32)
    at = pl.ds(pl.multiple_of(who_ref[0] * chunk, chunk), chunk)
    base = jnp.concatenate([titles_ref[at, :].astype(f32), first_rows(titles_ref)], axis=0)
    hidden = layer_norm(base + total, gains_ref[0:1, :]).astype(bf)
    out[:chunk, :] = hidden[:chunk]
    firsts = hidden[chunk:]
    first_hidden[...] = firsts
    terms = dot(gelu(dot(firsts, w_in_ref[...])).astype(bf), w_out_ref[...])
    first_terms[...] = terms
    out[chunk:, :] = terms.astype(bf)


def gelu(x):
    return 0.5 * x * (1.0 + lax.erf(x * (0.5**0.5)))


def ffn_kernel(ready, w_in_ref, w_out_ref, gains_ref, first_hidden, first_terms, *refs):
    *ins, kept, sent, first = refs
    chunk = kept.shape[0] // 2
    hidden = jnp.concatenate([ref[:chunk, :] for ref in ins], axis=0)
    inner = gelu(dot(hidden, w_in_ref[...])).astype(bf)
    total = dot(inner, w_out_ref[...])
    kept[...] = total[: 2 * chunk]
    sent[...] = total[2 * chunk :].astype(bf)
    terms = first_terms[...]
    for ref in ins[1:]:
        terms = terms + ref[chunk:, :].astype(f32)
    done = layer_norm(first_hidden[...].astype(f32) + terms, gains_ref[1:2, :])
    first[...] = done[: first.shape[0]].astype(bf)


def norm_two_kernel(ready, hidden_ref, gains_ref, own_ref, *refs):
    *parts, out = refs
    total = own_ref[...]
    for part in parts:
        total = total + part[...].astype(f32)
    hidden = hidden_ref[: out.shape[0], :].astype(f32)
    out[...] = layer_norm(hidden + total, gains_ref[1:2, :]).astype(bf)


def pack_kernel(ready, *refs):
    *parts, out = refs
    per_part = parts[0].shape[0]
    sub = lax.broadcasted_iota(jnp.int32, out.shape, 0)
    rows = jnp.zeros(out.shape, f32)
    for turn, ref in enumerate(parts):
        for title in range(per_part):
            row = ref[title : title + 1, :].astype(f32)
            rows = jnp.where(sub == turn * per_part + title, row, rows)
    out[...] = rows.astype(bf)


def own_kernel(ready, table_ref, w_ref, kv_ref, q_ref):
    cols = w_ref.shape[1]
    table = table_ref[...]
    kv_ref[:, :cols] = dot_nt(table, w_ref[1]).astype(bf)
    kv_ref[:, cols:] = dot_nt(table, w_ref[2]).astype(bf)
    q_ref[...] = dot_nt(table, w_ref[0]).astype(bf)


def tail_rows(count):
    return -(-count // PAD) * PAD


def graph_kernel(
    whose, ready, who_ref, cols_ref, at_ref, q_ref, kv_ref, w_ref, mask_ref, far_ref, first_ref, *refs
):
    *packs, out_ref, encoded_ref, k_all, v_all, firsts = refs
    dones, packs = packs[: len(whose)], packs[len(whose) :]
    chunk = dones[0].shape[0]
    for step, ref in zip(whose, dones):
        at = pl.multiple_of((who_ref[0] ^ step) * chunk, chunk)
        encoded_ref[pl.ds(at, chunk), :] = ref[...]
    nodes, cols = q_ref.shape
    row_tiles = nodes // TILE
    per_part = first_ref.shape[0]
    members = len(packs)
    for step, ref in enumerate(packs):
        rows = ref[...].astype(f32)
        for turn in range(firsts.shape[0] // per_part // members):
            for title in range(per_part):
                place = (turn * members + lax.rem(who_ref[0] ^ step, members)) * per_part + title
                at = turn * per_part + title
                firsts[pl.ds(place, 1), :] = rows[at : at + 1]
    firsts[0:per_part, :] = first_ref[...].astype(f32)
    first = firsts[...].astype(bf)
    first_kv = jnp.concatenate([dot_nt(first, w_ref[1]), dot_nt(first, w_ref[2])], axis=1).astype(bf)
    first_q = dot_nt(first, w_ref[0])
    for tile in range(row_tiles):
        span = slice(tile * TILE, (tile + 1) * TILE)
        rows = kv_ref[span, :].astype(f32)
        sub = lax.broadcasted_iota(jnp.int32, (TILE, 2 * cols), 0) + tile * TILE
        for title in range(per_part):
            row = first_kv[title : title + 1].astype(f32)
            rows = jnp.where(sub == at_ref[title], row, rows)
        rows = rows.astype(bf)
        k_all[span, :] = rows[:, :cols]
        v_all[span, :] = rows[:, cols:]
    lanes = lax.broadcasted_iota(jnp.int32, (TILE, first_kv.shape[0]), 1).astype(f32)
    for tile in range(far_ref.shape[0] // TILE):
        rows = far_ref[tile * TILE : (tile + 1) * TILE, :].astype(f32)
        code = jnp.where(rows[:, 0:1] != rows[:, 0:1], rows[:, 1:2], -1.0)
        hot = jnp.where(lanes == code, 1.0, 0.0).astype(bf)
        fixed = jnp.where(code >= 0.0, dot(hot, first_kv), rows).astype(bf)
        span = slice(nodes + tile * TILE, nodes + (tile + 1) * TILE)
        k_all[span, :] = fixed[:, :cols]
        v_all[span, :] = fixed[:, cols:]

    heads = cols // GHD
    head_of = lax.broadcasted_iota(jnp.int32, (TILE, cols), 1) // GHD
    for tile in range(row_tiles):
        q = q_ref[tile * TILE : (tile + 1) * TILE, :].astype(f32)
        sub = lax.broadcasted_iota(jnp.int32, (TILE, cols), 0) + tile * TILE
        for title in range(per_part):
            q = jnp.where(sub == at_ref[title], first_q[title : title + 1], q)
        q = q.astype(bf)
        stacked = jnp.concatenate(
            [jnp.where(head_of == h, q, jnp.zeros_like(q)) for h in range(heads)], axis=0
        )
        starts = [pl.multiple_of(cols_ref[tile, c] * TILE, TILE) for c in range(TPR)]
        keys = jnp.concatenate([k_all[pl.ds(start, TILE), :] for start in starts], axis=0)
        values = jnp.concatenate([v_all[pl.ds(start, TILE), :] for start in starts], axis=0)
        scores = dot_nt(stacked, keys) * (1.0 / GHD**0.5)
        mask = mask_ref[tile * TILE : (tile + 1) * TILE, :].astype(f32)
        mask = jnp.concatenate([mask] * heads, axis=0) > 0.5
        masked = jnp.where(mask, scores, -jnp.inf)
        expo = jnp.exp(masked - jnp.max(masked, axis=-1, keepdims=True))
        scale = 1.0 / jnp.sum(expo, axis=-1, keepdims=True)
        mixed = dot(expo.astype(bf), values) * scale
        out = mixed[:TILE]
        for h in range(1, heads):
            out = jnp.where(head_of == h, mixed[h * TILE : (h + 1) * TILE], out)
        out_ref[:, tile * TILE : (tile + 1) * TILE] = out.T.astype(bf)


def local(

    titles,
    w_attn_in,
    w_attn_out,
    w_ffn_in,
    w_ffn_out,
    gains,
    node_table,
    w_graph,
    title_nodes,
    send_ids,
    tile_cols,
    nbr_slots,
):
    tok_rows, width = titles.shape
    nodes = node_table.shape[0]
    cols = w_graph.shape[2]
    mp = lax.axis_size("mp")
    dp = lax.axis_size("dp")
    me_mp = lax.axis_index("mp").astype(jnp.int32)
    me_dp = lax.axis_index("dp").astype(jnp.int32)
    me, who = me_dp.reshape(1), me_mp.reshape(1)
    chunk = tok_rows // mp
    per_part = title_nodes.shape[0]
    fetch = send_ids.shape[2]

    def swap(value, step, axis="mp"):
        return lax.ppermute(value, axis, [(i, i ^ step) for i in range(lax.axis_size(axis))])

    def gather(value):
        whose, blocks, step = [0], [value], mp // 2
        while step:
            blocks = blocks + [swap(block, step) for block in blocks]
            whose = whose + [other ^ step for other in whose]
            step //= 2
        return whose, blocks

    def halves(kept, came, pad):
        dims = (chunk + pad, width)
        return call(
            functools.partial(half_kernel, chunk),
            (shape(dims, f32), shape(dims, bf)),
            (kept, came),
            name="half",
        )

    w_attn_in = jnp.swapaxes(w_attn_in, 1, 2)
    w_graph = jnp.swapaxes(w_graph, 1, 2)
    sent = call(
        send_kernel,
        shape((dp * fetch, 2 * cols), bf),
        (me, title_nodes, send_ids[0], node_table, w_graph),
        smem=(0,),
        hbm=(2, 3, 4, 1),
        pieces={3: [(i, nodes // 4) for i in range(0, nodes, nodes // 4)], 4: [(1, 1), (2, 1)]},
        scalars=(1,),
        out_specs=HBM,
        scratch=[pltpu.VMEM((dp * fetch, 2 * cols), bf), pltpu.SemaphoreType.DMA((dp,))],
        flops=2 * nodes * width * 2 * cols + 2 * dp * fetch * nodes * 2 * cols,
        name="send",
    )
    far = lax.all_to_all(
        sent.reshape(dp, fetch, 2 * cols), "dp", split_axis=0, concat_axis=0, tiled=True
    ).reshape(dp * fetch, 2 * cols)
    titles, _ = lax.optimization_barrier((titles, sent))

    kept, given = call(
        attn_kernel,
        (shape((2 * chunk + PAD, width), f32), shape((2 * chunk + PAD, width), bf)),
        (who, titles, w_attn_in, w_attn_out),
        smem=(0,),
        scratch=[pltpu.VMEM((tok_rows, width), f32)],
        flops=2 * tok_rows * width * 4 * w_attn_in.shape[1],
        name="attn",
    )
    keep, give = halves(kept, swap(given, 1), PAD)
    part = swap(give, 2)
    kv, q = call(
        own_kernel,
        (shape((nodes, 2 * cols), bf), shape((nodes, cols), bf)),
        (node_table, w_graph),
        flops=2 * 10**9,
        name="own",
    )
    part, kv, q = lax.optimization_barrier((part, kv, q))
    hidden, first_hidden, first_terms = call(
        norm_one_kernel,
        (shape((chunk + PAD, width), bf), shape((PAD, width), bf), shape((PAD, width), f32)),
        (who, titles, gains, w_ffn_in, w_ffn_out, keep, part),
        smem=(0,),
        name="norm_one",
    )
    whose, hiddens = gather(hidden)
    kept, given, first = call(
        ffn_kernel,
        (
            shape((2 * chunk, width), f32),
            shape((2 * chunk, width), bf),
            shape((per_part, width), bf),
        ),
        (w_ffn_in, w_ffn_out, gains, first_hidden, first_terms, *hiddens),
        flops=4 * tok_rows * width * w_ffn_in.shape[1],
        name="ffn",
    )
    pair = 2
    turns = dp // pair
    firsts = [
        lax.ppermute(
            first,
            ("dp", "mp"),
            [
                (p * mp + m, (p ^ (turn * pair + m % pair)) * mp + m)
                for p in range(dp)
                for m in range(mp)
                if turn or m % pair
            ],
        )
        for turn in range(turns)
    ]
    keep, give = halves(kept, swap(given, 1), 0)
    give, slots = lax.optimization_barrier((give, nbr_slots))
    part = swap(give, 2)
    mask = call(
        mask_kernel, shape((nodes, TPR * TILE), bf), (slots.T,), flops=4 * 10**9, name="mask"
    )
    part, mask = lax.optimization_barrier((part, mask))
    done = call(
        norm_two_kernel, shape((chunk, width), bf), (hidden, gains, keep, part), name="norm_two"
    )
    across = swap(done, 2)
    across, firsts, far = lax.optimization_barrier((across, firsts, far))
    pack = call(pack_kernel, shape((tail_rows(turns * per_part), width), bf), firsts, name="pack")
    packs = [pack, swap(pack, 1)]
    dones = [done, across, swap(done, 1), swap(across, 1)]
    keys = nodes + dp * fetch
    graph_out, encoded = call(
        functools.partial(graph_kernel, whose),
        (shape((cols, nodes), bf), shape((tok_rows, width), bf)),
        (who, tile_cols, title_nodes, q, kv, w_graph, mask, far, first, *dones, *packs),
        smem=(0, 1, 2),
        scratch=[
            pltpu.VMEM((keys, cols), bf),
            pltpu.VMEM((keys, cols), bf),
            pltpu.VMEM((dp * per_part, width), f32),
        ],
        flops=4 * 10**9,
        name="graph",
    )
    return (encoded, graph_out.T)


def solution(mesh):
    in_specs = (
        P("dp", None),
        P(None, None, "mp"),
        P("mp", None),
        P(None, "mp"),
        P("mp", None),
        P(),
        P("dp", None),
        P(None, None, "mp"),
        P("dp"),
        P("dp", None, None),
        P("dp", None),
        P("dp", None),
    )
    out_specs = (P("dp", None), P("dp", "mp"))
    return jax.shard_map(
        local, mesh=mesh, in_specs=in_specs, out_specs=out_specs, check_vma=False
    )
```

```python
import functools
import jax
import jax.numpy as jnp
from jax import lax
from jax.experimental import pallas as pl
from jax.experimental.pallas import tpu as pltpu
from jax.sharding import PartitionSpec as P

SEQ = 128
TILE = 128
DEG = 16
TPR = 6
HD = 64
GHD = 96

eps_norm = 1e-06
bf = jnp.bfloat16
f32 = jnp.float32

VMEM = pl.BlockSpec(memory_space=pltpu.VMEM)
SMEM = pl.BlockSpec(memory_space=pltpu.SMEM)
HBM = pl.BlockSpec(memory_space=pltpu.HBM)
PAD = 16
LANES = 128
NT = (((1,), (1,)), ((), ()))
TN = (((0,), (0,)), ((), ()))


def call(
    kernel,
    outs,
    args,
    smem=(),
    hbm=(),
    pieces=None,
    scalars=(),
    scratch=(),
    out_specs=None,
    flops=0,
    name=None,
):
    count, out_count, own = len(args), len(jax.tree.leaves(outs)), len(scratch)
    specs = [SMEM if i in smem else HBM if i in hbm else VMEM for i in range(count)]
    nbytes = sum(a.size * a.dtype.itemsize for a in args)
    space = [pltpu.SMEM if i in scalars else pltpu.VMEM for i in hbm]
    buffers = [kind(args[i].shape, args[i].dtype) for kind, i in zip(space, hbm)]
    spans = {i: (pieces or {}).get(i, ((0, args[i].shape[0]),)) for i in hbm}
    sems = [pltpu.SemaphoreType.DMA((len(spans[i]),)) for i in hbm]

    def body(*refs):
        ins, rest = list(refs[:count]), refs[count:]
        kept, moved = rest[: out_count + own], rest[out_count + own :]
        moves = {}
        for j, i in enumerate(hbm):
            moves[i] = []
            for k, (start, size) in enumerate(spans[i]):
                at = pl.ds(start, size)
                move = pltpu.make_async_copy(
                    ins[i].at[at], moved[j].at[at], moved[len(hbm) + j].at[k]
                )
                move.start()
                moves[i].append(move)
            ins[i] = moved[j]

        def ready(*wanted):
            for i in wanted:
                for move in moves[i]:
                    move.wait()

        kernel(ready, *ins, *kept)

    return pl.pallas_call(
        body,
        out_shape=outs,
        in_specs=specs,
        out_specs=jax.tree.map(lambda _: VMEM, outs) if out_specs is None else out_specs,
        scratch_shapes=list(scratch) + buffers + sems,
        compiler_params=pltpu.CompilerParams(vmem_limit_bytes=(60 if hbm else 40) * 1024 * 1024),
        cost_estimate=pl.CostEstimate(flops=flops, bytes_accessed=nbytes, transcendentals=0),
        name=name,
    )(*args)


def shape(dims, dtype):
    return jax.ShapeDtypeStruct(dims, dtype)


def dot(a, b):
    return jnp.dot(a, b, preferred_element_type=f32)


def dot_nt(a, b):
    return lax.dot_general(a, b, NT, preferred_element_type=f32)


def dot_tn(a, b):
    return lax.dot_general(a, b, TN, preferred_element_type=f32)


def layer_norm(values, gain):
    mean = jnp.mean(values, axis=-1, keepdims=True)
    centred = values - mean
    var = jnp.mean(centred * centred, axis=-1, keepdims=True)
    return centred * lax.rsqrt(var + eps_norm) * gain


def one_hot(picked, nodes):
    lanes = lax.broadcasted_iota(jnp.int32, (picked.shape[0], nodes), 1)
    return jnp.where(lanes == picked, 1.0, 0.0).astype(bf)


def mark(rows, picked, at_ref, step):
    per_part = at_ref.shape[0]
    code = jnp.full(picked.shape, -1, jnp.int32)
    for title in range(per_part):
        code = jnp.where(picked == at_ref[title], step * per_part + title, code)
    lead = lax.broadcasted_iota(jnp.int32, rows.shape, 1) == 0
    return jnp.where(code >= 0, jnp.where(lead, jnp.nan, code.astype(f32)), rows)


def send_kernel(ready, me_ref, at_ref, ids_ref, table_ref, w_ref, sent_ref, rows_ref, sems):
    cols = w_ref.shape[1]
    fetch, nodes = ids_ref.shape[1], table_ref.shape[0]
    ready(2)
    ids = ids_ref[...].astype(f32).T.astype(jnp.int32)
    ready(1, 3, 4)
    table = table_ref[...]
    kv = jnp.concatenate([dot_nt(table, w_ref[1]), dot_nt(table, w_ref[2])], axis=1).astype(bf)
    moves = []
    parts = ids.shape[1]
    group = min(parts, max(1, 1024 // fetch))
    for start in range(0, parts, group):
        picks = [ids[:, part : part + 1] for part in range(start, start + group)]
        rows = dot(one_hot(jnp.concatenate(picks, axis=0), nodes), kv)
        for j, picked in enumerate(picks):
            part = start + j
            mine = rows[j * fetch : (j + 1) * fetch]
            at = pl.ds(part * fetch, fetch)
            lead = mark(mine[:, :LANES], picked, at_ref, me_ref[0] ^ part)
            rows_ref[at, :LANES] = lead.astype(bf)
            rows_ref[at, LANES:] = mine[:, LANES:].astype(bf)
            move = pltpu.make_async_copy(rows_ref.at[at, :], sent_ref.at[at, :], sems.at[part])
            move.start()
            moves.append(move)
    for move in moves:
        move.wait()


def mask_kernel(ready, slots_ref, mask_ref):
    all_slots = slots_ref[...].astype(f32).T.astype(jnp.int32)
    for tile in range(all_slots.shape[0] // TILE):
        slots = all_slots[tile * TILE : (tile + 1) * TILE, :]
        lanes = lax.broadcasted_iota(jnp.int32, (TILE, TPR * TILE), 1)
        edges = lanes == lax.broadcasted_iota(jnp.int32, (TILE, TPR * TILE), 0)
        for edge in range(DEG):
            edges = edges | (lanes == slots[:, edge : edge + 1])
        mask_ref[tile * TILE : (tile + 1) * TILE, :] = jnp.where(edges, 1.0, 0.0).astype(bf)


def bias_kernel(ready, mask_ref, bias_ref):
    bias_ref[...] = jnp.where(mask_ref[...].astype(f32) > 0.5, 0.0, -jnp.inf)


def attn_kernel(ready, who_ref, titles_ref, w_in_ref, w_out_ref, *refs):
    outs, total = refs[:-1], refs[-1]
    titles = titles_ref[...]
    q = dot_nt(titles, w_in_ref[0]).astype(bf)
    k = dot_nt(titles, w_in_ref[1]).astype(bf)
    v = dot_nt(titles, w_in_ref[2]).astype(bf)
    cols = q.shape[1]
    heads = cols // HD
    lanes = lax.broadcasted_iota(jnp.int32, (SEQ, cols), 1) // HD
    for title in range(titles.shape[0] // SEQ):
        rows = slice(title * SEQ, (title + 1) * SEQ)
        qt, kt, vt = q[rows], k[rows], v[rows]
        stacked = jnp.concatenate(
            [jnp.where(lanes == h, qt, jnp.zeros_like(qt)) for h in range(heads)], axis=0
        )
        scores = dot_nt(stacked, kt) * (1.0 / HD**0.5)
        expo = jnp.exp(scores - jnp.max(scores, axis=-1, keepdims=True))
        probs = (expo / jnp.sum(expo, axis=-1, keepdims=True)).astype(bf)
        mixed = dot(probs, vt)
        context = mixed[:SEQ]
        for h in range(1, heads):
            context = jnp.where(lanes == h, mixed[h * SEQ : (h + 1) * SEQ], context)
        total[rows, :] = dot(context.astype(bf), w_out_ref[...])
    chunk = (outs[0].shape[0] - PAD) // 2
    firsts = first_rows(total)
    for out, pair in zip(outs, ((0, 2), (1, 3))):
        for j, step in enumerate(pair):
            at = pl.ds(pl.multiple_of((who_ref[0] ^ step) * chunk, chunk), chunk)
            out[j * chunk : (j + 1) * chunk, :] = total[at, :].astype(out.dtype)
        out[2 * chunk :, :] = firsts.astype(out.dtype)


def half_kernel(chunk, ready, kept_ref, came_ref, keep_ref, give_ref):
    total = kept_ref[...] + came_ref[...].astype(f32)
    keep_ref[:chunk, :] = total[:chunk]
    give_ref[:chunk, :] = total[chunk : 2 * chunk].astype(bf)
    if keep_ref.shape[0] > chunk:
        keep_ref[chunk:, :] = total[2 * chunk :]
        give_ref[chunk:, :] = total[2 * chunk :].astype(bf)


def first_rows(ref):
    sub = lax.broadcasted_iota(jnp.int32, (PAD, ref.shape[1]), 0)
    rows = jnp.zeros((PAD, ref.shape[1]), f32)
    for title in range(ref.shape[0] // SEQ):
        row = ref[title * SEQ : title * SEQ + 1, :].astype(f32)
        rows = jnp.where(sub == title, row, rows)
    return rows


def norm_one_kernel(
    ready, who_ref, titles_ref, gains_ref, w_in_ref, w_out_ref, own_ref, *refs
):
    *parts, out, first_hidden, first_terms = refs
    chunk = own_ref.shape[0] - PAD
    total = own_ref[...]
    for part in parts:
        total = total + part[...].astype(f32)
    at = pl.ds(pl.multiple_of(who_ref[0] * chunk, chunk), chunk)
    base = jnp.concatenate([titles_ref[at, :].astype(f32), first_rows(titles_ref)], axis=0)
    hidden = layer_norm(base + total, gains_ref[0:1, :]).astype(bf)
    out[:chunk, :] = hidden[:chunk]
    firsts = hidden[chunk:]
    first_hidden[...] = firsts
    terms = dot(gelu(dot(firsts, w_in_ref[...])).astype(bf), w_out_ref[...])
    first_terms[...] = terms
    out[chunk:, :] = terms.astype(bf)


def gelu(x):
    return 0.5 * x * (1.0 + lax.erf(x * (0.5**0.5)))


def ffn_kernel(ready, w_in_ref, w_out_ref, gains_ref, first_hidden, first_terms, *refs):
    *ins, kept, sent, first = refs
    chunk = kept.shape[0] // 2
    hidden = jnp.concatenate([ref[:chunk, :] for ref in ins], axis=0)
    inner = gelu(dot(hidden, w_in_ref[...])).astype(bf)
    total = dot(inner, w_out_ref[...])
    kept[...] = total[: 2 * chunk]
    sent[...] = total[2 * chunk :].astype(bf)
    terms = first_terms[...]
    for ref in ins[1:]:
        terms = terms + ref[chunk:, :].astype(f32)
    done = layer_norm(first_hidden[...].astype(f32) + terms, gains_ref[1:2, :])
    first[...] = done[: first.shape[0]].astype(bf)


def norm_two_kernel(ready, hidden_ref, gains_ref, own_ref, *refs):
    *parts, out = refs
    total = own_ref[...]
    for part in parts:
        total = total + part[...].astype(f32)
    hidden = hidden_ref[: out.shape[0], :].astype(f32)
    out[...] = layer_norm(hidden + total, gains_ref[1:2, :]).astype(bf)


def pack_kernel(ready, *refs):
    *parts, out = refs
    per_part = parts[0].shape[0]
    sub = lax.broadcasted_iota(jnp.int32, out.shape, 0)
    rows = jnp.zeros(out.shape, f32)
    for turn, ref in enumerate(parts):
        for title in range(per_part):
            row = ref[title : title + 1, :].astype(f32)
            rows = jnp.where(sub == turn * per_part + title, row, rows)
    out[...] = rows.astype(bf)


def own_kernel(ready, table_ref, w_ref, kv_ref, q_ref):
    cols = w_ref.shape[1]
    table = table_ref[...]
    kv_ref[:, :cols] = dot_nt(table, w_ref[1]).astype(bf)
    kv_ref[:, cols:] = dot_nt(table, w_ref[2]).astype(bf)
    q_ref[...] = dot_nt(table, w_ref[0]).astype(bf)


def tail_rows(count):
    return -(-count // PAD) * PAD


def graph_kernel(
    whose, ready, who_ref, cols_ref, at_ref, q_ref, kv_ref, w_ref, bias_ref, far_ref, first_ref, *refs
):
    *packs, out_ref, encoded_ref, k_all, v_all, firsts = refs
    dones, packs = packs[: len(whose)], packs[len(whose) :]
    chunk = dones[0].shape[0]
    for step, ref in zip(whose, dones):
        at = pl.multiple_of((who_ref[0] ^ step) * chunk, chunk)
        encoded_ref[pl.ds(at, chunk), :] = ref[...]
    nodes, cols = q_ref.shape
    row_tiles = nodes // TILE
    per_part = first_ref.shape[0]
    members = len(packs)
    for step, ref in enumerate(packs):
        rows = ref[...].astype(f32)
        for turn in range(firsts.shape[0] // per_part // members):
            for title in range(per_part):
                place = (turn * members + lax.rem(who_ref[0] ^ step, members)) * per_part + title
                at = turn * per_part + title
                firsts[pl.ds(place, 1), :] = rows[at : at + 1]
    firsts[0:per_part, :] = first_ref[...].astype(f32)
    first = firsts[...].astype(bf)
    first_kv = jnp.concatenate([dot_nt(first, w_ref[1]), dot_nt(first, w_ref[2])], axis=1).astype(bf)
    first_q = dot_nt(first, w_ref[0])
    for tile in range(row_tiles):
        span = slice(tile * TILE, (tile + 1) * TILE)
        rows = kv_ref[span, :].astype(f32)
        sub = lax.broadcasted_iota(jnp.int32, (TILE, 2 * cols), 0) + tile * TILE
        for title in range(per_part):
            row = first_kv[title : title + 1].astype(f32)
            rows = jnp.where(sub == at_ref[title], row, rows)
        rows = rows.astype(bf)
        k_all[span, :] = rows[:, :cols]
        v_all[span, :] = rows[:, cols:]
    lanes = lax.broadcasted_iota(jnp.int32, (TILE, first_kv.shape[0]), 1).astype(f32)
    for tile in range(far_ref.shape[0] // TILE):
        rows = far_ref[tile * TILE : (tile + 1) * TILE, :].astype(f32)
        code = jnp.where(rows[:, 0:1] != rows[:, 0:1], rows[:, 1:2], -1.0)
        hot = jnp.where(lanes == code, 1.0, 0.0).astype(bf)
        fixed = jnp.where(code >= 0.0, dot(hot, first_kv), rows).astype(bf)
        span = slice(nodes + tile * TILE, nodes + (tile + 1) * TILE)
        k_all[span, :] = fixed[:, :cols]
        v_all[span, :] = fixed[:, cols:]

    heads = cols // GHD
    head_of = lax.broadcasted_iota(jnp.int32, (TILE, cols), 1) // GHD
    for tile in range(row_tiles):
        q = q_ref[tile * TILE : (tile + 1) * TILE, :].astype(f32)
        sub = lax.broadcasted_iota(jnp.int32, (TILE, cols), 0) + tile * TILE
        for title in range(per_part):
            q = jnp.where(sub == at_ref[title], first_q[title : title + 1], q)
        q = q.astype(bf)
        stacked = jnp.concatenate(
            [jnp.where(head_of == h, q, jnp.zeros_like(q)) for h in range(heads)], axis=0
        )
        starts = [pl.multiple_of(cols_ref[tile, c] * TILE, TILE) for c in range(TPR)]
        keys = jnp.concatenate([k_all[pl.ds(start, TILE), :] for start in starts], axis=0)
        values = jnp.concatenate([v_all[pl.ds(start, TILE), :] for start in starts], axis=0)
        scores = dot_nt(stacked, keys) * (1.0 / GHD**0.5)
        bias = bias_ref[tile * TILE : (tile + 1) * TILE, :]
        masked = scores + jnp.concatenate([bias] * heads, axis=0)
        expo = jnp.exp(masked - jnp.max(masked, axis=-1, keepdims=True))
        scale = 1.0 / jnp.sum(expo, axis=-1, keepdims=True)
        mixed = dot(expo.astype(bf), values) * scale
        out = mixed[:TILE]
        for h in range(1, heads):
            out = jnp.where(head_of == h, mixed[h * TILE : (h + 1) * TILE], out)
        out_ref[:, tile * TILE : (tile + 1) * TILE] = out.T.astype(bf)


def local(

    titles,
    w_attn_in,
    w_attn_out,
    w_ffn_in,
    w_ffn_out,
    gains,
    node_table,
    w_graph,
    title_nodes,
    send_ids,
    tile_cols,
    nbr_slots,
):
    tok_rows, width = titles.shape
    nodes = node_table.shape[0]
    cols = w_graph.shape[2]
    mp = lax.axis_size("mp")
    dp = lax.axis_size("dp")
    me_mp = lax.axis_index("mp").astype(jnp.int32)
    me_dp = lax.axis_index("dp").astype(jnp.int32)
    me, who = me_dp.reshape(1), me_mp.reshape(1)
    chunk = tok_rows // mp
    per_part = title_nodes.shape[0]
    fetch = send_ids.shape[2]

    def swap(value, step, axis="mp"):
        return lax.ppermute(value, axis, [(i, i ^ step) for i in range(lax.axis_size(axis))])

    def gather(value):
        whose, blocks, step = [0], [value], mp // 2
        while step:
            blocks = blocks + [swap(block, step) for block in blocks]
            whose = whose + [other ^ step for other in whose]
            step //= 2
        return whose, blocks

    def halves(kept, came, pad):
        dims = (chunk + pad, width)
        return call(
            functools.partial(half_kernel, chunk),
            (shape(dims, f32), shape(dims, bf)),
            (kept, came),
            name="half",
        )

    w_attn_in = jnp.swapaxes(w_attn_in, 1, 2)
    w_graph = jnp.swapaxes(w_graph, 1, 2)
    sent = call(
        send_kernel,
        shape((dp * fetch, 2 * cols), bf),
        (me, title_nodes, send_ids[0], node_table, w_graph),
        smem=(0,),
        hbm=(2, 3, 4, 1),
        pieces={3: [(i, nodes // 4) for i in range(0, nodes, nodes // 4)], 4: [(1, 1), (2, 1)]},
        scalars=(1,),
        out_specs=HBM,
        scratch=[pltpu.VMEM((dp * fetch, 2 * cols), bf), pltpu.SemaphoreType.DMA((dp,))],
        flops=2 * nodes * width * 2 * cols + 2 * dp * fetch * nodes * 2 * cols,
        name="send",
    )
    far = lax.all_to_all(
        sent.reshape(dp, fetch, 2 * cols), "dp", split_axis=0, concat_axis=0, tiled=True
    ).reshape(dp * fetch, 2 * cols)
    titles, _ = lax.optimization_barrier((titles, sent))

    kept, given = call(
        attn_kernel,
        (shape((2 * chunk + PAD, width), f32), shape((2 * chunk + PAD, width), bf)),
        (who, titles, w_attn_in, w_attn_out),
        smem=(0,),
        scratch=[pltpu.VMEM((tok_rows, width), f32)],
        flops=2 * tok_rows * width * 4 * w_attn_in.shape[1],
        name="attn",
    )
    keep, give = halves(kept, swap(given, 1), PAD)
    part = swap(give, 2)
    kv, q = call(
        own_kernel,
        (shape((nodes, 2 * cols), bf), shape((nodes, cols), bf)),
        (node_table, w_graph),
        flops=2 * 10**9,
        name="own",
    )
    part, kv, q = lax.optimization_barrier((part, kv, q))
    hidden, first_hidden, first_terms = call(
        norm_one_kernel,
        (shape((chunk + PAD, width), bf), shape((PAD, width), bf), shape((PAD, width), f32)),
        (who, titles, gains, w_ffn_in, w_ffn_out, keep, part),
        smem=(0,),
        name="norm_one",
    )
    whose, hiddens = gather(hidden)
    kept, given, first = call(
        ffn_kernel,
        (
            shape((2 * chunk, width), f32),
            shape((2 * chunk, width), bf),
            shape((per_part, width), bf),
        ),
        (w_ffn_in, w_ffn_out, gains, first_hidden, first_terms, *hiddens),
        flops=4 * tok_rows * width * w_ffn_in.shape[1],
        name="ffn",
    )
    pair = 2
    turns = dp // pair
    firsts = [
        lax.ppermute(
            first,
            ("dp", "mp"),
            [
                (p * mp + m, (p ^ (turn * pair + m % pair)) * mp + m)
                for p in range(dp)
                for m in range(mp)
                if turn or m % pair
            ],
        )
        for turn in range(turns)
    ]
    keep, give = halves(kept, swap(given, 1), 0)
    give, slots = lax.optimization_barrier((give, nbr_slots))
    part = swap(give, 2)
    mask = call(
        mask_kernel, shape((nodes, TPR * TILE), bf), (slots.T,), flops=4 * 10**9, name="mask"
    )
    part, mask = lax.optimization_barrier((part, mask))
    done = call(
        norm_two_kernel, shape((chunk, width), bf), (hidden, gains, keep, part), name="norm_two"
    )
    across = swap(done, 2)
    across, firsts, far = lax.optimization_barrier((across, firsts, far))
    pack = call(pack_kernel, shape((tail_rows(turns * per_part), width), bf), firsts, name="pack")
    mask, pack = lax.optimization_barrier((mask, pack))
    packs = [pack, swap(pack, 1)]
    bias = call(bias_kernel, shape(mask.shape, f32), (mask,), flops=10**9, name="bias")
    dones = [done, across, swap(done, 1), swap(across, 1)]
    keys = nodes + dp * fetch
    graph_out, encoded = call(
        functools.partial(graph_kernel, whose),
        (shape((cols, nodes), bf), shape((tok_rows, width), bf)),
        (who, tile_cols, title_nodes, q, kv, w_graph, bias, far, first, *dones, *packs),
        smem=(0, 1, 2),
        scratch=[
            pltpu.VMEM((keys, cols), bf),
            pltpu.VMEM((keys, cols), bf),
            pltpu.VMEM((dp * per_part, width), f32),
        ],
        flops=4 * 10**9,
        name="graph",
    )
    return (encoded, graph_out.T)


def solution(mesh):
    in_specs = (
        P("dp", None),
        P(None, None, "mp"),
        P("mp", None),
        P(None, "mp"),
        P("mp", None),
        P(),
        P("dp", None),
        P(None, None, "mp"),
        P("dp"),
        P("dp", None, None),
        P("dp", None),
        P("dp", None),
    )
    out_specs = (P("dp", None), P("dp", "mp"))
    return jax.shard_map(
        local, mesh=mesh, in_specs=in_specs, out_specs=out_specs, check_vma=False
    )
```

```python
import functools
import jax
import jax.numpy as jnp
from jax import lax
from jax.experimental import pallas as pl
from jax.experimental.pallas import tpu as pltpu
from jax.sharding import PartitionSpec as P

SEQ = 128
TILE = 128
DEG = 16
TPR = 6
HD = 64
GHD = 96

eps_norm = 1e-06
bf = jnp.bfloat16
f32 = jnp.float32

VMEM = pl.BlockSpec(memory_space=pltpu.VMEM)
SMEM = pl.BlockSpec(memory_space=pltpu.SMEM)
HBM = pl.BlockSpec(memory_space=pltpu.HBM)
PAD = 16
LANES = 128
NT = (((1,), (1,)), ((), ()))
TN = (((0,), (0,)), ((), ()))


def call(
    kernel,
    outs,
    args,
    smem=(),
    hbm=(),
    pieces=None,
    scalars=(),
    scratch=(),
    out_specs=None,
    flops=0,
    name=None,
):
    count, out_count, own = len(args), len(jax.tree.leaves(outs)), len(scratch)
    specs = [SMEM if i in smem else HBM if i in hbm else VMEM for i in range(count)]
    nbytes = sum(a.size * a.dtype.itemsize for a in args)
    space = [pltpu.SMEM if i in scalars else pltpu.VMEM for i in hbm]
    buffers = [kind(args[i].shape, args[i].dtype) for kind, i in zip(space, hbm)]
    spans = {i: (pieces or {}).get(i, ((0, args[i].shape[0]),)) for i in hbm}
    sems = [pltpu.SemaphoreType.DMA((len(spans[i]),)) for i in hbm]

    def body(*refs):
        ins, rest = list(refs[:count]), refs[count:]
        kept, moved = rest[: out_count + own], rest[out_count + own :]
        moves = {}
        for j, i in enumerate(hbm):
            moves[i] = []
            for k, (start, size) in enumerate(spans[i]):
                at = pl.ds(start, size)
                move = pltpu.make_async_copy(
                    ins[i].at[at], moved[j].at[at], moved[len(hbm) + j].at[k]
                )
                move.start()
                moves[i].append(move)
            ins[i] = moved[j]

        def ready(*wanted):
            for i in wanted:
                for move in moves[i]:
                    move.wait()

        kernel(ready, *ins, *kept)

    return pl.pallas_call(
        body,
        out_shape=outs,
        in_specs=specs,
        out_specs=jax.tree.map(lambda _: VMEM, outs) if out_specs is None else out_specs,
        scratch_shapes=list(scratch) + buffers + sems,
        compiler_params=pltpu.CompilerParams(vmem_limit_bytes=(60 if hbm else 40) * 1024 * 1024),
        cost_estimate=pl.CostEstimate(flops=flops, bytes_accessed=nbytes, transcendentals=0),
        name=name,
    )(*args)


def shape(dims, dtype):
    return jax.ShapeDtypeStruct(dims, dtype)


def dot(a, b):
    return jnp.dot(a, b, preferred_element_type=f32)


def dot_nt(a, b):
    return lax.dot_general(a, b, NT, preferred_element_type=f32)


def dot_tn(a, b):
    return lax.dot_general(a, b, TN, preferred_element_type=f32)


def layer_norm(values, gain):
    mean = jnp.mean(values, axis=-1, keepdims=True)
    centred = values - mean
    var = jnp.mean(centred * centred, axis=-1, keepdims=True)
    return centred * lax.rsqrt(var + eps_norm) * gain


def one_hot(picked, nodes):
    lanes = lax.broadcasted_iota(jnp.int32, (picked.shape[0], nodes), 1)
    return jnp.where(lanes == picked, 1.0, 0.0).astype(bf)


def mark(rows, picked, at_ref, step):
    per_part = at_ref.shape[0]
    code = jnp.full(picked.shape, -1, jnp.int32)
    for title in range(per_part):
        code = jnp.where(picked == at_ref[title], step * per_part + title, code)
    lead = lax.broadcasted_iota(jnp.int32, rows.shape, 1) == 0
    return jnp.where(code >= 0, jnp.where(lead, jnp.nan, code.astype(f32)), rows)


def send_kernel(ready, me_ref, at_ref, ids_ref, table_ref, w_ref, sent_ref, rows_ref, sems):
    cols = w_ref.shape[1]
    fetch, nodes = ids_ref.shape[1], table_ref.shape[0]
    ready(2)
    ids = ids_ref[...].astype(f32).T.astype(jnp.int32)
    ready(1, 3, 4)
    table = table_ref[...]
    kv = jnp.concatenate([dot_nt(table, w_ref[1]), dot_nt(table, w_ref[2])], axis=1).astype(bf)
    moves = []
    parts = ids.shape[1]
    group = min(parts, max(1, 512 // fetch))
    for start in range(0, parts, group):
        picks = [ids[:, part : part + 1] for part in range(start, start + group)]
        rows = dot(one_hot(jnp.concatenate(picks, axis=0), nodes), kv)
        for j, picked in enumerate(picks):
            part = start + j
            mine = rows[j * fetch : (j + 1) * fetch]
            at = pl.ds(part * fetch, fetch)
            lead = mark(mine[:, :LANES], picked, at_ref, me_ref[0] ^ part)
            rows_ref[at, :LANES] = lead.astype(bf)
            rows_ref[at, LANES:] = mine[:, LANES:].astype(bf)
            move = pltpu.make_async_copy(rows_ref.at[at, :], sent_ref.at[at, :], sems.at[part])
            move.start()
            moves.append(move)
    for move in moves:
        move.wait()


def mask_kernel(ready, slots_ref, mask_ref):
    all_slots = slots_ref[...].astype(f32).T.astype(jnp.int32)
    for tile in range(all_slots.shape[0] // TILE):
        slots = all_slots[tile * TILE : (tile + 1) * TILE, :]
        lanes = lax.broadcasted_iota(jnp.int32, (TILE, TPR * TILE), 1)
        edges = lanes == lax.broadcasted_iota(jnp.int32, (TILE, TPR * TILE), 0)
        for edge in range(DEG):
            edges = edges | (lanes == slots[:, edge : edge + 1])
        mask_ref[tile * TILE : (tile + 1) * TILE, :] = jnp.where(edges, 1.0, 0.0).astype(bf)


def bias_kernel(ready, mask_ref, bias_ref):
    bias_ref[...] = jnp.where(mask_ref[...].astype(f32) > 0.5, 0.0, -jnp.inf)


def attn_kernel(ready, who_ref, titles_ref, w_in_ref, w_out_ref, *refs):
    outs, total = refs[:-1], refs[-1]
    titles = titles_ref[...]
    q = dot_nt(titles, w_in_ref[0]).astype(bf)
    k = dot_nt(titles, w_in_ref[1]).astype(bf)
    v = dot_nt(titles, w_in_ref[2]).astype(bf)
    cols = q.shape[1]
    heads = cols // HD
    lanes = lax.broadcasted_iota(jnp.int32, (SEQ, cols), 1) // HD
    for title in range(titles.shape[0] // SEQ):
        rows = slice(title * SEQ, (title + 1) * SEQ)
        qt, kt, vt = q[rows], k[rows], v[rows]
        stacked = jnp.concatenate(
            [jnp.where(lanes == h, qt, jnp.zeros_like(qt)) for h in range(heads)], axis=0
        )
        scores = dot_nt(stacked, kt) * (1.0 / HD**0.5)
        expo = jnp.exp(scores - jnp.max(scores, axis=-1, keepdims=True))
        probs = (expo / jnp.sum(expo, axis=-1, keepdims=True)).astype(bf)
        mixed = dot(probs, vt)
        context = mixed[:SEQ]
        for h in range(1, heads):
            context = jnp.where(lanes == h, mixed[h * SEQ : (h + 1) * SEQ], context)
        total[rows, :] = dot(context.astype(bf), w_out_ref[...])
    chunk = (outs[0].shape[0] - PAD) // 2
    firsts = first_rows(total)
    for out, pair in zip(outs, ((0, 2), (1, 3))):
        for j, step in enumerate(pair):
            at = pl.ds(pl.multiple_of((who_ref[0] ^ step) * chunk, chunk), chunk)
            out[j * chunk : (j + 1) * chunk, :] = total[at, :].astype(out.dtype)
        out[2 * chunk :, :] = firsts.astype(out.dtype)


def half_kernel(chunk, ready, kept_ref, came_ref, keep_ref, give_ref):
    total = kept_ref[...] + came_ref[...].astype(f32)
    keep_ref[:chunk, :] = total[:chunk]
    give_ref[:chunk, :] = total[chunk : 2 * chunk].astype(bf)
    if keep_ref.shape[0] > chunk:
        keep_ref[chunk:, :] = total[2 * chunk :]
        give_ref[chunk:, :] = total[2 * chunk :].astype(bf)


def first_rows(ref):
    sub = lax.broadcasted_iota(jnp.int32, (PAD, ref.shape[1]), 0)
    rows = jnp.zeros((PAD, ref.shape[1]), f32)
    for title in range(ref.shape[0] // SEQ):
        row = ref[title * SEQ : title * SEQ + 1, :].astype(f32)
        rows = jnp.where(sub == title, row, rows)
    return rows


def norm_one_kernel(
    ready, who_ref, titles_ref, gains_ref, w_in_ref, w_out_ref, own_ref, *refs
):
    *parts, out, first_hidden, first_terms = refs
    chunk = own_ref.shape[0] - PAD
    total = own_ref[...]
    for part in parts:
        total = total + part[...].astype(f32)
    at = pl.ds(pl.multiple_of(who_ref[0] * chunk, chunk), chunk)
    base = jnp.concatenate([titles_ref[at, :].astype(f32), first_rows(titles_ref)], axis=0)
    hidden = layer_norm(base + total, gains_ref[0:1, :]).astype(bf)
    out[:chunk, :] = hidden[:chunk]
    firsts = hidden[chunk:]
    first_hidden[...] = firsts
    terms = dot(gelu(dot(firsts, w_in_ref[...])).astype(bf), w_out_ref[...])
    first_terms[...] = terms
    out[chunk:, :] = terms.astype(bf)


def gelu(x):
    return 0.5 * x * (1.0 + lax.erf(x * (0.5**0.5)))


def ffn_kernel(ready, w_in_ref, w_out_ref, gains_ref, first_hidden, first_terms, *refs):
    *ins, kept, sent, first = refs
    chunk = kept.shape[0] // 2
    hidden = jnp.concatenate([ref[:chunk, :] for ref in ins], axis=0)
    inner = gelu(dot(hidden, w_in_ref[...])).astype(bf)
    total = dot(inner, w_out_ref[...])
    kept[...] = total[: 2 * chunk]
    sent[...] = total[2 * chunk :].astype(bf)
    terms = first_terms[...]
    for ref in ins[1:]:
        terms = terms + ref[chunk:, :].astype(f32)
    done = layer_norm(first_hidden[...].astype(f32) + terms, gains_ref[1:2, :])
    first[...] = done[: first.shape[0]].astype(bf)


def norm_two_kernel(ready, hidden_ref, gains_ref, own_ref, *refs):
    *parts, out = refs
    total = own_ref[...]
    for part in parts:
        total = total + part[...].astype(f32)
    hidden = hidden_ref[: out.shape[0], :].astype(f32)
    out[...] = layer_norm(hidden + total, gains_ref[1:2, :]).astype(bf)


def pack_kernel(ready, *refs):
    *parts, out = refs
    per_part = parts[0].shape[0]
    sub = lax.broadcasted_iota(jnp.int32, out.shape, 0)
    rows = jnp.zeros(out.shape, f32)
    for turn, ref in enumerate(parts):
        for title in range(per_part):
            row = ref[title : title + 1, :].astype(f32)
            rows = jnp.where(sub == turn * per_part + title, row, rows)
    out[...] = rows.astype(bf)


def own_kernel(ready, table_ref, w_ref, kv_ref, q_ref):
    cols = w_ref.shape[1]
    table = table_ref[...]
    kv_ref[:, :cols] = dot_nt(table, w_ref[1]).astype(bf)
    kv_ref[:, cols:] = dot_nt(table, w_ref[2]).astype(bf)
    q_ref[...] = dot_nt(table, w_ref[0]).astype(bf)


def tail_rows(count):
    return -(-count // PAD) * PAD


def graph_kernel(
    whose, ready, who_ref, cols_ref, at_ref, q_ref, kv_ref, w_ref, bias_ref, far_ref, first_ref, *refs
):
    *packs, out_ref, encoded_ref, k_all, v_all, firsts = refs
    dones, packs = packs[: len(whose)], packs[len(whose) :]
    chunk = dones[0].shape[0]
    for step, ref in zip(whose, dones):
        at = pl.multiple_of((who_ref[0] ^ step) * chunk, chunk)
        encoded_ref[pl.ds(at, chunk), :] = ref[...]
    nodes, cols = q_ref.shape
    row_tiles = nodes // TILE
    per_part = first_ref.shape[0]
    members = len(packs)
    for step, ref in enumerate(packs):
        rows = ref[...].astype(f32)
        for turn in range(firsts.shape[0] // per_part // members):
            for title in range(per_part):
                place = (turn * members + lax.rem(who_ref[0] ^ step, members)) * per_part + title
                at = turn * per_part + title
                firsts[pl.ds(place, 1), :] = rows[at : at + 1]
    firsts[0:per_part, :] = first_ref[...].astype(f32)
    first = firsts[...].astype(bf)
    first_kv = jnp.concatenate([dot_nt(first, w_ref[1]), dot_nt(first, w_ref[2])], axis=1).astype(bf)
    first_q = dot_nt(first, w_ref[0])
    for tile in range(row_tiles):
        span = slice(tile * TILE, (tile + 1) * TILE)
        rows = kv_ref[span, :].astype(f32)
        sub = lax.broadcasted_iota(jnp.int32, (TILE, 2 * cols), 0) + tile * TILE
        for title in range(per_part):
            row = first_kv[title : title + 1].astype(f32)
            rows = jnp.where(sub == at_ref[title], row, rows)
        rows = rows.astype(bf)
        k_all[span, :] = rows[:, :cols]
        v_all[span, :] = rows[:, cols:]
    lanes = lax.broadcasted_iota(jnp.int32, (TILE, first_kv.shape[0]), 1).astype(f32)
    for tile in range(far_ref.shape[0] // TILE):
        rows = far_ref[tile * TILE : (tile + 1) * TILE, :].astype(f32)
        code = jnp.where(rows[:, 0:1] != rows[:, 0:1], rows[:, 1:2], -1.0)
        hot = jnp.where(lanes == code, 1.0, 0.0).astype(bf)
        fixed = jnp.where(code >= 0.0, dot(hot, first_kv), rows).astype(bf)
        span = slice(nodes + tile * TILE, nodes + (tile + 1) * TILE)
        k_all[span, :] = fixed[:, :cols]
        v_all[span, :] = fixed[:, cols:]

    heads = cols // GHD
    head_of = lax.broadcasted_iota(jnp.int32, (TILE, cols), 1) // GHD
    for tile in range(row_tiles):
        q = q_ref[tile * TILE : (tile + 1) * TILE, :].astype(f32)
        sub = lax.broadcasted_iota(jnp.int32, (TILE, cols), 0) + tile * TILE
        for title in range(per_part):
            q = jnp.where(sub == at_ref[title], first_q[title : title + 1], q)
        q = q.astype(bf)
        stacked = jnp.concatenate(
            [jnp.where(head_of == h, q, jnp.zeros_like(q)) for h in range(heads)], axis=0
        )
        starts = [pl.multiple_of(cols_ref[tile, c] * TILE, TILE) for c in range(TPR)]
        keys = jnp.concatenate([k_all[pl.ds(start, TILE), :] for start in starts], axis=0)
        values = jnp.concatenate([v_all[pl.ds(start, TILE), :] for start in starts], axis=0)
        scores = dot_nt(stacked, keys) * (1.0 / GHD**0.5)
        bias = bias_ref[tile * TILE : (tile + 1) * TILE, :]
        masked = scores + jnp.concatenate([bias] * heads, axis=0)
        expo = jnp.exp(masked - jnp.max(masked, axis=-1, keepdims=True))
        scale = 1.0 / jnp.sum(expo, axis=-1, keepdims=True)
        mixed = dot(expo.astype(bf), values) * scale
        out = mixed[:TILE]
        for h in range(1, heads):
            out = jnp.where(head_of == h, mixed[h * TILE : (h + 1) * TILE], out)
        out_ref[:, tile * TILE : (tile + 1) * TILE] = out.T.astype(bf)


def local(

    titles,
    w_attn_in,
    w_attn_out,
    w_ffn_in,
    w_ffn_out,
    gains,
    node_table,
    w_graph,
    title_nodes,
    send_ids,
    tile_cols,
    nbr_slots,
):
    tok_rows, width = titles.shape
    nodes = node_table.shape[0]
    cols = w_graph.shape[2]
    mp = lax.axis_size("mp")
    dp = lax.axis_size("dp")
    me_mp = lax.axis_index("mp").astype(jnp.int32)
    me_dp = lax.axis_index("dp").astype(jnp.int32)
    me, who = me_dp.reshape(1), me_mp.reshape(1)
    chunk = tok_rows // mp
    per_part = title_nodes.shape[0]
    fetch = send_ids.shape[2]

    def swap(value, step, axis="mp"):
        return lax.ppermute(value, axis, [(i, i ^ step) for i in range(lax.axis_size(axis))])

    def gather(value):
        whose, blocks, step = [0], [value], mp // 2
        while step:
            blocks = blocks + [swap(block, step) for block in blocks]
            whose = whose + [other ^ step for other in whose]
            step //= 2
        return whose, blocks

    def halves(kept, came, pad):
        dims = (chunk + pad, width)
        return call(
            functools.partial(half_kernel, chunk),
            (shape(dims, f32), shape(dims, bf)),
            (kept, came),
            name="half",
        )

    w_attn_in = jnp.swapaxes(w_attn_in, 1, 2)
    w_graph = jnp.swapaxes(w_graph, 1, 2)
    sent = call(
        send_kernel,
        shape((dp * fetch, 2 * cols), bf),
        (me, title_nodes, send_ids[0], node_table, w_graph),
        smem=(0,),
        hbm=(2, 3, 4, 1),
        pieces={3: [(i, nodes // 4) for i in range(0, nodes, nodes // 4)], 4: [(1, 1), (2, 1)]},
        scalars=(1,),
        out_specs=HBM,
        scratch=[pltpu.VMEM((dp * fetch, 2 * cols), bf), pltpu.SemaphoreType.DMA((dp,))],
        flops=2 * nodes * width * 2 * cols + 2 * dp * fetch * nodes * 2 * cols,
        name="send",
    )
    far = lax.all_to_all(
        sent.reshape(dp, fetch, 2 * cols), "dp", split_axis=0, concat_axis=0, tiled=True
    ).reshape(dp * fetch, 2 * cols)
    titles, _ = lax.optimization_barrier((titles, sent))

    kept, given = call(
        attn_kernel,
        (shape((2 * chunk + PAD, width), f32), shape((2 * chunk + PAD, width), bf)),
        (who, titles, w_attn_in, w_attn_out),
        smem=(0,),
        scratch=[pltpu.VMEM((tok_rows, width), f32)],
        flops=2 * tok_rows * width * 4 * w_attn_in.shape[1],
        name="attn",
    )
    keep, give = halves(kept, swap(given, 1), PAD)
    part = swap(give, 2)
    kv, q = call(
        own_kernel,
        (shape((nodes, 2 * cols), bf), shape((nodes, cols), bf)),
        (node_table, w_graph),
        flops=2 * 10**9,
        name="own",
    )
    part, kv, q = lax.optimization_barrier((part, kv, q))
    hidden, first_hidden, first_terms = call(
        norm_one_kernel,
        (shape((chunk + PAD, width), bf), shape((PAD, width), bf), shape((PAD, width), f32)),
        (who, titles, gains, w_ffn_in, w_ffn_out, keep, part),
        smem=(0,),
        name="norm_one",
    )
    whose, hiddens = gather(hidden)
    kept, given, first = call(
        ffn_kernel,
        (
            shape((2 * chunk, width), f32),
            shape((2 * chunk, width), bf),
            shape((per_part, width), bf),
        ),
        (w_ffn_in, w_ffn_out, gains, first_hidden, first_terms, *hiddens),
        flops=4 * tok_rows * width * w_ffn_in.shape[1],
        name="ffn",
    )
    pair = 2
    turns = dp // pair
    firsts = [
        lax.ppermute(
            first,
            ("dp", "mp"),
            [
                (p * mp + m, (p ^ (turn * pair + m % pair)) * mp + m)
                for p in range(dp)
                for m in range(mp)
                if turn or m % pair
            ],
        )
        for turn in range(turns)
    ]
    keep, give = halves(kept, swap(given, 1), 0)
    give, slots = lax.optimization_barrier((give, nbr_slots))
    part = swap(give, 2)
    mask = call(
        mask_kernel, shape((nodes, TPR * TILE), bf), (slots.T,), flops=4 * 10**9, name="mask"
    )
    part, mask = lax.optimization_barrier((part, mask))
    done = call(
        norm_two_kernel, shape((chunk, width), bf), (hidden, gains, keep, part), name="norm_two"
    )
    across = swap(done, 2)
    across, firsts, far = lax.optimization_barrier((across, firsts, far))
    pack = call(pack_kernel, shape((tail_rows(turns * per_part), width), bf), firsts, name="pack")
    mask, pack, across = lax.optimization_barrier((mask, pack, across))
    packs = [pack, swap(pack, 1)]
    bias = call(bias_kernel, shape(mask.shape, f32), (mask,), flops=10**9, name="bias")
    dones = [done, across, swap(done, 1), swap(across, 1)]
    keys = nodes + dp * fetch
    graph_out, encoded = call(
        functools.partial(graph_kernel, whose),
        (shape((cols, nodes), bf), shape((tok_rows, width), bf)),
        (who, tile_cols, title_nodes, q, kv, w_graph, bias, far, first, *dones, *packs),
        smem=(0, 1, 2),
        scratch=[
            pltpu.VMEM((keys, cols), bf),
            pltpu.VMEM((keys, cols), bf),
            pltpu.VMEM((dp * per_part, width), f32),
        ],
        flops=4 * 10**9,
        name="graph",
    )
    return (encoded, graph_out.T)


def solution(mesh):
    in_specs = (
        P("dp", None),
        P(None, None, "mp"),
        P("mp", None),
        P(None, "mp"),
        P("mp", None),
        P(),
        P("dp", None),
        P(None, None, "mp"),
        P("dp"),
        P("dp", None, None),
        P("dp", None),
        P("dp", None),
    )
    out_specs = (P("dp", None), P("dp", "mp"))
    return jax.shard_map(
        local, mesh=mesh, in_specs=in_specs, out_specs=out_specs, check_vma=False
    )
```

```python
import functools
import jax
import jax.numpy as jnp
from jax import lax
from jax.experimental import pallas as pl
from jax.experimental.pallas import tpu as pltpu
from jax.sharding import PartitionSpec as P

SEQ = 128
TILE = 128
DEG = 16
TPR = 6
HD = 64
GHD = 96

eps_norm = 1e-06
bf = jnp.bfloat16
f32 = jnp.float32

VMEM = pl.BlockSpec(memory_space=pltpu.VMEM)
SMEM = pl.BlockSpec(memory_space=pltpu.SMEM)
HBM = pl.BlockSpec(memory_space=pltpu.HBM)
PAD = 16
LANES = 128
FIX = 256
NT = (((1,), (1,)), ((), ()))
TN = (((0,), (0,)), ((), ()))


def call(
    kernel,
    outs,
    args,
    smem=(),
    hbm=(),
    pieces=None,
    scalars=(),
    scratch=(),
    out_specs=None,
    flops=0,
    name=None,
):
    count, out_count, own = len(args), len(jax.tree.leaves(outs)), len(scratch)
    specs = [SMEM if i in smem else HBM if i in hbm else VMEM for i in range(count)]
    nbytes = sum(a.size * a.dtype.itemsize for a in args)
    space = [pltpu.SMEM if i in scalars else pltpu.VMEM for i in hbm]
    buffers = [kind(args[i].shape, args[i].dtype) for kind, i in zip(space, hbm)]
    spans = {i: (pieces or {}).get(i, ((0, args[i].shape[0]),)) for i in hbm}
    sems = [pltpu.SemaphoreType.DMA((len(spans[i]),)) for i in hbm]

    def body(*refs):
        ins, rest = list(refs[:count]), refs[count:]
        kept, moved = rest[: out_count + own], rest[out_count + own :]
        moves = {}
        for j, i in enumerate(hbm):
            moves[i] = []
            for k, (start, size) in enumerate(spans[i]):
                at = pl.ds(start, size)
                move = pltpu.make_async_copy(
                    ins[i].at[at], moved[j].at[at], moved[len(hbm) + j].at[k]
                )
                move.start()
                moves[i].append(move)
            ins[i] = moved[j]

        def ready(*wanted):
            for i in wanted:
                for move in moves[i]:
                    move.wait()

        kernel(ready, *ins, *kept)

    return pl.pallas_call(
        body,
        out_shape=outs,
        in_specs=specs,
        out_specs=jax.tree.map(lambda _: VMEM, outs) if out_specs is None else out_specs,
        scratch_shapes=list(scratch) + buffers + sems,
        compiler_params=pltpu.CompilerParams(vmem_limit_bytes=(60 if hbm else 40) * 1024 * 1024),
        cost_estimate=pl.CostEstimate(flops=flops, bytes_accessed=nbytes, transcendentals=0),
        name=name,
    )(*args)


def shape(dims, dtype):
    return jax.ShapeDtypeStruct(dims, dtype)


def dot(a, b):
    return jnp.dot(a, b, preferred_element_type=f32)


def dot_nt(a, b):
    return lax.dot_general(a, b, NT, preferred_element_type=f32)


def dot_tn(a, b):
    return lax.dot_general(a, b, TN, preferred_element_type=f32)


def layer_norm(values, gain):
    mean = jnp.mean(values, axis=-1, keepdims=True)
    centred = values - mean
    var = jnp.mean(centred * centred, axis=-1, keepdims=True)
    return centred * lax.rsqrt(var + eps_norm) * gain


def one_hot(picked, nodes):
    lanes = lax.broadcasted_iota(jnp.int32, (picked.shape[0], nodes), 1)
    return jnp.where(lanes == picked, 1.0, 0.0).astype(bf)


def mark(rows, picked, at_ref, step):
    per_part = at_ref.shape[0]
    code = jnp.full(picked.shape, -1, jnp.int32)
    for title in range(per_part):
        code = jnp.where(picked == at_ref[title], step * per_part + title, code)
    lead = lax.broadcasted_iota(jnp.int32, rows.shape, 1) == 0
    return jnp.where(code >= 0, jnp.where(lead, jnp.nan, code.astype(f32)), rows)


def send_kernel(ready, me_ref, at_ref, ids_ref, table_ref, w_ref, sent_ref, rows_ref, sems):
    cols = w_ref.shape[1]
    fetch, nodes = ids_ref.shape[1], table_ref.shape[0]
    ready(2)
    ids = ids_ref[...].astype(f32).T.astype(jnp.int32)
    ready(1, 3, 4)
    table = table_ref[...]
    kv = jnp.concatenate([dot_nt(table, w_ref[1]), dot_nt(table, w_ref[2])], axis=1).astype(bf)
    moves = []
    parts = ids.shape[1]
    group = min(parts, max(1, 1024 // fetch))
    for start in range(0, parts, group):
        picks = [ids[:, part : part + 1] for part in range(start, start + group)]
        rows = dot(one_hot(jnp.concatenate(picks, axis=0), nodes), kv)
        for j, picked in enumerate(picks):
            part = start + j
            mine = rows[j * fetch : (j + 1) * fetch]
            at = pl.ds(part * fetch, fetch)
            lead = mark(mine[:, :LANES], picked, at_ref, me_ref[0] ^ part)
            rows_ref[at, :LANES] = lead.astype(bf)
            rows_ref[at, LANES:] = mine[:, LANES:].astype(bf)
            move = pltpu.make_async_copy(rows_ref.at[at, :], sent_ref.at[at, :], sems.at[part])
            move.start()
            moves.append(move)
    for move in moves:
        move.wait()


def mask_kernel(ready, slots_ref, mask_ref):
    all_slots = slots_ref[...].astype(f32).T.astype(jnp.int32)
    for tile in range(all_slots.shape[0] // TILE):
        slots = all_slots[tile * TILE : (tile + 1) * TILE, :]
        lanes = lax.broadcasted_iota(jnp.int32, (TILE, TPR * TILE), 1)
        edges = lanes == lax.broadcasted_iota(jnp.int32, (TILE, TPR * TILE), 0)
        for edge in range(DEG):
            edges = edges | (lanes == slots[:, edge : edge + 1])
        mask_ref[tile * TILE : (tile + 1) * TILE, :] = jnp.where(edges, 1.0, 0.0).astype(bf)


def bias_kernel(ready, mask_ref, bias_ref):
    bias_ref[...] = jnp.where(mask_ref[...].astype(f32) > 0.5, 0.0, -jnp.inf)


def attn_kernel(ready, who_ref, titles_ref, w_in_ref, w_out_ref, *refs):
    outs, total = refs[:-1], refs[-1]
    titles = titles_ref[...]
    q = dot_nt(titles, w_in_ref[0]).astype(bf)
    k = dot_nt(titles, w_in_ref[1]).astype(bf)
    v = dot_nt(titles, w_in_ref[2]).astype(bf)
    cols = q.shape[1]
    heads = cols // HD
    lanes = lax.broadcasted_iota(jnp.int32, (SEQ, cols), 1) // HD
    for title in range(titles.shape[0] // SEQ):
        rows = slice(title * SEQ, (title + 1) * SEQ)
        qt, kt, vt = q[rows], k[rows], v[rows]
        stacked = jnp.concatenate(
            [jnp.where(lanes == h, qt, jnp.zeros_like(qt)) for h in range(heads)], axis=0
        )
        scores = dot_nt(stacked, kt) * (1.0 / HD**0.5)
        expo = jnp.exp(scores - jnp.max(scores, axis=-1, keepdims=True))
        probs = (expo / jnp.sum(expo, axis=-1, keepdims=True)).astype(bf)
        mixed = dot(probs, vt)
        context = mixed[:SEQ]
        for h in range(1, heads):
            context = jnp.where(lanes == h, mixed[h * SEQ : (h + 1) * SEQ], context)
        total[rows, :] = dot(context.astype(bf), w_out_ref[...])
    chunk = (outs[0].shape[0] - PAD) // 2
    firsts = first_rows(total)
    for out, pair in zip(outs, ((0, 2), (1, 3))):
        for j, step in enumerate(pair):
            at = pl.ds(pl.multiple_of((who_ref[0] ^ step) * chunk, chunk), chunk)
            out[j * chunk : (j + 1) * chunk, :] = total[at, :].astype(out.dtype)
        out[2 * chunk :, :] = firsts.astype(out.dtype)


def half_kernel(chunk, ready, kept_ref, came_ref, keep_ref, give_ref):
    total = kept_ref[...] + came_ref[...].astype(f32)
    keep_ref[:chunk, :] = total[:chunk]
    give_ref[:chunk, :] = total[chunk : 2 * chunk].astype(bf)
    if keep_ref.shape[0] > chunk:
        keep_ref[chunk:, :] = total[2 * chunk :]
        give_ref[chunk:, :] = total[2 * chunk :].astype(bf)


def first_rows(ref):
    sub = lax.broadcasted_iota(jnp.int32, (PAD, ref.shape[1]), 0)
    rows = jnp.zeros((PAD, ref.shape[1]), f32)
    for title in range(ref.shape[0] // SEQ):
        row = ref[title * SEQ : title * SEQ + 1, :].astype(f32)
        rows = jnp.where(sub == title, row, rows)
    return rows


def norm_one_kernel(
    ready, who_ref, titles_ref, gains_ref, w_in_ref, w_out_ref, own_ref, *refs
):
    *parts, out, first_hidden, first_terms = refs
    chunk = own_ref.shape[0] - PAD
    total = own_ref[...]
    for part in parts:
        total = total + part[...].astype(f32)
    at = pl.ds(pl.multiple_of(who_ref[0] * chunk, chunk), chunk)
    base = jnp.concatenate([titles_ref[at, :].astype(f32), first_rows(titles_ref)], axis=0)
    hidden = layer_norm(base + total, gains_ref[0:1, :]).astype(bf)
    out[:chunk, :] = hidden[:chunk]
    firsts = hidden[chunk:]
    first_hidden[...] = firsts
    terms = dot(gelu(dot(firsts, w_in_ref[...])).astype(bf), w_out_ref[...])
    first_terms[...] = terms
    out[chunk:, :] = terms.astype(bf)


def gelu(x):
    return 0.5 * x * (1.0 + lax.erf(x * (0.5**0.5)))


def ffn_kernel(ready, w_in_ref, w_out_ref, gains_ref, first_hidden, first_terms, *refs):
    *ins, kept, sent, first = refs
    chunk = kept.shape[0] // 2
    hidden = jnp.concatenate([ref[:chunk, :] for ref in ins], axis=0)
    inner = gelu(dot(hidden, w_in_ref[...])).astype(bf)
    total = dot(inner, w_out_ref[...])
    kept[...] = total[: 2 * chunk]
    sent[...] = total[2 * chunk :].astype(bf)
    terms = first_terms[...]
    for ref in ins[1:]:
        terms = terms + ref[chunk:, :].astype(f32)
    done = layer_norm(first_hidden[...].astype(f32) + terms, gains_ref[1:2, :])
    first[...] = done[: first.shape[0]].astype(bf)


def norm_two_kernel(ready, hidden_ref, gains_ref, own_ref, *refs):
    *parts, out = refs
    total = own_ref[...]
    for part in parts:
        total = total + part[...].astype(f32)
    hidden = hidden_ref[: out.shape[0], :].astype(f32)
    out[...] = layer_norm(hidden + total, gains_ref[1:2, :]).astype(bf)


def pack_kernel(ready, *refs):
    *parts, out = refs
    per_part = parts[0].shape[0]
    sub = lax.broadcasted_iota(jnp.int32, out.shape, 0)
    rows = jnp.zeros(out.shape, f32)
    for turn, ref in enumerate(parts):
        for title in range(per_part):
            row = ref[title : title + 1, :].astype(f32)
            rows = jnp.where(sub == turn * per_part + title, row, rows)
    out[...] = rows.astype(bf)


def own_kernel(ready, table_ref, w_ref, kv_ref, q_ref):
    cols = w_ref.shape[1]
    table = table_ref[...]
    kv_ref[:, :cols] = dot_nt(table, w_ref[1]).astype(bf)
    kv_ref[:, cols:] = dot_nt(table, w_ref[2]).astype(bf)
    q_ref[...] = dot_nt(table, w_ref[0]).astype(bf)


def tail_rows(count):
    return -(-count // PAD) * PAD


def graph_kernel(
    whose, ready, who_ref, cols_ref, at_ref, q_ref, kv_ref, w_ref, bias_ref, far_ref, first_ref, *refs
):
    *packs, out_ref, encoded_ref, k_all, v_all, firsts = refs
    dones, packs = packs[: len(whose)], packs[len(whose) :]
    chunk = dones[0].shape[0]
    for step, ref in zip(whose, dones):
        at = pl.multiple_of((who_ref[0] ^ step) * chunk, chunk)
        encoded_ref[pl.ds(at, chunk), :] = ref[...]
    nodes, cols = q_ref.shape
    row_tiles = nodes // TILE
    per_part = first_ref.shape[0]
    members = len(packs)
    for step, ref in enumerate(packs):
        rows = ref[...].astype(f32)
        for turn in range(firsts.shape[0] // per_part // members):
            for title in range(per_part):
                place = (turn * members + lax.rem(who_ref[0] ^ step, members)) * per_part + title
                at = turn * per_part + title
                firsts[pl.ds(place, 1), :] = rows[at : at + 1]
    firsts[0:per_part, :] = first_ref[...].astype(f32)
    first = firsts[...].astype(bf)
    first_kv = jnp.concatenate([dot_nt(first, w_ref[1]), dot_nt(first, w_ref[2])], axis=1).astype(bf)
    first_q = dot_nt(first, w_ref[0])
    for tile in range(row_tiles):
        span = slice(tile * TILE, (tile + 1) * TILE)
        rows = kv_ref[span, :].astype(f32)
        sub = lax.broadcasted_iota(jnp.int32, (TILE, 2 * cols), 0) + tile * TILE
        for title in range(per_part):
            row = first_kv[title : title + 1].astype(f32)
            rows = jnp.where(sub == at_ref[title], row, rows)
        rows = rows.astype(bf)
        k_all[span, :] = rows[:, :cols]
        v_all[span, :] = rows[:, cols:]
    lanes = lax.broadcasted_iota(jnp.int32, (FIX, first_kv.shape[0]), 1).astype(f32)
    for tile in range(far_ref.shape[0] // FIX):
        rows = far_ref[tile * FIX : (tile + 1) * FIX, :].astype(f32)
        code = jnp.where(rows[:, 0:1] != rows[:, 0:1], rows[:, 1:2], -1.0)
        hot = jnp.where(lanes == code, 1.0, 0.0).astype(bf)
        fixed = jnp.where(code >= 0.0, dot(hot, first_kv), rows).astype(bf)
        span = slice(nodes + tile * FIX, nodes + (tile + 1) * FIX)
        k_all[span, :] = fixed[:, :cols]
        v_all[span, :] = fixed[:, cols:]

    heads = cols // GHD
    head_of = lax.broadcasted_iota(jnp.int32, (TILE, cols), 1) // GHD
    for tile in range(row_tiles):
        q = q_ref[tile * TILE : (tile + 1) * TILE, :].astype(f32)
        sub = lax.broadcasted_iota(jnp.int32, (TILE, cols), 0) + tile * TILE
        for title in range(per_part):
            q = jnp.where(sub == at_ref[title], first_q[title : title + 1], q)
        q = q.astype(bf)
        stacked = jnp.concatenate(
            [jnp.where(head_of == h, q, jnp.zeros_like(q)) for h in range(heads)], axis=0
        )
        starts = [pl.multiple_of(cols_ref[tile, c] * TILE, TILE) for c in range(TPR)]
        keys = jnp.concatenate([k_all[pl.ds(start, TILE), :] for start in starts], axis=0)
        values = jnp.concatenate([v_all[pl.ds(start, TILE), :] for start in starts], axis=0)
        scores = dot_nt(stacked, keys) * (1.0 / GHD**0.5)
        bias = bias_ref[tile * TILE : (tile + 1) * TILE, :]
        masked = scores + jnp.concatenate([bias] * heads, axis=0)
        expo = jnp.exp(masked - jnp.max(masked, axis=-1, keepdims=True))
        scale = 1.0 / jnp.sum(expo, axis=-1, keepdims=True)
        mixed = dot(expo.astype(bf), values) * scale
        out = mixed[:TILE]
        for h in range(1, heads):
            out = jnp.where(head_of == h, mixed[h * TILE : (h + 1) * TILE], out)
        out_ref[:, tile * TILE : (tile + 1) * TILE] = out.T.astype(bf)


def local(

    titles,
    w_attn_in,
    w_attn_out,
    w_ffn_in,
    w_ffn_out,
    gains,
    node_table,
    w_graph,
    title_nodes,
    send_ids,
    tile_cols,
    nbr_slots,
):
    tok_rows, width = titles.shape
    nodes = node_table.shape[0]
    cols = w_graph.shape[2]
    mp = lax.axis_size("mp")
    dp = lax.axis_size("dp")
    me_mp = lax.axis_index("mp").astype(jnp.int32)
    me_dp = lax.axis_index("dp").astype(jnp.int32)
    me, who = me_dp.reshape(1), me_mp.reshape(1)
    chunk = tok_rows // mp
    per_part = title_nodes.shape[0]
    fetch = send_ids.shape[2]

    def swap(value, step, axis="mp"):
        return lax.ppermute(value, axis, [(i, i ^ step) for i in range(lax.axis_size(axis))])

    def gather(value):
        whose, blocks, step = [0], [value], mp // 2
        while step:
            blocks = blocks + [swap(block, step) for block in blocks]
            whose = whose + [other ^ step for other in whose]
            step //= 2
        return whose, blocks

    def halves(kept, came, pad):
        dims = (chunk + pad, width)
        return call(
            functools.partial(half_kernel, chunk),
            (shape(dims, f32), shape(dims, bf)),
            (kept, came),
            name="half",
        )

    w_attn_in = jnp.swapaxes(w_attn_in, 1, 2)
    w_graph = jnp.swapaxes(w_graph, 1, 2)
    sent = call(
        send_kernel,
        shape((dp * fetch, 2 * cols), bf),
        (me, title_nodes, send_ids[0], node_table, w_graph),
        smem=(0,),
        hbm=(2, 3, 4, 1),
        pieces={3: [(i, nodes // 4) for i in range(0, nodes, nodes // 4)], 4: [(1, 1), (2, 1)]},
        scalars=(1,),
        out_specs=HBM,
        scratch=[pltpu.VMEM((dp * fetch, 2 * cols), bf), pltpu.SemaphoreType.DMA((dp,))],
        flops=2 * nodes * width * 2 * cols + 2 * dp * fetch * nodes * 2 * cols,
        name="send",
    )
    far = lax.all_to_all(
        sent.reshape(dp, fetch, 2 * cols), "dp", split_axis=0, concat_axis=0, tiled=True
    ).reshape(dp * fetch, 2 * cols)
    titles, _ = lax.optimization_barrier((titles, sent))

    kept, given = call(
        attn_kernel,
        (shape((2 * chunk + PAD, width), f32), shape((2 * chunk + PAD, width), bf)),
        (who, titles, w_attn_in, w_attn_out),
        smem=(0,),
        scratch=[pltpu.VMEM((tok_rows, width), f32)],
        flops=2 * tok_rows * width * 4 * w_attn_in.shape[1],
        name="attn",
    )
    keep, give = halves(kept, swap(given, 1), PAD)
    part = swap(give, 2)
    kv, q = call(
        own_kernel,
        (shape((nodes, 2 * cols), bf), shape((nodes, cols), bf)),
        (node_table, w_graph),
        flops=2 * 10**9,
        name="own",
    )
    part, kv, q = lax.optimization_barrier((part, kv, q))
    hidden, first_hidden, first_terms = call(
        norm_one_kernel,
        (shape((chunk + PAD, width), bf), shape((PAD, width), bf), shape((PAD, width), f32)),
        (who, titles, gains, w_ffn_in, w_ffn_out, keep, part),
        smem=(0,),
        name="norm_one",
    )
    whose, hiddens = gather(hidden)
    kept, given, first = call(
        ffn_kernel,
        (
            shape((2 * chunk, width), f32),
            shape((2 * chunk, width), bf),
            shape((per_part, width), bf),
        ),
        (w_ffn_in, w_ffn_out, gains, first_hidden, first_terms, *hiddens),
        flops=4 * tok_rows * width * w_ffn_in.shape[1],
        name="ffn",
    )
    pair = 2
    turns = dp // pair
    firsts = [
        lax.ppermute(
            first,
            ("dp", "mp"),
            [
                (p * mp + m, (p ^ (turn * pair + m % pair)) * mp + m)
                for p in range(dp)
                for m in range(mp)
                if turn or m % pair
            ],
        )
        for turn in range(turns)
    ]
    keep, give = halves(kept, swap(given, 1), 0)
    give, slots = lax.optimization_barrier((give, nbr_slots))
    part = swap(give, 2)
    mask = call(
        mask_kernel, shape((nodes, TPR * TILE), bf), (slots.T,), flops=4 * 10**9, name="mask"
    )
    part, mask = lax.optimization_barrier((part, mask))
    done = call(
        norm_two_kernel, shape((chunk, width), bf), (hidden, gains, keep, part), name="norm_two"
    )
    across = swap(done, 2)
    across, firsts, far = lax.optimization_barrier((across, firsts, far))
    pack = call(pack_kernel, shape((tail_rows(turns * per_part), width), bf), firsts, name="pack")
    mask, pack = lax.optimization_barrier((mask, pack))
    packs = [pack, swap(pack, 1)]
    bias = call(bias_kernel, shape(mask.shape, f32), (mask,), flops=10**9, name="bias")
    dones = [done, across, swap(done, 1), swap(across, 1)]
    keys = nodes + dp * fetch
    graph_out, encoded = call(
        functools.partial(graph_kernel, whose),
        (shape((cols, nodes), bf), shape((tok_rows, width), bf)),
        (who, tile_cols, title_nodes, q, kv, w_graph, bias, far, first, *dones, *packs),
        smem=(0, 1, 2),
        scratch=[
            pltpu.VMEM((keys, cols), bf),
            pltpu.VMEM((keys, cols), bf),
            pltpu.VMEM((dp * per_part, width), f32),
        ],
        flops=4 * 10**9,
        name="graph",
    )
    return (encoded, graph_out.T)


def solution(mesh):
    in_specs = (
        P("dp", None),
        P(None, None, "mp"),
        P("mp", None),
        P(None, "mp"),
        P("mp", None),
        P(),
        P("dp", None),
        P(None, None, "mp"),
        P("dp"),
        P("dp", None, None),
        P("dp", None),
        P("dp", None),
    )
    out_specs = (P("dp", None), P("dp", "mp"))
    return jax.shard_map(
        local, mesh=mesh, in_specs=in_specs, out_specs=out_specs, check_vma=False
    )
```

```python
import functools
import jax
import jax.numpy as jnp
from jax import lax
from jax.experimental import pallas as pl
from jax.experimental.pallas import tpu as pltpu
from jax.sharding import PartitionSpec as P

SEQ = 128
TILE = 128
DEG = 16
TPR = 6
HD = 64
GHD = 96

eps_norm = 1e-06
bf = jnp.bfloat16
f32 = jnp.float32

VMEM = pl.BlockSpec(memory_space=pltpu.VMEM)
SMEM = pl.BlockSpec(memory_space=pltpu.SMEM)
HBM = pl.BlockSpec(memory_space=pltpu.HBM)
PAD = 16
LANES = 128
NT = (((1,), (1,)), ((), ()))
TN = (((0,), (0,)), ((), ()))


def call(
    kernel,
    outs,
    args,
    smem=(),
    hbm=(),
    pieces=None,
    scalars=(),
    scratch=(),
    out_specs=None,
    flops=0,
    name=None,
):
    count, out_count, own = len(args), len(jax.tree.leaves(outs)), len(scratch)
    specs = [SMEM if i in smem else HBM if i in hbm else VMEM for i in range(count)]
    nbytes = sum(a.size * a.dtype.itemsize for a in args)
    space = [pltpu.SMEM if i in scalars else pltpu.VMEM for i in hbm]
    buffers = [kind(args[i].shape, args[i].dtype) for kind, i in zip(space, hbm)]
    spans = {i: (pieces or {}).get(i, ((0, args[i].shape[0]),)) for i in hbm}
    sems = [pltpu.SemaphoreType.DMA((len(spans[i]),)) for i in hbm]

    def body(*refs):
        ins, rest = list(refs[:count]), refs[count:]
        kept, moved = rest[: out_count + own], rest[out_count + own :]
        moves = {}
        for j, i in enumerate(hbm):
            moves[i] = []
            for k, (start, size) in enumerate(spans[i]):
                at = pl.ds(start, size)
                move = pltpu.make_async_copy(
                    ins[i].at[at], moved[j].at[at], moved[len(hbm) + j].at[k]
                )
                move.start()
                moves[i].append(move)
            ins[i] = moved[j]

        def ready(*wanted):
            for i in wanted:
                for move in moves[i]:
                    move.wait()

        kernel(ready, *ins, *kept)

    return pl.pallas_call(
        body,
        out_shape=outs,
        in_specs=specs,
        out_specs=jax.tree.map(lambda _: VMEM, outs) if out_specs is None else out_specs,
        scratch_shapes=list(scratch) + buffers + sems,
        compiler_params=pltpu.CompilerParams(vmem_limit_bytes=(60 if hbm else 40) * 1024 * 1024),
        cost_estimate=pl.CostEstimate(flops=flops, bytes_accessed=nbytes, transcendentals=0),
        name=name,
    )(*args)


def shape(dims, dtype):
    return jax.ShapeDtypeStruct(dims, dtype)


def dot(a, b):
    return jnp.dot(a, b, preferred_element_type=f32)


def dot_nt(a, b):
    return lax.dot_general(a, b, NT, preferred_element_type=f32)


def dot_tn(a, b):
    return lax.dot_general(a, b, TN, preferred_element_type=f32)


def layer_norm(values, gain):
    mean = jnp.mean(values, axis=-1, keepdims=True)
    centred = values - mean
    var = jnp.mean(centred * centred, axis=-1, keepdims=True)
    return centred * lax.rsqrt(var + eps_norm) * gain


def one_hot(picked, nodes):
    lanes = lax.broadcasted_iota(jnp.int32, (picked.shape[0], nodes), 1)
    return jnp.where(lanes == picked, 1.0, 0.0).astype(bf)


def mark(rows, picked, at_ref, step):
    per_part = at_ref.shape[0]
    code = jnp.full(picked.shape, -1, jnp.int32)
    for title in range(per_part):
        code = jnp.where(picked == at_ref[title], step * per_part + title, code)
    lead = lax.broadcasted_iota(jnp.int32, rows.shape, 1) == 0
    return jnp.where(code >= 0, jnp.where(lead, jnp.nan, code.astype(f32)), rows)


def send_kernel(ready, me_ref, at_ref, ids_ref, table_ref, w_ref, sent_ref, rows_ref, sems):
    cols = w_ref.shape[1]
    fetch, nodes = ids_ref.shape[1], table_ref.shape[0]
    ready(2)
    ids = ids_ref[...].astype(f32).T.astype(jnp.int32)
    ready(1, 3, 4)
    table = table_ref[...]
    kv = jnp.concatenate([dot_nt(table, w_ref[1]), dot_nt(table, w_ref[2])], axis=1).astype(bf)
    moves = []
    parts = ids.shape[1]
    group = min(parts, max(1, 1024 // fetch))
    for start in range(0, parts, group):
        picks = [ids[:, part : part + 1] for part in range(start, start + group)]
        rows = dot(one_hot(jnp.concatenate(picks, axis=0), nodes), kv)
        for j, picked in enumerate(picks):
            part = start + j
            mine = rows[j * fetch : (j + 1) * fetch]
            at = pl.ds(part * fetch, fetch)
            lead = mark(mine[:, :LANES], picked, at_ref, me_ref[0] ^ part)
            rows_ref[at, :LANES] = lead.astype(bf)
            rows_ref[at, LANES:] = mine[:, LANES:].astype(bf)
            move = pltpu.make_async_copy(rows_ref.at[at, :], sent_ref.at[at, :], sems.at[part])
            move.start()
            moves.append(move)
    for move in moves:
        move.wait()


def mask_kernel(ready, slots_ref, mask_ref):
    all_slots = slots_ref[...].astype(f32).T.astype(jnp.int32)
    for tile in range(all_slots.shape[0] // TILE):
        slots = all_slots[tile * TILE : (tile + 1) * TILE, :]
        lanes = lax.broadcasted_iota(jnp.int32, (TILE, TPR * TILE), 1)
        edges = lanes == lax.broadcasted_iota(jnp.int32, (TILE, TPR * TILE), 0)
        for edge in range(DEG):
            edges = edges | (lanes == slots[:, edge : edge + 1])
        mask_ref[tile * TILE : (tile + 1) * TILE, :] = jnp.where(edges, 1.0, 0.0).astype(bf)


def bias_kernel(ready, mask_ref, bias_ref):
    bias_ref[...] = jnp.where(mask_ref[...].astype(f32) > 0.5, 0.0, -jnp.inf)


def attn_kernel(ready, who_ref, titles_ref, w_in_ref, w_out_ref, *refs):
    outs, total = refs[:-1], refs[-1]
    titles = titles_ref[...]
    q = dot_nt(titles, w_in_ref[0]).astype(bf)
    k = dot_nt(titles, w_in_ref[1]).astype(bf)
    v = dot_nt(titles, w_in_ref[2]).astype(bf)
    cols = q.shape[1]
    heads = cols // HD
    lanes = lax.broadcasted_iota(jnp.int32, (SEQ, cols), 1) // HD
    for title in range(titles.shape[0] // SEQ):
        rows = slice(title * SEQ, (title + 1) * SEQ)
        qt, kt, vt = q[rows], k[rows], v[rows]
        stacked = jnp.concatenate(
            [jnp.where(lanes == h, qt, jnp.zeros_like(qt)) for h in range(heads)], axis=0
        )
        scores = dot_nt(stacked, kt) * (1.0 / HD**0.5)
        expo = jnp.exp(scores - jnp.max(scores, axis=-1, keepdims=True))
        probs = (expo / jnp.sum(expo, axis=-1, keepdims=True)).astype(bf)
        mixed = dot(probs, vt)
        context = mixed[:SEQ]
        for h in range(1, heads):
            context = jnp.where(lanes == h, mixed[h * SEQ : (h + 1) * SEQ], context)
        total[rows, :] = dot(context.astype(bf), w_out_ref[...])
    chunk = (outs[0].shape[0] - PAD) // 2
    firsts = first_rows(total)
    for out, pair in zip(outs, ((0, 2), (1, 3))):
        for j, step in enumerate(pair):
            at = pl.ds(pl.multiple_of((who_ref[0] ^ step) * chunk, chunk), chunk)
            out[j * chunk : (j + 1) * chunk, :] = total[at, :].astype(out.dtype)
        out[2 * chunk :, :] = firsts.astype(out.dtype)


def half_kernel(chunk, ready, kept_ref, came_ref, keep_ref, give_ref):
    total = kept_ref[...] + came_ref[...].astype(f32)
    keep_ref[:chunk, :] = total[:chunk]
    give_ref[:chunk, :] = total[chunk : 2 * chunk].astype(bf)
    if keep_ref.shape[0] > chunk:
        keep_ref[chunk:, :] = total[2 * chunk :]
        give_ref[chunk:, :] = total[2 * chunk :].astype(bf)


def first_rows(ref):
    sub = lax.broadcasted_iota(jnp.int32, (PAD, ref.shape[1]), 0)
    rows = jnp.zeros((PAD, ref.shape[1]), f32)
    for title in range(ref.shape[0] // SEQ):
        row = ref[title * SEQ : title * SEQ + 1, :].astype(f32)
        rows = jnp.where(sub == title, row, rows)
    return rows


def norm_one_kernel(
    ready, who_ref, titles_ref, gains_ref, w_in_ref, w_out_ref, own_ref, *refs
):
    *parts, out, first_hidden, first_terms = refs
    chunk = own_ref.shape[0] - PAD
    total = own_ref[...]
    for part in parts:
        total = total + part[...].astype(f32)
    at = pl.ds(pl.multiple_of(who_ref[0] * chunk, chunk), chunk)
    base = jnp.concatenate([titles_ref[at, :].astype(f32), first_rows(titles_ref)], axis=0)
    hidden = layer_norm(base + total, gains_ref[0:1, :]).astype(bf)
    out[:chunk, :] = hidden[:chunk]
    firsts = hidden[chunk:]
    first_hidden[...] = firsts
    terms = dot(gelu(dot(firsts, w_in_ref[...])).astype(bf), w_out_ref[...])
    first_terms[...] = terms
    out[chunk:, :] = terms.astype(bf)


def gelu(x):
    return 0.5 * x * (1.0 + lax.erf(x * (0.5**0.5)))


def ffn_kernel(ready, w_in_ref, w_out_ref, gains_ref, first_hidden, first_terms, *refs):
    *ins, kept, sent, first = refs
    chunk = kept.shape[0] // 2
    hidden = jnp.concatenate([ref[:chunk, :] for ref in ins], axis=0)
    inner = gelu(dot(hidden, w_in_ref[...])).astype(bf)
    total = dot(inner, w_out_ref[...])
    kept[...] = total[: 2 * chunk]
    sent[...] = total[2 * chunk :].astype(bf)
    terms = first_terms[...]
    for ref in ins[1:]:
        terms = terms + ref[chunk:, :].astype(f32)
    done = layer_norm(first_hidden[...].astype(f32) + terms, gains_ref[1:2, :])
    first[...] = done[: first.shape[0]].astype(bf)


def norm_two_kernel(ready, hidden_ref, gains_ref, own_ref, *refs):
    *parts, out = refs
    total = own_ref[...]
    for part in parts:
        total = total + part[...].astype(f32)
    hidden = hidden_ref[: out.shape[0], :].astype(f32)
    out[...] = layer_norm(hidden + total, gains_ref[1:2, :]).astype(bf)


def pack_kernel(ready, *refs):
    *parts, out = refs
    per_part = parts[0].shape[0]
    sub = lax.broadcasted_iota(jnp.int32, out.shape, 0)
    rows = jnp.zeros(out.shape, f32)
    for turn, ref in enumerate(parts):
        for title in range(per_part):
            row = ref[title : title + 1, :].astype(f32)
            rows = jnp.where(sub == turn * per_part + title, row, rows)
    out[...] = rows.astype(bf)


def own_kernel(ready, table_ref, w_ref, kv_ref, q_ref):
    cols = w_ref.shape[1]
    table = table_ref[...]
    kv_ref[:, :cols] = dot_nt(table, w_ref[1]).astype(bf)
    kv_ref[:, cols:] = dot_nt(table, w_ref[2]).astype(bf)
    q_ref[...] = (dot_nt(table, w_ref[0]) * (1.0 / GHD**0.5)).astype(bf)


def tail_rows(count):
    return -(-count // PAD) * PAD


def graph_kernel(
    whose, ready, who_ref, cols_ref, at_ref, q_ref, kv_ref, w_ref, bias_ref, far_ref, first_ref, *refs
):
    *packs, out_ref, encoded_ref, k_all, v_all, firsts = refs
    dones, packs = packs[: len(whose)], packs[len(whose) :]
    chunk = dones[0].shape[0]
    for step, ref in zip(whose, dones):
        at = pl.multiple_of((who_ref[0] ^ step) * chunk, chunk)
        encoded_ref[pl.ds(at, chunk), :] = ref[...]
    nodes, cols = q_ref.shape
    row_tiles = nodes // TILE
    per_part = first_ref.shape[0]
    members = len(packs)
    for step, ref in enumerate(packs):
        rows = ref[...].astype(f32)
        for turn in range(firsts.shape[0] // per_part // members):
            for title in range(per_part):
                place = (turn * members + lax.rem(who_ref[0] ^ step, members)) * per_part + title
                at = turn * per_part + title
                firsts[pl.ds(place, 1), :] = rows[at : at + 1]
    firsts[0:per_part, :] = first_ref[...].astype(f32)
    first = firsts[...].astype(bf)
    first_kv = jnp.concatenate([dot_nt(first, w_ref[1]), dot_nt(first, w_ref[2])], axis=1).astype(bf)
    first_q = dot_nt(first, w_ref[0]) * (1.0 / GHD**0.5)
    for tile in range(row_tiles):
        span = slice(tile * TILE, (tile + 1) * TILE)
        rows = kv_ref[span, :].astype(f32)
        sub = lax.broadcasted_iota(jnp.int32, (TILE, 2 * cols), 0) + tile * TILE
        for title in range(per_part):
            row = first_kv[title : title + 1].astype(f32)
            rows = jnp.where(sub == at_ref[title], row, rows)
        rows = rows.astype(bf)
        k_all[span, :] = rows[:, :cols]
        v_all[span, :] = rows[:, cols:]
    lanes = lax.broadcasted_iota(jnp.int32, (TILE, first_kv.shape[0]), 1).astype(f32)
    for tile in range(far_ref.shape[0] // TILE):
        rows = far_ref[tile * TILE : (tile + 1) * TILE, :].astype(f32)
        code = jnp.where(rows[:, 0:1] != rows[:, 0:1], rows[:, 1:2], -1.0)
        hot = jnp.where(lanes == code, 1.0, 0.0).astype(bf)
        fixed = jnp.where(code >= 0.0, dot(hot, first_kv), rows).astype(bf)
        span = slice(nodes + tile * TILE, nodes + (tile + 1) * TILE)
        k_all[span, :] = fixed[:, :cols]
        v_all[span, :] = fixed[:, cols:]

    heads = cols // GHD
    head_of = lax.broadcasted_iota(jnp.int32, (TILE, cols), 1) // GHD
    for tile in range(row_tiles):
        q = q_ref[tile * TILE : (tile + 1) * TILE, :].astype(f32)
        sub = lax.broadcasted_iota(jnp.int32, (TILE, cols), 0) + tile * TILE
        for title in range(per_part):
            q = jnp.where(sub == at_ref[title], first_q[title : title + 1], q)
        q = q.astype(bf)
        stacked = jnp.concatenate(
            [jnp.where(head_of == h, q, jnp.zeros_like(q)) for h in range(heads)], axis=0
        )
        starts = [pl.multiple_of(cols_ref[tile, c] * TILE, TILE) for c in range(TPR)]
        keys = jnp.concatenate([k_all[pl.ds(start, TILE), :] for start in starts], axis=0)
        values = jnp.concatenate([v_all[pl.ds(start, TILE), :] for start in starts], axis=0)
        scores = dot_nt(stacked, keys)
        bias = bias_ref[tile * TILE : (tile + 1) * TILE, :]
        masked = scores + jnp.concatenate([bias] * heads, axis=0)
        expo = jnp.exp(masked - jnp.max(masked, axis=-1, keepdims=True))
        scale = 1.0 / jnp.sum(expo, axis=-1, keepdims=True)
        mixed = dot(expo.astype(bf), values) * scale
        out = mixed[:TILE]
        for h in range(1, heads):
            out = jnp.where(head_of == h, mixed[h * TILE : (h + 1) * TILE], out)
        out_ref[:, tile * TILE : (tile + 1) * TILE] = out.T.astype(bf)


def local(

    titles,
    w_attn_in,
    w_attn_out,
    w_ffn_in,
    w_ffn_out,
    gains,
    node_table,
    w_graph,
    title_nodes,
    send_ids,
    tile_cols,
    nbr_slots,
):
    tok_rows, width = titles.shape
    nodes = node_table.shape[0]
    cols = w_graph.shape[2]
    mp = lax.axis_size("mp")
    dp = lax.axis_size("dp")
    me_mp = lax.axis_index("mp").astype(jnp.int32)
    me_dp = lax.axis_index("dp").astype(jnp.int32)
    me, who = me_dp.reshape(1), me_mp.reshape(1)
    chunk = tok_rows // mp
    per_part = title_nodes.shape[0]
    fetch = send_ids.shape[2]

    def swap(value, step, axis="mp"):
        return lax.ppermute(value, axis, [(i, i ^ step) for i in range(lax.axis_size(axis))])

    def gather(value):
        whose, blocks, step = [0], [value], mp // 2
        while step:
            blocks = blocks + [swap(block, step) for block in blocks]
            whose = whose + [other ^ step for other in whose]
            step //= 2
        return whose, blocks

    def halves(kept, came, pad):
        dims = (chunk + pad, width)
        return call(
            functools.partial(half_kernel, chunk),
            (shape(dims, f32), shape(dims, bf)),
            (kept, came),
            name="half",
        )

    w_attn_in = jnp.swapaxes(w_attn_in, 1, 2)
    w_graph = jnp.swapaxes(w_graph, 1, 2)
    sent = call(
        send_kernel,
        shape((dp * fetch, 2 * cols), bf),
        (me, title_nodes, send_ids[0], node_table, w_graph),
        smem=(0,),
        hbm=(2, 3, 4, 1),
        pieces={3: [(i, nodes // 4) for i in range(0, nodes, nodes // 4)], 4: [(1, 1), (2, 1)]},
        scalars=(1,),
        out_specs=HBM,
        scratch=[pltpu.VMEM((dp * fetch, 2 * cols), bf), pltpu.SemaphoreType.DMA((dp,))],
        flops=2 * nodes * width * 2 * cols + 2 * dp * fetch * nodes * 2 * cols,
        name="send",
    )
    far = lax.all_to_all(
        sent.reshape(dp, fetch, 2 * cols), "dp", split_axis=0, concat_axis=0, tiled=True
    ).reshape(dp * fetch, 2 * cols)
    titles, _ = lax.optimization_barrier((titles, sent))

    kept, given = call(
        attn_kernel,
        (shape((2 * chunk + PAD, width), f32), shape((2 * chunk + PAD, width), bf)),
        (who, titles, w_attn_in, w_attn_out),
        smem=(0,),
        scratch=[pltpu.VMEM((tok_rows, width), f32)],
        flops=2 * tok_rows * width * 4 * w_attn_in.shape[1],
        name="attn",
    )
    keep, give = halves(kept, swap(given, 1), PAD)
    part = swap(give, 2)
    kv, q = call(
        own_kernel,
        (shape((nodes, 2 * cols), bf), shape((nodes, cols), bf)),
        (node_table, w_graph),
        flops=2 * 10**9,
        name="own",
    )
    part, kv, q = lax.optimization_barrier((part, kv, q))
    hidden, first_hidden, first_terms = call(
        norm_one_kernel,
        (shape((chunk + PAD, width), bf), shape((PAD, width), bf), shape((PAD, width), f32)),
        (who, titles, gains, w_ffn_in, w_ffn_out, keep, part),
        smem=(0,),
        name="norm_one",
    )
    whose, hiddens = gather(hidden)
    kept, given, first = call(
        ffn_kernel,
        (
            shape((2 * chunk, width), f32),
            shape((2 * chunk, width), bf),
            shape((per_part, width), bf),
        ),
        (w_ffn_in, w_ffn_out, gains, first_hidden, first_terms, *hiddens),
        flops=4 * tok_rows * width * w_ffn_in.shape[1],
        name="ffn",
    )
    pair = 2
    turns = dp // pair
    firsts = [
        lax.ppermute(
            first,
            ("dp", "mp"),
            [
                (p * mp + m, (p ^ (turn * pair + m % pair)) * mp + m)
                for p in range(dp)
                for m in range(mp)
                if turn or m % pair
            ],
        )
        for turn in range(turns)
    ]
    keep, give = halves(kept, swap(given, 1), 0)
    give, slots = lax.optimization_barrier((give, nbr_slots))
    part = swap(give, 2)
    mask = call(
        mask_kernel, shape((nodes, TPR * TILE), bf), (slots.T,), flops=4 * 10**9, name="mask"
    )
    part, mask = lax.optimization_barrier((part, mask))
    done = call(
        norm_two_kernel, shape((chunk, width), bf), (hidden, gains, keep, part), name="norm_two"
    )
    across = swap(done, 2)
    across, firsts, far = lax.optimization_barrier((across, firsts, far))
    pack = call(pack_kernel, shape((tail_rows(turns * per_part), width), bf), firsts, name="pack")
    mask, pack = lax.optimization_barrier((mask, pack))
    packs = [pack, swap(pack, 1)]
    bias = call(bias_kernel, shape(mask.shape, f32), (mask,), flops=10**9, name="bias")
    dones = [done, across, swap(done, 1), swap(across, 1)]
    keys = nodes + dp * fetch
    graph_out, encoded = call(
        functools.partial(graph_kernel, whose),
        (shape((cols, nodes), bf), shape((tok_rows, width), bf)),
        (who, tile_cols, title_nodes, q, kv, w_graph, bias, far, first, *dones, *packs),
        smem=(0, 1, 2),
        scratch=[
            pltpu.VMEM((keys, cols), bf),
            pltpu.VMEM((keys, cols), bf),
            pltpu.VMEM((dp * per_part, width), f32),
        ],
        flops=4 * 10**9,
        name="graph",
    )
    return (encoded, graph_out.T)


def solution(mesh):
    in_specs = (
        P("dp", None),
        P(None, None, "mp"),
        P("mp", None),
        P(None, "mp"),
        P("mp", None),
        P(),
        P("dp", None),
        P(None, None, "mp"),
        P("dp"),
        P("dp", None, None),
        P("dp", None),
        P("dp", None),
    )
    out_specs = (P("dp", None), P("dp", "mp"))
    return jax.shard_map(
        local, mesh=mesh, in_specs=in_specs, out_specs=out_specs, check_vma=False
    )
```
